32 devices in a mesh: tm: 16 (over z, x, core), head: 2 (over y).
Axes of the slice: x: 2, y: 2, z: 4, core: 2. Of those that a mesh axis runs over, the one named last changes fastest.
Arguments:
- query_states: bfloat16 [24576, 1024], P('tm', 'head'), may hold values from -30 to 30
- key_states: bfloat16 [24576, 1024], P('tm', 'head'), may hold values from -30 to 30
- value_states: bfloat16 [24576, 1024], P('tm', 'head'), may hold values from -6 to 6
- win_start: int32 [32], P('tm'), may hold values from 0 to 30, as said below
- group_end: int32 [32], P('tm'), may hold values from 0 to 31, as said below
- out_weight: bfloat16 [1024, 1536], replicated, may hold values from -0.1875 to 0.1875
Outputs:
- projected: bfloat16 [24576, 1536], P(('tm', 'head'))
The draws below stay inside these ranges and needn't reach their ends.
Inputs may be any that keep to these rules, and one draw needn't show every extreme that they name: For every frame f, win_start[f] = max(f - lag, 0) with a lag of 1 to 3; frame 32 - 2 has a lag of 3 in every draw, and the last frame has a lag of 1. `group_end`: frames 2p and 2p + 1 form one group (both end at 2p + 1) or two groups of one frame (each ends at itself); both kinds occur in every draw.
All inputs are finite; a program needn't handle non-finite values.
Results may differ from the reference program's by a relative error of at most 0.0051.
Values may be sent and summed in bfloat16 or wider, within the bound.
No kernel may reach another device: no remote copies, remote signals or barrier semaphores. Data moves between devices by JAX's collectives and lax.ppermute only.
A program may use at most 384 MiB of HBM per device.

```python
import jax
import jax.numpy as jnp
from jax import lax

D = 1536
HEADS = 8
HD = 128
FT = 768
NF = 32
TOKENS = 24576


def paired_states(key):
    width = HEADS * HD
    key_base = jax.random.fold_in(key, 11)
    query_base = jax.random.fold_in(key, 12)
    key_draw = jnp.clip(2.0 * jax.random.normal(key_base, (TOKENS, width), jnp.float32), -12.0, 12.0)
    query_draw = jnp.clip(2.0 * jax.random.normal(query_base, (TOKENS, width), jnp.float32), -12.0, 12.0)
    return (query_draw, key_draw)


def draw_query_states(key, part):
    return paired_states(key)[0].astype(jnp.bfloat16)


def draw_key_states(key, part):
    return paired_states(key)[1].astype(jnp.bfloat16)


def draw_win_start(key, part):
    frame = jnp.arange(NF, dtype=jnp.int32)
    lagged = jax.random.randint(jax.random.fold_in(key, 21), (NF,), 1, 4, dtype=jnp.int32)
    lagged = jnp.where(frame % 8 == 5, 3, lagged)
    lagged = jnp.where(frame == NF - 2, 3, lagged)
    lagged = jnp.where(frame == NF - 1, 1, lagged)
    return jnp.maximum(frame - lagged, 0).astype(jnp.int32)


def draw_group_end(key, part):
    frame = jnp.arange(NF, dtype=jnp.int32)
    paired = frame // 2
    joined = jax.random.randint(jax.random.fold_in(key, 22), (NF // 2,), 0, 2, dtype=jnp.int32)
    joined = jnp.where(jnp.arange(NF // 2) % 4 == 1, 1, jnp.where(jnp.arange(NF // 2) % 4 == 3, 0, joined))
    joined_frame = joined[paired]
    return jnp.where(joined_frame == 1, 2 * paired + 1, frame).astype(jnp.int32)


def block_levels(own_key, extent, split, low, top_value):
    level = 1.0
    for dim, shards_of in split:
        draws = jax.random.uniform(jax.random.fold_in(jax.random.fold_in(own_key, 6), dim), (shards_of,), jnp.float32, low / len(split), top_value / len(split))
        level = level * jnp.repeat(jnp.exp(draws), extent[dim] // shards_of).reshape((-1,) + (1,) * (len(extent) - 1 - dim))
    return level


def scatter_about(own_key, extent, scale, reach, pieces=(), held_as=jnp.bfloat16):
    level = block_levels(own_key, extent, pieces, -0.22, 0.18) if pieces else 1.0
    array = jax.random.normal(own_key, extent, jnp.float32) * scale * level
    return jnp.minimum(jnp.maximum(array, -reach), reach).astype(held_as)


def setup_inputs(seed: int = 0) -> dict:
    key_list = jax.random.split(jax.random.key(seed), 7)
    return {
        "query_states": draw_query_states(jax.random.fold_in(key_list[6], 71), 0),
        "key_states": draw_key_states(jax.random.fold_in(key_list[6], 71), 0),
        "value_states": scatter_about(key_list[2], (TOKENS, HEADS * HD), 1.0, 6.0, ((0, 16), (1, 2))),
        "win_start": draw_win_start(jax.random.fold_in(key_list[6], 71), 0),
        "group_end": draw_group_end(jax.random.fold_in(key_list[6], 71), 0),
        "out_weight": scatter_about(key_list[5], (HEADS * HD, D), (HEADS * HD) ** -0.5, 0.1875),
    }


def reference(query_states, key_states, value_states, win_start, group_end, out_weight):
    width = HEADS * HD
    scale = HD ** -0.5
    padding = jnp.zeros((3 * FT, width), key_states.dtype)
    tail_pad = jnp.zeros((FT, width), key_states.dtype)
    padded_keys = jnp.concatenate([padding, key_states, tail_pad], axis=0)
    padded_values = jnp.concatenate([padding, value_states, tail_pad], axis=0)
    sink_keys = key_states[:FT]
    sink_values = value_states[:FT]

    def one_frame(frame):
        query_rows = lax.dynamic_slice_in_dim(query_states, (frame * FT).astype(jnp.int32), FT, 0)
        window_keys = lax.dynamic_slice_in_dim(padded_keys, (frame * FT).astype(jnp.int32), 5 * FT, 0)
        window_values = lax.dynamic_slice_in_dim(padded_values, (frame * FT).astype(jnp.int32), 5 * FT, 0)
        all_keys = jnp.concatenate([sink_keys, window_keys], axis=0)
        all_values = jnp.concatenate([sink_values, window_values], axis=0)
        frame_ids = frame - 3 + jnp.arange(5 * FT, dtype=jnp.int32) // FT
        window_seen = (frame_ids >= 1) & (frame_ids >= win_start[frame]) & (frame_ids <= group_end[frame])
        visible = jnp.concatenate([jnp.ones((FT,), dtype=bool), window_seen])
        query_heads = query_rows.reshape(FT, HEADS, HD).astype(jnp.float32)
        key_heads = all_keys.reshape(6 * FT, HEADS, HD).astype(jnp.float32)
        value_heads = all_values.reshape(6 * FT, HEADS, HD).astype(jnp.float32)
        scores = jnp.einsum("qhd,khd->hqk", query_heads, key_heads) * scale
        scores = jnp.where(visible[None, None, :], scores, -1e30)
        peak = jnp.max(scores, axis=-1, keepdims=True)
        weights = jnp.where(visible[None, None, :], jnp.exp(scores - peak), 0.0)
        total = jnp.sum(weights, axis=-1)
        rounded = lax.optimization_barrier(weights.astype(jnp.bfloat16))
        mixed = jnp.einsum("hqk,khd->qhd", rounded.astype(jnp.float32), value_heads)
        mixed = mixed / jnp.transpose(total)[:, :, None]
        return mixed.astype(jnp.bfloat16).reshape(FT, width)

    attended = lax.map(one_frame, jnp.arange(NF, dtype=jnp.int32)).reshape(TOKENS, width)
    return jnp.dot(attended, out_weight, preferred_element_type=jnp.float32).astype(jnp.bfloat16)
```

```python
import functools

import jax
import jax.numpy as jnp
from jax import lax
from jax.experimental import pallas as pl
from jax.experimental.pallas import tpu as pltpu
from jax.sharding import PartitionSpec as P

HD = 128
FT = 768
BQ = 256
BK = 256
LOG2E = 1.4426950408889634
SCALE = HD ** -0.5 * LOG2E
LIMIT = 1e30


def qk(q, k):
    return lax.dot_general(q, k, (((1,), (1,)), ((), ())), preferred_element_type=jnp.float32)


def accumulate(q, k, v, m, acc, l):
    nq, nk = FT // BQ, FT // BK
    units = [(i, j) for i in range(nq) for j in range(nk)]

    def scores(unit):
        i, j = unit
        return qk(q[i * BQ : (i + 1) * BQ, :], k[j * BK : (j + 1) * BK, :])

    ahead = scores(units[0])
    for n, (i, j) in enumerate(units):
        s = ahead
        if n + 1 < len(units):
            ahead = scores(units[n + 1])
        rows = slice(i * BQ, (i + 1) * BQ)
        if j == 0:
            total = acc[rows, :]
            weight_sum = l[rows, :]
        shift = m[rows, :]
        parts = []
        for c in range(BK // 128):
            part = jnp.exp2(s[:, c * 128 : (c + 1) * 128] * SCALE - shift)
            weight_sum = weight_sum + part
            parts.append(part.astype(jnp.bfloat16))
        weights = jnp.concatenate(parts, axis=1)
        total = total + jnp.dot(
            weights, v[j * BK : (j + 1) * BK, :], preferred_element_type=jnp.float32
        )
        if j == nk - 1:
            acc[rows, :] = total
            l[rows, :] = weight_sum


def visible(info, slot, frame):
    return (frame >= 1) & (frame >= info[2 + slot]) & (frame <= info[4 + slot])


def local_kernel(info, q, k0, v0, k1, v1, m, acc, l):
    slot = pl.program_id(1)
    first = info[0]

    def start(k):
        for i in range(FT // BQ):
            rows = slice(i * BQ, (i + 1) * BQ)
            s = qk(q[rows, :], k[0:BK, :]) * SCALE
            m[rows, :] = jnp.broadcast_to(jnp.max(s, axis=1, keepdims=True), (BQ, 128))

    @pl.when(slot == 0)
    def _():
        start(k0)

    @pl.when(slot == 1)
    def _():
        start(k1)

    acc[...] = jnp.zeros_like(acc)
    l[...] = jnp.zeros_like(l)

    @pl.when(visible(info, slot, first))
    def _():
        accumulate(q, k0, v0, m, acc, l)

    @pl.when(visible(info, slot, first + 1))
    def _():
        accumulate(q, k1, v1, m, acc, l)


def near_kernel(info, q, k0, v0, k1, v1, m, acc_in, l_in, acc, l):
    slot = pl.program_id(1)
    first = info[0]
    acc[...] = acc_in[...]
    l[...] = l_in[...]

    @pl.when(visible(info, slot, first - 1))
    def _():
        accumulate(q, k1, v1, m, acc, l)

    @pl.when(visible(info, slot, first - 2))
    def _():
        accumulate(q, k0, v0, m, acc, l)


def final_kernel(
    info, q, sink_a, sink_b, far_k, far_v, relay_k, relay_v, m, acc_in, l_in,
    key_hbm, value_hbm, near_k_hbm, near_v_hbm, sink_a_hbm, sink_b_hbm, far_hbm, relay_hbm,
    out, acc, l, exact_m, k_buf, v_buf, sem,
):
    head = pl.program_id(0)
    slot = pl.program_id(1)
    first = info[0]
    core = info[6]
    acc[...] = acc_in[...]
    l[...] = l_in[...]

    @pl.when(core == 0)
    def _():
        accumulate(q, sink_a, sink_b, m, acc, l)

    @pl.when(core == 1)
    def _():
        accumulate(q, sink_b, sink_a, m, acc, l)

    far_seen = (slot == 0) & visible(info, slot, first - 3)

    @pl.when(far_seen & (core == 0))
    def _():
        accumulate(q, far_k, far_v, m, acc, l)

    @pl.when(far_seen & (core == 1))
    def _():
        accumulate(q, relay_k, relay_v, m, acc, l)

    total = jnp.sum(l[...], axis=1, keepdims=True)
    out[...] = (acc[...] / total).astype(out.dtype)
    in_range = jnp.max(total) < LIMIT

    @pl.when(jnp.logical_not(in_range))
    def _():
        columns = pl.ds(pl.multiple_of(head * HD, HD), HD)

        def sweep(step):
            def run(seen, k_hbm, v_hbm, k_row, v_row):
                @pl.when(seen)
                def _():
                    copies = (
                        pltpu.make_async_copy(
                            k_hbm.at[pl.ds(k_row, FT), columns], k_buf, sem.at[0]
                        ),
                        pltpu.make_async_copy(
                            v_hbm.at[pl.ds(v_row, FT), columns], v_buf, sem.at[1]
                        ),
                    )
                    for copy in copies:
                        copy.start()
                    for copy in copies:
                        copy.wait()
                    step()

            run(core == 0, sink_a_hbm, sink_b_hbm, 0, 0)
            run(core == 1, sink_b_hbm, sink_a_hbm, 0, 0)
            run(visible(info, slot, first), key_hbm, value_hbm, 0, 0)
            run(visible(info, slot, first + 1), key_hbm, value_hbm, FT, FT)
            run(visible(info, slot, first - 1), near_k_hbm, near_v_hbm, FT, FT)
            run(visible(info, slot, first - 2), near_k_hbm, near_v_hbm, 0, 0)
            run(far_seen & (core == 0), far_hbm, far_hbm, 0, FT)
            run(far_seen & (core == 1), relay_hbm, relay_hbm, 0, FT)

        def peak():
            for i in range(FT // BQ):
                rows = slice(i * BQ, (i + 1) * BQ)
                s = qk(q[rows, :], k_buf[...]) * SCALE
                here = jnp.max(s, axis=1, keepdims=True)
                exact_m[rows, :] = jnp.maximum(exact_m[rows, :], here)

        exact_m[...] = jnp.full_like(exact_m, -jnp.inf)
        sweep(peak)
        acc[...] = jnp.zeros_like(acc)
        l[...] = jnp.zeros_like(l)
        sweep(lambda: accumulate(q, k_buf, v_buf, exact_m, acc, l))
        out[...] = (acc[...] / jnp.sum(l[...], axis=1, keepdims=True)).astype(out.dtype)


def frame_spec(row_block):
    return pl.BlockSpec((FT, HD), lambda h, s, info: (row_block, h))


SLOT_SPEC = pl.BlockSpec((FT, HD), lambda h, s, info: (s, h))
HBM_SPEC = pl.BlockSpec(memory_space=pl.ANY)


def stage(kernel, info, heads, arrays, in_specs, out_shape, pairs, scratch=()):
    flops = int(pairs * heads * 4 * FT * FT * HD * 2)
    grid_spec = pltpu.PrefetchScalarGridSpec(
        num_scalar_prefetch=1,
        grid=(heads, 2),
        in_specs=in_specs,
        out_specs=jax.tree.map(lambda _: SLOT_SPEC, out_shape),
        scratch_shapes=list(scratch),
    )
    return pl.pallas_call(
        kernel,
        grid_spec=grid_spec,
        out_shape=out_shape,
        compiler_params=pltpu.CompilerParams(vmem_limit_bytes=48 * 1024 * 1024),
        cost_estimate=pl.CostEstimate(
            flops=flops, bytes_accessed=16_000_000, transcendentals=int(pairs * heads * FT * FT)
        ),
    )(info, *arrays)


def sink_from_first(key_rows, value_rows, axis):
    size = lax.axis_size(axis)
    me = lax.axis_index(axis)
    core = me % 2
    moved = lax.ppermute(value_rows, axis, [(0, 1)])
    held = jnp.where(core == 0, key_rows, moved)
    bits = [1 << b for b in range(1, size.bit_length() - 1)]
    orders = (bits[::-1], [bits[0]] + bits[:0:-1])
    done = [0, 0]
    for step in range(len(bits)):
        pairs = []
        for which in (0, 1):
            bit = orders[which][step]
            holders = [i for i in range(0, size, 2) if i & ~done[which] == 0]
            pairs += [(i + which, (i | bit) + which) for i in holders]
            done[which] |= bit
        moved = lax.ppermute(held, axis, pairs)
        takes = jnp.zeros((), bool)
        for _, target in pairs:
            takes = takes | (me == target)
        held = jnp.where(takes, moved, held)
    other = lax.ppermute(held, axis, [(i, i ^ 1) for i in range(size)])
    return held, other


def local(query_states, key_states, value_states, win_start, group_end, out_weight):
    axis = "tm"
    size = lax.axis_size(axis)
    me = lax.axis_index(axis)
    heads = query_states.shape[1] // HD
    first = me * 2
    info = jnp.concatenate(
        [
            jnp.stack([first, lax.axis_index("head")]).astype(jnp.int32),
            win_start.astype(jnp.int32),
            group_end.astype(jnp.int32),
            jnp.stack([me % 2]).astype(jnp.int32),
        ]
    )

    sink_a, sink_b = sink_from_first(key_states[:FT], value_states[:FT], axis)
    onward = [(i, i + 1) for i in range(size - 1)]
    near_k = lax.ppermute(key_states, axis, onward)
    near_v = lax.ppermute(value_states, axis, onward)
    own_last = jnp.concatenate([key_states[FT:], value_states[FT:]], axis=0)
    far = lax.ppermute(own_last, axis, [(i, i + 2) for i in range(0, size - 2, 2)])
    near_last = jnp.concatenate([near_k[FT:], near_v[FT:]], axis=0)
    relay = lax.ppermute(near_last, axis, [(i, i + 1) for i in range(0, size, 2)])

    rows, width = query_states.shape
    wide = jax.ShapeDtypeStruct((rows, width), jnp.float32)
    m, acc, l = stage(
        local_kernel, info, heads,
        [query_states, key_states, value_states, key_states, value_states],
        [SLOT_SPEC, frame_spec(0), frame_spec(0), frame_spec(1), frame_spec(1)],
        (wide, wide, wide), 4,
    )
    acc, l = stage(
        near_kernel, info, heads,
        [query_states, near_k, near_v, near_k, near_v, m, acc, l],
        [SLOT_SPEC, frame_spec(0), frame_spec(0), frame_spec(1), frame_spec(1)] + [SLOT_SPEC] * 3,
        (wide, wide), 4,
    )
    attended = stage(
        final_kernel, info, heads,
        [query_states, sink_a, sink_b, far, far, relay, relay, m, acc, l,
         key_states, value_states, near_k, near_v, sink_a, sink_b, far, relay],
        [SLOT_SPEC, frame_spec(0), frame_spec(0), frame_spec(0), frame_spec(1),
         frame_spec(0), frame_spec(1)] + [SLOT_SPEC] * 3 + [HBM_SPEC] * 8,
        jax.ShapeDtypeStruct((rows, width), jnp.bfloat16), 3,
        [pltpu.VMEM((FT, HD), jnp.float32)] * 3
        + [pltpu.VMEM((FT, HD), jnp.bfloat16)] * 2
        + [pltpu.SemaphoreType.DMA((2,))],
    )
    token_rows = lax.all_to_all(attended, "head", split_axis=0, concat_axis=1, tiled=True)
    return jnp.dot(token_rows, out_weight, preferred_element_type=jnp.float32).astype(jnp.bfloat16)


def solution(mesh):
    in_specs = (P("tm", "head"), P("tm", "head"), P("tm", "head"), P("tm"), P("tm"), P())
    out_specs = P(("tm", "head"), None)
    return jax.shard_map(local, mesh=mesh, in_specs=in_specs, out_specs=out_specs, check_vma=False)
```

```python
import jax
import jax.numpy as jnp
from jax import lax
from jax.experimental import pallas as pl
from jax.experimental.pallas import tpu as pltpu
from jax.sharding import PartitionSpec as P

HD = 128
FT = 768
BK = 256
LOG2E = 1.4426950408889634
SCALE = HD ** -0.5 * LOG2E
LIMIT = 1e30
HIDDEN = 1e30
PARAMS = pltpu.CompilerParams(vmem_limit_bytes=56 * 1024 * 1024)
HBM_SPEC = pl.BlockSpec(memory_space=pltpu.HBM)
TOKEN = jax.ShapeDtypeStruct((8, 128), jnp.float32)
TOKEN_SPEC = pl.BlockSpec((8, 128), lambda *_: (0, 0))


def slot_rows(slot):
    return slice(slot * FT, (slot + 1) * FT)


def dot(a, b):
    return jnp.dot(a, b, preferred_element_type=jnp.float32)


def scores(q, kt, unit):
    slot, frame, j = unit
    return dot(q[slot_rows(slot), :], kt[frame, :, j * BK : (j + 1) * BK])


def accumulate(units, q, kt, values, shift, old, new, known=None):
    known = dict(known or {})
    seen = set()

    def get(unit):
        return known.pop(unit) if unit in known else scores(q, kt, unit)

    ahead = get(units[0])
    for n, (slot, frame, j) in enumerate(units):
        s = ahead
        if n + 1 < len(units):
            ahead = get(units[n + 1])
        rows = slot_rows(slot)
        acc_from, l_from = new if slot in seen else old
        seen.add(slot)
        row_shift = shift[frame, rows, :]
        parts = [
            jnp.exp2(s[:, c : c + 128] * SCALE - row_shift) for c in range(0, BK, 128)
        ]
        weights = jnp.concatenate([part.astype(jnp.bfloat16) for part in parts], axis=1)
        added = dot(weights, values[frame][j * BK : (j + 1) * BK, :])
        if acc_from is None:
            new[0][rows, :] = added
            new[1][rows, :] = sum(parts[1:], parts[0])
        else:
            new[0][rows, :] = acc_from[rows, :] + added
            new[1][rows, :] = sum(parts, l_from[rows, :])


def visible(info, slot, frame):
    return (frame >= 1) & (frame >= info[2 + slot]) & (frame <= info[4 + slot])


def set_shift(shift, frame, slot, seen, m):
    rows = slot_rows(slot)
    shift[frame, rows, :] = jnp.where(seen, m[rows, :], HIDDEN)


def blocks(slots, frames):
    return [(s, f, j) for f in frames for j in range(FT // BK) for s in slots]


def local_kernel(info, q, k, v, m, acc, l, token, kt, shift):
    first = info[0]
    token[...] = jnp.zeros_like(token)
    for frame in (0, 1):
        kt[frame] = k[slot_rows(frame), :].T
    known = {}
    for slot in (0, 1):
        unit = (slot, slot, 0)
        known[unit] = scores(q, kt, unit)
        peak = jnp.max(known[unit], axis=1, keepdims=True) * SCALE
        m[slot_rows(slot), :] = jnp.broadcast_to(peak, (FT, HD))
        for frame in (0, 1):
            set_shift(shift, frame, slot, visible(info, slot, first + frame), m)
    units = list(known)
    units += [unit for unit in blocks((0, 1), (0, 1)) if unit not in known]
    values = [v.at[slot_rows(frame)] for frame in (0, 1)]
    accumulate(units, q, kt, values, shift, (None, None), (acc, l), known)


def near_kernel(info, q, k, v, m, acc_in, l_in, acc, l, kt, shift):
    first = info[0]
    for frame in (0, 1):
        kt[frame] = k[slot_rows(frame), :].T
        for slot in (0, 1):
            set_shift(shift, frame, slot, visible(info, slot, first - 2 + frame), m)
    values = [v.at[slot_rows(frame)] for frame in (0, 1)]
    accumulate(blocks((0, 1), (1, 0)), q, kt, values, shift, (acc_in, l_in), (acc, l))


def by_core(info, kt, value, for_core_0, for_core_1):
    for core, (k, v) in ((0, for_core_0), (1, for_core_1)):

        @pl.when(info[6] == core)
        def _():
            kt[0] = k[...].T
            value[...] = v[...]


def sink_kernel(info, q, sink_a, sink_b, m, acc_in, l_in, acc, l, kt, value, shift):
    by_core(info, kt, value, (sink_a, sink_b), (sink_b, sink_a))
    for slot in (0, 1):
        set_shift(shift, 0, slot, True, m)
    accumulate(blocks((0, 1), (0,)), q, kt, [value], shift, (acc_in, l_in), (acc, l))


def far_kernel(offset, info, q, far_k, far_v, relay_k, relay_v, m, acc_in, l_in, *refs):
    key_hbm, value_hbm, near_k, near_v, sink_a, sink_b, far, relay = refs[:8]
    outs = refs[8:-6]
    acc, l, kt, value, shift, sem = refs[-6:]
    head = pl.program_id(0) + offset
    first = info[0]
    by_core(info, kt, value, (far_k, far_v), (relay_k, relay_v))
    far_seen = visible(info, 0, first - 3)
    set_shift(shift, 0, 0, far_seen, m)
    acc[slot_rows(1), :] = acc_in[slot_rows(1), :]
    l[slot_rows(1), :] = l_in[slot_rows(1), :]
    accumulate(blocks((0,), (0,)), q, kt, [value], shift, (acc_in, l_in), (acc, l))

    def write():
        largest = jnp.zeros((), jnp.float32)
        for slot in (0, 1):
            rows = slot_rows(slot)
            total = jnp.sum(l[rows, :], axis=1, keepdims=True)
            largest = jnp.maximum(largest, jnp.max(total))
            attended = (acc[rows, :] / total).astype(jnp.bfloat16)
            if len(outs) == 1:
                outs[0][rows, :] = attended
                continue

            @pl.when(info[1] == slot)
            def _():
                outs[0][...] = attended

            @pl.when(info[1] != slot)
            def _():
                outs[1][...] = attended

        return largest

    in_range = write() < LIMIT

    @pl.when(jnp.logical_not(in_range))
    def _():
        columns = pl.ds(pl.multiple_of(head * HD, HD), HD)

        def sweep(slot, step):
            def over(seen, k_hbm, k_row, v_hbm, v_row):
                @pl.when(seen)
                def _():
                    copy = pltpu.make_async_copy(
                        k_hbm.at[pl.ds(k_row, FT), columns], value, sem.at[0]
                    )
                    copy.start()
                    copy.wait()
                    kt[0] = value[...].T
                    copy = pltpu.make_async_copy(
                        v_hbm.at[pl.ds(v_row, FT), columns], value, sem.at[1]
                    )
                    copy.start()
                    copy.wait()
                    step()

            over(info[6] == 0, sink_a, 0, sink_b, 0)
            over(info[6] == 1, sink_b, 0, sink_a, 0)
            for frame in (0, 1):
                row = frame * FT
                over(visible(info, slot, first + frame), key_hbm, row, value_hbm, row)
                over(visible(info, slot, first - 2 + frame), near_k, row, near_v, row)
            if slot == 0:
                over(far_seen & (info[6] == 0), far, 0, far, FT)
                over(far_seen & (info[6] == 1), relay, 0, relay, FT)

        for slot in (0, 1):
            rows = slot_rows(slot)
            shift[0, rows, :] = jnp.full((FT, HD), -jnp.inf, jnp.float32)
            acc[rows, :] = jnp.zeros((FT, HD), jnp.float32)
            l[rows, :] = jnp.zeros((FT, HD), jnp.float32)

            def peak():
                for j in range(FT // BK):
                    s = scores(q, kt, (slot, 0, j))
                    here = jnp.max(s, axis=1, keepdims=True) * SCALE
                    shift[0, rows, :] = jnp.maximum(shift[0, rows, :], here)

            def add():
                accumulate(blocks((slot,), (0,)), q, kt, [value], shift, (acc, l), (acc, l))

            sweep(slot, peak)
            sweep(slot, add)
        write()


def stage(kernel, info, group, arrays, specs, outs, frames, scratch=(), token=False):
    offset, heads = group

    def spec(entry):
        if entry is None:
            return HBM_SPEC
        rows, block, whole = entry
        base = offset if whole else 0
        return pl.BlockSpec((rows, HD), lambda h, info: (block, h + base))

    shapes = [jax.ShapeDtypeStruct((rows, heads * HD), dtype) for rows, dtype in outs]
    return pl.pallas_call(
        kernel,
        grid_spec=pltpu.PrefetchScalarGridSpec(
            num_scalar_prefetch=1,
            grid=(heads,),
            in_specs=[spec(entry) for entry in specs],
            out_specs=[spec((rows, 0, False)) for rows, _ in outs] + [TOKEN_SPEC] * token,
            scratch_shapes=list(scratch)
            + [pltpu.VMEM((frames, HD, FT), jnp.bfloat16)]
            + ([pltpu.VMEM((FT, HD), jnp.bfloat16)] if frames == 1 else [])
            + [pltpu.VMEM((frames, 2 * FT, HD), jnp.float32)]
            + ([pltpu.SemaphoreType.DMA((2,))] if scratch else []),
        ),
        out_shape=shapes + [TOKEN] * token,
        compiler_params=PARAMS,
        cost_estimate=pl.CostEstimate(flops=1000, bytes_accessed=1000, transcendentals=0),
    )(info, *arrays)


def copies(plan, arrays, outs, flags=None, tokens=()):
    n = len(arrays)

    def kernel(flags, *refs):
        sem = refs[-1]
        listed = plan(refs[:n], refs[n + len(tokens) : -1], flags)

        def guarded(act):
            for i, (condition, source, target) in enumerate(listed):
                copy = pltpu.make_async_copy(source, target, sem.at[i])
                if condition is None:
                    act(copy)
                else:
                    pl.when(condition)(lambda copy=copy: act(copy))

        guarded(lambda copy: copy.start())
        guarded(lambda copy: copy.wait())

    shapes = [jax.ShapeDtypeStruct(shape, jnp.bfloat16) for shape in outs]
    return pl.pallas_call(
        kernel,
        grid_spec=pltpu.PrefetchScalarGridSpec(
            num_scalar_prefetch=1,
            grid=(1,),
            in_specs=[HBM_SPEC] * n + [TOKEN_SPEC] * len(tokens),
            out_specs=[HBM_SPEC] * len(outs),
            scratch_shapes=[pltpu.SemaphoreType.DMA((4,))],
        ),
        out_shape=shapes,
        compiler_params=PARAMS,
        cost_estimate=pl.CostEstimate(flops=0, bytes_accessed=1000, transcendentals=0),
    )(jnp.zeros((1,), jnp.int32) if flags is None else flags, *arrays, *tokens)


def pick(flag, taken, kept, waits_for):
    def plan(sources, outs, flags):
        return [
            (flags[0] == 1, sources[0], outs[0]),
            (flags[0] == 0, sources[1], outs[0]),
        ]

    flag = jnp.reshape(flag, (1,)).astype(jnp.int32)
    return copies(plan, [taken, kept], [taken.shape], flag, waits_for)[0]


def sink_steps(size):
    bits = [1 << b for b in range(1, size.bit_length() - 1)]
    orders = (bits[::-1], [bits[0]] + bits[:0:-1])
    done = [0, 0]
    steps = []
    for step in range(len(bits)):
        pairs = []
        for which in (0, 1):
            bit = orders[which][step]
            holders = [i for i in range(0, size, 2) if i & ~done[which] == 0]
            pairs += [(i + which, (i | bit) + which) for i in holders]
            done[which] |= bit
        steps.append(pairs)
    return steps


def project(info, parts, base, weight, out_dtype, rows, total_rows):
    columns = weight.shape[1]
    block = columns // 3
    depth = parts[0][0].shape[1]
    per_device = weight.shape[0] // 2 // depth
    n = len(parts)

    def kernel(info, *refs):
        total = refs[2 * n][...] if base is not None else None
        for a, w in zip(refs[:n], refs[n : 2 * n]):
            product = dot(a[...], w[...])
            total = product if total is None else total + product
        refs[-1][...] = total.astype(out_dtype)

    def weight_spec(part, other):
        def index(n, info):
            owner = 1 - info[1] if other else info[1]
            return (owner * per_device + part, n)

        return pl.BlockSpec((depth, block), index)

    out_spec = pl.BlockSpec((rows, block), lambda n, info: (0, n))
    return pl.pallas_call(
        kernel,
        grid_spec=pltpu.PrefetchScalarGridSpec(
            num_scalar_prefetch=1,
            grid=(3,),
            in_specs=[pl.BlockSpec((rows, depth), lambda n, info: (0, 0))] * n
            + [weight_spec(part, other) for _, part, other in parts]
            + ([out_spec] if base is not None else []),
            out_specs=out_spec,
        ),
        out_shape=jax.ShapeDtypeStruct((rows, columns), out_dtype),
        compiler_params=PARAMS,
        cost_estimate=pl.CostEstimate(
            flops=n * 2 * rows * depth * columns, bytes_accessed=8_000_000, transcendentals=0
        ),
    )(info, *[a for a, _, _ in parts], *[weight] * n, *([base] if base is not None else []))


def local(query_states, key_states, value_states, win_start, group_end, out_weight):
    axis = "tm"
    size = lax.axis_size(axis)
    over_head = lax.axis_size("head")
    me = lax.axis_index(axis)
    core = me % 2
    rows, width = query_states.shape
    heads = width // HD
    info = jnp.concatenate(
        [
            jnp.stack([me * 2, lax.axis_index("head")]).astype(jnp.int32),
            win_start.astype(jnp.int32),
            group_end.astype(jnp.int32),
            jnp.stack([core]).astype(jnp.int32),
        ]
    )
    frame_shape, unit_shape = (FT, width), (2 * FT, width)
    groups = [(0, heads // 2), (heads // 2, heads // 2)] if heads % 2 == 0 else [(0, heads)]
    both = (2 * FT, 0, True)
    state = [(2 * FT, 0, False)] * 3
    state_out = [(2 * FT, jnp.float32)] * 2

    onward = [(i, i + 1) for i in range(size - 1)]
    near_k = lax.ppermute(key_states, axis, onward)
    near_v = lax.ppermute(value_states, axis, onward)

    def last_frame(k, v, out):
        last = pl.ds(FT, FT)
        return [(None, k.at[last], out.at[pl.ds(0, FT)]), (None, v.at[last], out.at[last])]

    first_v, own_last = copies(
        lambda refs, outs, flags: [(None, refs[1].at[pl.ds(0, FT)], outs[0])]
        + last_frame(refs[0], refs[1], outs[1]),
        [key_states, value_states], [frame_shape, unit_shape],
    )
    moved = lax.ppermute(first_v, axis, [(0, 1)])

    def local_stage(group):
        return stage(
            local_kernel, info, group, [query_states, key_states, value_states], [both] * 3,
            [(2 * FT, jnp.float32)] * 3, 2, token=True,
        )

    states = []
    held = copies(
        lambda refs, outs, flags: [
            (flags[0] == 0, refs[0].at[pl.ds(0, FT)], outs[0]),
            (flags[0] == 1, refs[1], outs[0]),
        ],
        [key_states, moved], [frame_shape],
        jnp.reshape(core, (1,)).astype(jnp.int32),
    )[0]
    for step, pairs in enumerate(sink_steps(size)):
        moved = lax.ppermute(held, axis, pairs)
        waits_for = []
        if step < len(groups):
            states.append(local_stage(groups[step]))
            waits_for = [states[step][3]]
        takes = jnp.zeros((), bool)
        for _, target in pairs:
            takes = takes | (me == target)
        held = pick(takes, moved, held, waits_for)
    other = lax.ppermute(held, axis, [(i, i ^ 1) for i in range(size)])

    near_last = copies(
        lambda refs, outs, flags: last_frame(refs[0], refs[1], outs[0]),
        [near_k, near_v], [unit_shape],
    )[0]
    relay = lax.ppermute(near_last, axis, [(i, i + 1) for i in range(0, size, 2)])
    far = lax.ppermute(own_last, axis, [(i, i + 2) for i in range(0, size - 2, 2)])

    for g, group in enumerate(groups):
        m, acc, l = states[g][:3]
        acc, l = stage(
            near_kernel, info, group, [query_states, near_k, near_v, m, acc, l],
            [both] * 3 + state, state_out, 2,
        )
        states[g] = m, acc, l
    one = (FT, 0, True)
    two = (FT, 1, True)
    for g, group in enumerate(groups):
        m, acc, l = states[g]
        acc, l = stage(
            sink_kernel, info, group, [query_states, held, other, m, acc, l],
            [both, one, one] + state, state_out, 1,
        )
        states[g] = m, acc, l
    paired = over_head == 2
    mine, theirs = [], []
    for g, group in enumerate(groups):
        outs = [(FT, jnp.bfloat16)] * 2 if paired else [(2 * FT, jnp.bfloat16)]
        results = stage(
            lambda *refs, offset=group[0]: far_kernel(offset, *refs), info, group,
            [query_states, far, far, relay, relay, *states[g],
             key_states, value_states, near_k, near_v, held, other, far, relay],
            [both, one, two, one, two] + state + [None] * 8, outs, 1,
            [pltpu.VMEM((2 * FT, HD), jnp.float32)] * 2,
        )
        mine.append(results[0])
        if paired:
            theirs.append(lax.ppermute(results[1], "head", [(0, 1), (1, 0)]))
    if not paired:
        attended = jnp.concatenate(mine, axis=1)
        token_rows = lax.all_to_all(attended, "head", split_axis=0, concat_axis=1, tiled=True)
        return dot(token_rows, out_weight).astype(jnp.bfloat16)
    own = [(array, g, False) for g, array in enumerate(mine)]
    received = [(array, g, True) for g, array in enumerate(theirs)]
    base = project(info, own, None, out_weight, jnp.float32, FT, rows)
    return project(info, received, base, out_weight, jnp.bfloat16, FT, rows)


def solution(mesh):
    in_specs = (P("tm", "head"), P("tm", "head"), P("tm", "head"), P("tm"), P("tm"), P())
    out_specs = P(("tm", "head"), None)
    return jax.shard_map(local, mesh=mesh, in_specs=in_specs, out_specs=out_specs, check_vma=False)
```

```python
import jax
import jax.numpy as jnp
from jax import lax
from jax.experimental import pallas as pl
from jax.experimental.pallas import tpu as pltpu
from jax.sharding import PartitionSpec as P

HD = 128
FT = 768
BK = 256
LOG2E = 1.4426950408889634
SCALE = HD ** -0.5 * LOG2E
LIMIT = 1e30
HIDDEN = 1e30
PARAMS = pltpu.CompilerParams(vmem_limit_bytes=28 * 1024 * 1024)
ANY_SPEC = pl.BlockSpec(memory_space=pl.ANY)
COST = pl.CostEstimate(flops=1000, bytes_accessed=1000, transcendentals=0)
TOKEN = jax.ShapeDtypeStruct((8, 128), jnp.float32)
TOKEN_SPEC = pl.BlockSpec((8, 128), lambda *_: (0, 0))


def dot(a, b):
    return jnp.dot(a, b, preferred_element_type=jnp.float32)


def scores(q, kt, unit):
    frame, j = unit
    return dot(q[...], kt[frame, :, j * BK : (j + 1) * BK])


def blocks(*frames):
    return [(frame, j) for frame in frames for j in range(FT // BK)]


def accumulate(units, q, kt, values, shift, old, new, known=None):
    ahead = scores(q, kt, units[0]) if known is None else known
    for n, (frame, j) in enumerate(units):
        s = ahead
        if n + 1 < len(units):
            ahead = scores(q, kt, units[n + 1])
        row_shift = shift[frame]
        parts = [
            jnp.exp2(s[:, c : c + 128] * SCALE - row_shift) for c in range(0, BK, 128)
        ]
        weights = jnp.concatenate([part.astype(jnp.bfloat16) for part in parts], axis=1)
        added = dot(weights, values[frame][j * BK : (j + 1) * BK, :])
        acc_from, l_from = old if n == 0 else new
        if acc_from is None:
            new[0][...] = added
            new[1][...] = sum(parts[1:], parts[0])
        else:
            new[0][...] = acc_from[...] + added
            new[1][...] = sum(parts, l_from[...])


def visible(info, slot, frame):
    return (frame >= 1) & (frame >= info[2 + slot]) & (frame <= info[4 + slot])


def set_shift(shift, frame, seen, m):
    shift[frame] = jnp.where(seen, m[...].astype(jnp.float32), HIDDEN)


def transposed(slot, kt, keys):
    @pl.when(slot == 0)
    def _():
        for frame, k in enumerate(keys):
            kt[frame] = k[...].T


def local_kernel(info, q, k0, k1, v0, v1, m, acc, l, token, kt, shift):
    slot = pl.program_id(1)
    first = info[0]
    token[...] = jnp.zeros_like(token)
    transposed(slot, kt, (k0, k1))

    def run(own):
        known = scores(q, kt, (own, 0))
        peak = jnp.max(known, axis=1, keepdims=True) * SCALE
        m[...] = jnp.broadcast_to(peak, (FT, HD)).astype(m.dtype)
        for frame in (0, 1):
            set_shift(shift, frame, visible(info, own, first + frame), m)
        units = blocks(own, 1 - own)
        accumulate(units, q, kt, (v0, v1), shift, (None, None), (acc, l), known)

    pl.when(slot == 0)(lambda: run(0))
    pl.when(slot == 1)(lambda: run(1))


def near_kernel(info, q, k0, k1, v0, v1, m, acc_in, l_in, acc, l, kt, shift):
    slot = pl.program_id(1)
    first = info[0]
    transposed(slot, kt, (k0, k1))
    for frame in (0, 1):
        set_shift(shift, frame, visible(info, slot, first - 2 + frame), m)
    accumulate(blocks(1, 0), q, kt, (v0, v1), shift, (acc_in, l_in), (acc, l))


def final_kernel(
    offset, info, q, sink_a, sink_b, far_k, far_v, relay_k, relay_v, m, acc_in, l_in,
    key_hbm, value_hbm, near_k, near_v, sink_a_hbm, sink_b_hbm, far, relay, *refs,
):
    outs = refs[:-7]
    acc, l, sem, kt, shift, values, k_buf = refs[-7:]
    head = pl.program_id(0) + offset
    slot = pl.program_id(1)
    first = info[0]
    core = info[6]

    @pl.when(slot == 0)
    def _():
        for here, listed in (
            (0, (sink_a, sink_b, far_k, far_v)),
            (1, (sink_b, sink_a, relay_k, relay_v)),
        ):

            @pl.when(core == here)
            def _():
                for frame in (0, 1):
                    kt[frame] = listed[2 * frame][...].T
                    values[frame] = listed[2 * frame + 1][...]

    far_seen = (slot == 0) & visible(info, slot, first - 3)
    set_shift(shift, 0, True, m)

    @pl.when(slot == 0)
    def _():
        set_shift(shift, 1, far_seen, m)
        accumulate(blocks(0, 1), q, kt, values, shift, (acc_in, l_in), (acc, l))

    @pl.when(slot == 1)
    def _():
        accumulate(blocks(0), q, kt, values, shift, (acc_in, l_in), (acc, l))

    def write():
        total = jnp.sum(l[...], axis=1, keepdims=True)
        attended = (acc[...] / total).astype(jnp.bfloat16)
        if len(outs) == 1:
            outs[0][pl.ds(pl.multiple_of(slot * FT, FT), FT), :] = attended
        else:

            @pl.when(info[1] == slot)
            def _():
                outs[0][...] = attended

            @pl.when(info[1] != slot)
            def _():
                outs[1][...] = attended

        return jnp.max(total)

    in_range = write() < LIMIT

    @pl.when(jnp.logical_not(in_range))
    def _():
        columns = pl.ds(pl.multiple_of(head * HD, HD), HD)
        sources = [
            (core == 0, sink_a_hbm, 0, sink_b_hbm, 0),
            (core == 1, sink_b_hbm, 0, sink_a_hbm, 0),
            (far_seen & (core == 0), far, 0, far, FT),
            (far_seen & (core == 1), relay, 0, relay, FT),
        ]
        for frame in (0, 1):
            row = frame * FT
            own = visible(info, slot, first + frame)
            sources.append((own, key_hbm, row, value_hbm, row))
            behind = visible(info, slot, first - 2 + frame)
            sources.append((behind, near_k, row, near_v, row))

        def sweep(step):
            def turn(t, carry):
                seen = False
                for i, (shown, k_hbm, k_row, v_hbm, v_row) in enumerate(sources):
                    chosen = (t == i) & shown
                    seen = seen | chosen

                    @pl.when(chosen)
                    def _():
                        pairs = ((k_hbm, k_row, k_buf), (v_hbm, v_row, values.at[0]))
                        for n, (hbm, row, buf) in enumerate(pairs):
                            copy = pltpu.make_async_copy(
                                hbm.at[pl.ds(row, FT), columns], buf, sem.at[n]
                            )
                            copy.start()
                            copy.wait()

                @pl.when(seen)
                def _():
                    kt[0] = k_buf[...].T
                    step()

                return carry

            lax.fori_loop(0, len(sources), turn, 0)

        def peak():
            for unit in blocks(0):
                here = jnp.max(scores(q, kt, unit), axis=1, keepdims=True) * SCALE
                shift[0] = jnp.maximum(shift[0], here)

        shift[0] = jnp.full((FT, HD), -jnp.inf, jnp.float32)
        acc[...] = jnp.zeros((FT, HD), jnp.float32)
        l[...] = jnp.zeros((FT, HD), jnp.float32)
        sweep(peak)
        sweep(lambda: accumulate(blocks(0), q, kt, values, shift, (acc, l), (acc, l)))
        write()

        @pl.when(slot == 0)
        def _():
            for here, (k, v) in ((0, (sink_a, sink_b)), (1, (sink_b, sink_a))):

                @pl.when(core == here)
                def _():
                    kt[0] = k[...].T
                    values[0] = v[...]


SLOT = "slot"


def stage(kernel, info, group, arrays, specs, outs, scratch=(), token=False):
    offset, heads = group

    def spec(entry):
        if entry is None:
            return ANY_SPEC
        block, whole = entry
        base = offset if whole else 0
        if block == SLOT:
            return pl.BlockSpec((FT, HD), lambda h, s, info: (s, h + base))
        return pl.BlockSpec((FT, HD), lambda h, s, info: (block, h + base))

    out_specs, shapes = [], []
    for rows, dtype, block in outs:
        shapes.append(jax.ShapeDtypeStruct((rows, heads * HD), dtype))
        if block is None:
            out_specs.append(pl.BlockSpec((rows, HD), lambda h, s, info: (0, h)))
        else:
            out_specs.append(spec((block, False)))
    return pl.pallas_call(
        kernel,
        grid_spec=pltpu.PrefetchScalarGridSpec(
            num_scalar_prefetch=1,
            grid=(heads, 2),
            in_specs=[spec(entry) for entry in specs],
            out_specs=out_specs + [TOKEN_SPEC] * token,
            scratch_shapes=list(scratch)
            + [
                pltpu.VMEM((2, HD, FT), jnp.bfloat16),
                pltpu.VMEM((2, FT, HD), jnp.float32),
            ]
            + ([pltpu.VMEM((2, FT, HD), jnp.bfloat16), pltpu.VMEM((FT, HD), jnp.bfloat16)]
               if scratch else []),
        ),
        out_shape=shapes + [TOKEN] * token,
        compiler_params=PARAMS,
        cost_estimate=COST,
    )(info, *arrays)


def pick(flag, taken, kept, tokens=()):
    flag = jnp.reshape(flag, (1,)).astype(jnp.int32)
    rows, width = taken.shape
    turns = 3
    block = rows // turns

    def kernel(flag, taken, kept, *refs):
        out = refs[-1]

        @pl.when(flag[0] == 1)
        def _():
            out[...] = taken[...]

        @pl.when(flag[0] == 0)
        def _():
            out[...] = kept[...]

    def spec(index):
        return pl.BlockSpec((block, width), index)

    return pl.pallas_call(
        kernel,
        grid_spec=pltpu.PrefetchScalarGridSpec(
            num_scalar_prefetch=1,
            grid=(turns,),
            in_specs=[
                spec(lambda i, flag: (i * flag[0], 0)), spec(lambda i, flag: (i - i * flag[0], 0))
            ] + [TOKEN_SPEC] * len(tokens),
            out_specs=spec(lambda i, flag: (i, 0)),
        ),
        out_shape=jax.ShapeDtypeStruct((rows, width), taken.dtype),
        compiler_params=PARAMS,
        cost_estimate=COST,
    )(flag, taken, kept, *tokens)


def last_frames(keys, values):
    width = keys.shape[1]
    turns = 4
    block = 2 * FT // turns

    def kernel(keys, values, out):
        i = pl.program_id(0)

        @pl.when(i < turns // 2)
        def _():
            out[...] = keys[...]

        @pl.when(i >= turns // 2)
        def _():
            out[...] = values[...]

    def spec(index):
        return pl.BlockSpec((block, width), index)

    half = turns // 2
    return pl.pallas_call(
        kernel,
        grid=(turns,),
        in_specs=[
            spec(lambda i: (half + jnp.minimum(i, half - 1), 0)),
            spec(lambda i: (jnp.maximum(i, half), 0)),
        ],
        out_specs=spec(lambda i: (i, 0)),
        out_shape=jax.ShapeDtypeStruct((2 * FT, width), keys.dtype),
        compiler_params=PARAMS,
        cost_estimate=COST,
    )(keys, values)


def sink_steps(size):
    bits = [1 << b for b in range(1, size.bit_length() - 1)]
    orders = (bits[::-1], [bits[0]] + bits[:0:-1])
    done = [0, 0]
    steps = []
    for step in range(len(bits)):
        pairs = []
        for which in (0, 1):
            bit = orders[which][step]
            holders = [i for i in range(0, size, 2) if i & ~done[which] == 0]
            pairs += [(i + which, (i | bit) + which) for i in holders]
            done[which] |= bit
        steps.append(pairs)
    return steps


def project(info, parts, weight):
    columns = weight.shape[1]
    turns = 6
    block = columns // turns
    rows, depth = parts[0][0].shape
    per_device = weight.shape[0] // 2 // depth
    n = len(parts)

    def kernel(info, *refs):
        products = [dot(a[...], w[...]) for a, w in zip(refs[:n], refs[n : 2 * n])]
        refs[-1][...] = sum(products[1:], products[0]).astype(jnp.bfloat16)

    def weight_spec(part, received):
        def index(i, info):
            owner = 1 - info[1] if received else info[1]
            return (owner * per_device + part, i)

        return pl.BlockSpec((depth, block), index)

    return pl.pallas_call(
        kernel,
        grid_spec=pltpu.PrefetchScalarGridSpec(
            num_scalar_prefetch=1,
            grid=(turns,),
            in_specs=[pl.BlockSpec((rows, depth), lambda i, info: (0, 0))] * n
            + [weight_spec(part, received) for _, part, received in parts],
            out_specs=pl.BlockSpec((rows, block), lambda i, info: (0, i)),
        ),
        out_shape=jax.ShapeDtypeStruct((rows, columns), jnp.bfloat16),
        compiler_params=PARAMS,
        cost_estimate=COST,
    )(info, *[a for a, _, _ in parts], *[weight] * n)


def local(query_states, key_states, value_states, win_start, group_end, out_weight):
    axis = "tm"
    size = lax.axis_size(axis)
    paired = lax.axis_size("head") == 2
    me = lax.axis_index(axis)
    core = me % 2
    heads = query_states.shape[1] // HD
    info = jnp.concatenate(
        [
            jnp.stack([me * 2, lax.axis_index("head")]).astype(jnp.int32),
            win_start.astype(jnp.int32),
            group_end.astype(jnp.int32),
            jnp.stack([core]).astype(jnp.int32),
        ]
    )
    groups = [(0, heads // 2), (heads // 2, heads // 2)] if heads % 2 == 0 else [(0, heads)]
    slot_all, slot_part = (SLOT, True), (SLOT, False)
    frames = [(0, True), (1, True)]
    sums = [(2 * FT, jnp.float32, SLOT)] * 2

    onward = [(i, i + 1) for i in range(size - 1)]
    near_k = lax.ppermute(key_states, axis, onward)
    near_v = lax.ppermute(value_states, axis, onward)

    def local_stage(group):
        return stage(
            local_kernel, info, group,
            [query_states, key_states, key_states, value_states, value_states],
            [slot_all] + frames * 2, [(2 * FT, jnp.bfloat16, SLOT)] + sums, token=True,
        )

    moved = lax.ppermute(value_states[:FT], axis, [(0, 1)])
    held = pick(core, moved, key_states[:FT])
    states = []
    for step, pairs in enumerate(sink_steps(size)):
        moved = lax.ppermute(held, axis, pairs)
        tokens = []
        if step < len(groups):
            *state, token = local_stage(groups[step])
            states.append(state)
            tokens = [token]
        takes = jnp.zeros((), bool)
        for _, target in pairs:
            takes = takes | (me == target)
        held = pick(takes, moved, held, tokens)
    other = lax.ppermute(held, axis, [(i, i ^ 1) for i in range(size)])

    own_last = last_frames(key_states, value_states)
    far = lax.ppermute(own_last, axis, [(i, i + 2) for i in range(0, size - 2, 2)])
    near_last = last_frames(near_k, near_v)
    relay = lax.ppermute(near_last, axis, [(i, i + 1) for i in range(0, size, 2)])

    for g, group in enumerate(groups):
        m, acc, l = states[g]
        acc, l = stage(
            near_kernel, info, group, [query_states, near_k, near_k, near_v, near_v, m, acc, l],
            [slot_all] + frames * 2 + [slot_part] * 3, sums,
        )
        states[g] = m, acc, l
    mine, theirs = [], []
    for g, group in enumerate(groups):
        outs = [(FT, jnp.bfloat16, 0)] * 2 if paired else [(2 * FT, jnp.bfloat16, None)]
        results = stage(
            lambda *refs, offset=group[0]: final_kernel(offset, *refs), info, group,
            [query_states, held, other, far, far, relay, relay, *states[g],
             key_states, value_states, near_k, near_v, held, other, far, relay],
            [slot_all, frames[0], frames[0]] + frames * 2 + [slot_part] * 3 + [None] * 8, outs,
            [pltpu.VMEM((FT, HD), jnp.float32)] * 2 + [pltpu.SemaphoreType.DMA((2,))],
        )
        mine.append(results[0])
        if paired:
            theirs.append(lax.ppermute(results[1], "head", [(0, 1), (1, 0)]))
    if not paired:
        attended = jnp.concatenate(mine, axis=1)
        token_rows = lax.all_to_all(attended, "head", split_axis=0, concat_axis=1, tiled=True)
        return dot(token_rows, out_weight).astype(jnp.bfloat16)
    parts = [(array, g, False) for g, array in enumerate(mine)]
    parts += [(array, g, True) for g, array in enumerate(theirs)]
    return project(info, parts, out_weight)


def solution(mesh):
    in_specs = (P("tm", "head"), P("tm", "head"), P("tm", "head"), P("tm"), P("tm"), P())
    out_specs = P(("tm", "head"), None)
    return jax.shard_map(local, mesh=mesh, in_specs=in_specs, out_specs=out_specs, check_vma=False)
```

```python
import jax
import jax.numpy as jnp
from jax import lax
from jax.experimental import pallas as pl
from jax.experimental.pallas import tpu as pltpu
from jax.sharding import PartitionSpec as P

HD = 128
FT = 768
BK = 256
LOG2E = 1.4426950408889634
SCALE = HD ** -0.5 * LOG2E
LIMIT = 1e30
HIDDEN = 1e30
PARAMS = pltpu.CompilerParams(vmem_limit_bytes=56 * 1024 * 1024)
ANY_SPEC = pl.BlockSpec(memory_space=pl.ANY)
COST = pl.CostEstimate(flops=1000, bytes_accessed=1000, transcendentals=0)
TOKEN = jax.ShapeDtypeStruct((8, 128), jnp.float32)
TOKEN_SPEC = pl.BlockSpec((8, 128), lambda *_: (0, 0))


def dot(a, b):
    return jnp.dot(a, b, preferred_element_type=jnp.float32)


def scores(q, kt, unit):
    frame, j = unit
    return dot(q[...], kt[frame, :, j * BK : (j + 1) * BK])


def blocks(*frames):
    return [(frame, j) for frame in frames for j in range(FT // BK)]


def accumulate(units, q, kt, values, shift, old, new, known=None):
    ahead = scores(q, kt, units[0]) if known is None else known
    for n, (frame, j) in enumerate(units):
        s = ahead
        if n + 1 < len(units):
            ahead = scores(q, kt, units[n + 1])
        row_shift = shift[frame]
        parts = [
            jnp.exp2(s[:, c : c + 128] * SCALE - row_shift) for c in range(0, BK, 128)
        ]
        weights = jnp.concatenate([part.astype(jnp.bfloat16) for part in parts], axis=1)
        added = dot(weights, values[frame][j * BK : (j + 1) * BK, :])
        acc_from, l_from = old if n == 0 else new
        if acc_from is None:
            new[0][...] = added
            new[1][...] = sum(parts[1:], parts[0])
        else:
            new[0][...] = acc_from[...] + added
            new[1][...] = sum(parts, l_from[...])


def visible(info, slot, frame):
    return (frame >= 1) & (frame >= info[2 + slot]) & (frame <= info[4 + slot])


def set_shift(shift, frame, seen, m):
    shift[frame] = jnp.where(seen, m[...].astype(jnp.float32), HIDDEN)


def transposed(slot, kt, keys):
    @pl.when(slot == 0)
    def _():
        for frame, k in enumerate(keys):
            kt[frame] = k[...].T


def local_kernel(info, q, k0, k1, v0, v1, m, acc, l, token, kt, shift):
    slot = pl.program_id(1)
    first = info[0]
    token[...] = jnp.zeros_like(token)
    transposed(slot, kt, (k0, k1))

    def run(own):
        known = scores(q, kt, (own, 0))
        peak = jnp.max(known, axis=1, keepdims=True) * SCALE
        m[...] = jnp.broadcast_to(peak, (FT, HD)).astype(m.dtype)
        for frame in (0, 1):
            set_shift(shift, frame, visible(info, own, first + frame), m)
        units = blocks(own, 1 - own)
        accumulate(units, q, kt, (v0, v1), shift, (None, None), (acc, l), known)

    pl.when(slot == 0)(lambda: run(0))
    pl.when(slot == 1)(lambda: run(1))


def near_kernel(info, q, k0, k1, v0, v1, m, acc_in, l_in, acc, l, token, kt, shift):
    slot = pl.program_id(1)
    token[...] = jnp.zeros_like(token)
    first = info[0]
    transposed(slot, kt, (k0, k1))
    for frame in (0, 1):
        set_shift(shift, frame, visible(info, slot, first - 2 + frame), m)
    accumulate(blocks(1, 0), q, kt, (v0, v1), shift, (acc_in, l_in), (acc, l))


def final_kernel(
    offset, info, q, sink_a, sink_b, far_k, far_v, relay_k, relay_v, m, acc_in, l_in,
    key_hbm, value_hbm, near_k, near_v, sink_a_hbm, sink_b_hbm, far, relay, *refs,
):
    outs = refs[:-7]
    acc, l, sem, kt, shift, values, k_buf = refs[-7:]
    head = pl.program_id(0) + offset
    slot = pl.program_id(1)
    first = info[0]
    core = info[6]

    @pl.when(slot == 0)
    def _():
        for here, listed in (
            (0, (sink_a, sink_b, far_k, far_v)),
            (1, (sink_b, sink_a, relay_k, relay_v)),
        ):

            @pl.when(core == here)
            def _():
                for frame in (0, 1):
                    kt[frame] = listed[2 * frame][...].T
                    values[frame] = listed[2 * frame + 1][...]

    far_seen = (slot == 0) & visible(info, slot, first - 3)
    set_shift(shift, 0, True, m)

    @pl.when(slot == 0)
    def _():
        set_shift(shift, 1, far_seen, m)
        accumulate(blocks(0, 1), q, kt, values, shift, (acc_in, l_in), (acc, l))

    @pl.when(slot == 1)
    def _():
        accumulate(blocks(0), q, kt, values, shift, (acc_in, l_in), (acc, l))

    def write():
        total = jnp.sum(l[...], axis=1, keepdims=True)
        attended = (acc[...] / total).astype(jnp.bfloat16)
        if len(outs) == 1:
            outs[0][pl.ds(pl.multiple_of(slot * FT, FT), FT), :] = attended
        else:

            @pl.when(info[1] == slot)
            def _():
                outs[0][...] = attended

            @pl.when(info[1] != slot)
            def _():
                outs[1][...] = attended

        return jnp.max(total)

    in_range = write() < LIMIT

    @pl.when(jnp.logical_not(in_range))
    def _():
        columns = pl.ds(pl.multiple_of(head * HD, HD), HD)
        sources = [
            (core == 0, sink_a_hbm, 0, sink_b_hbm, 0),
            (core == 1, sink_b_hbm, 0, sink_a_hbm, 0),
            (far_seen & (core == 0), far, 0, far, FT),
            (far_seen & (core == 1), relay, 0, relay, FT),
        ]
        for frame in (0, 1):
            row = frame * FT
            own = visible(info, slot, first + frame)
            sources.append((own, key_hbm, row, value_hbm, row))
            behind = visible(info, slot, first - 2 + frame)
            sources.append((behind, near_k, row, near_v, row))

        def sweep(step):
            def turn(t, carry):
                seen = False
                for i, (shown, k_hbm, k_row, v_hbm, v_row) in enumerate(sources):
                    chosen = (t == i) & shown
                    seen = seen | chosen

                    @pl.when(chosen)
                    def _():
                        pairs = ((k_hbm, k_row, k_buf), (v_hbm, v_row, values.at[0]))
                        for n, (hbm, row, buf) in enumerate(pairs):
                            copy = pltpu.make_async_copy(
                                hbm.at[pl.ds(row, FT), columns], buf, sem.at[n]
                            )
                            copy.start()
                            copy.wait()

                @pl.when(seen)
                def _():
                    kt[0] = k_buf[...].T
                    step()

                return carry

            lax.fori_loop(0, len(sources), turn, 0)

        def peak():
            for unit in blocks(0):
                here = jnp.max(scores(q, kt, unit), axis=1, keepdims=True) * SCALE
                shift[0] = jnp.maximum(shift[0], here)

        shift[0] = jnp.full((FT, HD), -jnp.inf, jnp.float32)
        acc[...] = jnp.zeros((FT, HD), jnp.float32)
        l[...] = jnp.zeros((FT, HD), jnp.float32)
        sweep(peak)
        sweep(lambda: accumulate(blocks(0), q, kt, values, shift, (acc, l), (acc, l)))
        write()

        @pl.when(slot == 0)
        def _():
            for here, (k, v) in ((0, (sink_a, sink_b)), (1, (sink_b, sink_a))):

                @pl.when(core == here)
                def _():
                    kt[0] = k[...].T
                    values[0] = v[...]


SLOT = "slot"


def stage(kernel, info, group, arrays, specs, outs, scratch=(), token=False):
    offset, heads = group

    def spec(entry):
        if entry is None:
            return ANY_SPEC
        block, whole = entry
        base = offset if whole else 0
        if block == SLOT and whole:
            return pl.BlockSpec((FT, HD), lambda h, s, info: (s, h + base))
        if block == SLOT:
            return pl.BlockSpec((None, FT, HD), lambda h, s, info: (h, s, 0))
        return pl.BlockSpec((FT, HD), lambda h, s, info: (block, h + base))

    out_specs, shapes = [], []
    for rows, dtype, block in outs:
        by_head = block == SLOT
        shape = (heads, rows, HD) if by_head else (rows, heads * HD)
        shapes.append(jax.ShapeDtypeStruct(shape, dtype))
        if block is None:
            out_specs.append(pl.BlockSpec((rows, HD), lambda h, s, info: (0, h)))
        else:
            out_specs.append(spec((block, False)))
    return pl.pallas_call(
        kernel,
        grid_spec=pltpu.PrefetchScalarGridSpec(
            num_scalar_prefetch=1,
            grid=(heads, 2),
            in_specs=[spec(entry) for entry in specs],
            out_specs=out_specs + [TOKEN_SPEC] * token,
            scratch_shapes=list(scratch)
            + [
                pltpu.VMEM((2, HD, FT), jnp.bfloat16),
                pltpu.VMEM((2, FT, HD), jnp.float32),
            ]
            + ([pltpu.VMEM((2, FT, HD), jnp.bfloat16), pltpu.VMEM((FT, HD), jnp.bfloat16)]
               if scratch else []),
        ),
        out_shape=shapes + [TOKEN] * token,
        compiler_params=PARAMS,
        cost_estimate=COST,
    )(info, *arrays)


def move(plan, arrays, rows, flag=None, tokens=()):
    width = arrays[0].shape[1]
    n = len(arrays)
    slots = len({target for _, _, _, target in plan})

    def kernel(flag, *refs):
        sources = refs[:n]
        out, token, buf, sem = refs[n + len(tokens) :]
        token[...] = jnp.zeros_like(token)

        def each(act):
            for when, source, row, target in plan:
                slot = target // FT
                copy = pltpu.make_async_copy(
                    sources[source].at[pl.ds(row, FT)], buf.at[slot], sem.at[0, slot]
                )
                if when is None:
                    act(copy)
                else:
                    pl.when(flag[0] == when)(lambda copy=copy: act(copy))

        each(lambda copy: copy.start())
        each(lambda copy: copy.wait())
        outward = [
            pltpu.make_async_copy(buf.at[slot], out.at[pl.ds(slot * FT, FT)], sem.at[1, slot])
            for slot in range(slots)
        ]
        for copy in outward:
            copy.start()
        for copy in outward:
            copy.wait()

    flag = jnp.zeros((1,), jnp.int32) if flag is None else jnp.reshape(flag, (1,))
    return pl.pallas_call(
        kernel,
        grid_spec=pltpu.PrefetchScalarGridSpec(
            num_scalar_prefetch=1,
            grid=(1,),
            in_specs=[ANY_SPEC] * n + [TOKEN_SPEC] * len(tokens),
            out_specs=[ANY_SPEC, TOKEN_SPEC],
            scratch_shapes=[
                pltpu.VMEM((slots, FT, width), jnp.bfloat16), pltpu.SemaphoreType.DMA((2, slots))
            ],
        ),
        out_shape=[jax.ShapeDtypeStruct((rows, width), jnp.bfloat16), TOKEN],
        compiler_params=PARAMS,
        cost_estimate=COST,
    )(flag.astype(jnp.int32), *arrays, *tokens)


def pick(flag, taken, kept, tokens=()):
    plan = [(1, 0, 0, 0), (0, 1, 0, 0)]
    return move(plan, [taken, kept], FT, flag, tokens)[0]


def last_frames(keys, values, tokens=()):
    plan = [(None, 0, FT, 0), (None, 1, FT, FT)]
    return move(plan, [keys, values], 2 * FT, None, tokens)


def sink_steps(size):
    bits = [1 << b for b in range(1, size.bit_length() - 1)]
    orders = (bits[::-1], [bits[0]] + bits[:0:-1])
    done = [0, 0]
    steps = []
    for step in range(len(bits)):
        pairs = []
        for which in (0, 1):
            bit = orders[which][step]
            holders = [i for i in range(0, size, 2) if i & ~done[which] == 0]
            pairs += [(i + which, (i | bit) + which) for i in holders]
            done[which] |= bit
        steps.append(pairs)
    return steps


def project(info, parts, weight):
    columns = weight.shape[1]
    turns = 6
    block = columns // turns
    rows, depth = parts[0][0].shape
    per_device = weight.shape[0] // 2 // depth
    n = len(parts)

    def kernel(info, *refs):
        products = [dot(a[...], w[...]) for a, w in zip(refs[:n], refs[n : 2 * n])]
        refs[-1][...] = sum(products[1:], products[0]).astype(jnp.bfloat16)

    def weight_spec(part, received):
        def index(i, info):
            owner = 1 - info[1] if received else info[1]
            return (owner * per_device + part, i)

        return pl.BlockSpec((depth, block), index)

    return pl.pallas_call(
        kernel,
        grid_spec=pltpu.PrefetchScalarGridSpec(
            num_scalar_prefetch=1,
            grid=(turns,),
            in_specs=[pl.BlockSpec((rows, depth), lambda i, info: (0, 0))] * n
            + [weight_spec(part, received) for _, part, received in parts],
            out_specs=pl.BlockSpec((rows, block), lambda i, info: (0, i)),
        ),
        out_shape=jax.ShapeDtypeStruct((rows, columns), jnp.bfloat16),
        compiler_params=PARAMS,
        cost_estimate=COST,
    )(info, *[a for a, _, _ in parts], *[weight] * n)


def local(query_states, key_states, value_states, win_start, group_end, out_weight):
    axis = "tm"
    size = lax.axis_size(axis)
    paired = lax.axis_size("head") == 2
    me = lax.axis_index(axis)
    core = me % 2
    heads = query_states.shape[1] // HD
    info = jnp.concatenate(
        [
            jnp.stack([me * 2, lax.axis_index("head")]).astype(jnp.int32),
            win_start.astype(jnp.int32),
            group_end.astype(jnp.int32),
            jnp.stack([core]).astype(jnp.int32),
        ]
    )
    groups = [(0, heads // 2), (heads // 2, heads // 2)] if heads % 2 == 0 else [(0, heads)]
    slot_all, slot_part = (SLOT, True), (SLOT, False)
    frames = [(0, True), (1, True)]
    sums = [(2 * FT, jnp.float32, SLOT)] * 2

    onward = [(i, i + 1) for i in range(size - 1)]
    near_k = lax.ppermute(key_states, axis, onward)
    near_v = lax.ppermute(value_states, axis, onward)

    def local_stage(group):
        return stage(
            local_kernel, info, group,
            [query_states, key_states, key_states, value_states, value_states],
            [slot_all] + frames * 2, [(2 * FT, jnp.bfloat16, SLOT)] + sums, token=True,
        )

    moved = lax.ppermute(value_states, axis, [(0, 1)])
    held = pick(core, moved, key_states)
    near_last, near_here = last_frames(near_k, near_v)
    relay = lax.ppermute(near_last, axis, [(i, i + 1) for i in range(0, size, 2)])
    own_last, _ = last_frames(key_states, value_states, [near_here])
    far = lax.ppermute(own_last, axis, [(i, i + 2) for i in range(0, size - 2, 2)])

    def near_stage(group, state):
        return stage(
            near_kernel, info, group, [query_states, near_k, near_k, near_v, near_v, *state],
            [slot_all] + frames * 2 + [slot_part] * 3, sums, token=True,
        )

    states = []
    steps = sink_steps(size)
    for step, pairs in enumerate(steps):
        moved = lax.ppermute(held, axis, pairs)
        tokens = []
        if step < len(groups):
            *state, token = local_stage(groups[step])
            states.append(state)
            tokens = [token]
        if step == len(steps) - 2:
            tokens.append(near_here)
        if step == len(steps) - 1:
            *sums_now, token = near_stage(groups[0], states[0])
            states[0] = [states[0][0], *sums_now]
            tokens.append(token)
        takes = jnp.zeros((), bool)
        for _, target in pairs:
            takes = takes | (me == target)
        held = pick(takes, moved, held, tokens)
    other = lax.ppermute(held, axis, [(i, i ^ 1) for i in range(size)])

    for g, group in enumerate(groups[1:], 1):
        *sums_now, _ = near_stage(group, states[g])
        states[g] = [states[g][0], *sums_now]
    mine, theirs = [], []
    for g, group in enumerate(groups):
        outs = [(FT, jnp.bfloat16, 0)] * 2 if paired else [(2 * FT, jnp.bfloat16, None)]
        results = stage(
            lambda *refs, offset=group[0]: final_kernel(offset, *refs), info, group,
            [query_states, held, other, far, far, relay, relay, *states[g],
             key_states, value_states, near_k, near_v, held, other, far, relay],
            [slot_all, frames[0], frames[0]] + frames * 2 + [slot_part] * 3 + [None] * 8, outs,
            [pltpu.VMEM((FT, HD), jnp.float32)] * 2 + [pltpu.SemaphoreType.DMA((2,))],
        )
        mine.append(results[0])
        if paired:
            theirs.append(lax.ppermute(results[1], "head", [(0, 1), (1, 0)]))
    if not paired:
        attended = jnp.concatenate(mine, axis=1)
        token_rows = lax.all_to_all(attended, "head", split_axis=0, concat_axis=1, tiled=True)
        return dot(token_rows, out_weight).astype(jnp.bfloat16)
    parts = [(array, g, False) for g, array in enumerate(mine)]
    parts += [(array, g, True) for g, array in enumerate(theirs)]
    return project(info, parts, out_weight)


def solution(mesh):
    in_specs = (P("tm", "head"), P("tm", "head"), P("tm", "head"), P("tm"), P("tm"), P())
    out_specs = P(("tm", "head"), None)
    return jax.shard_map(local, mesh=mesh, in_specs=in_specs, out_specs=out_specs, check_vma=False)
```

```python
import jax
import jax.numpy as jnp
from jax import lax
from jax.experimental import pallas as pl
from jax.experimental.pallas import tpu as pltpu
from jax.sharding import PartitionSpec as P

HD = 128
FT = 768
BQ = 256
BK = 256
LOG2E = 1.4426950408889634
SCALE = HD ** -0.5 * LOG2E
LIMIT = 1e30
HIDDEN = 1e30
PARAMS = pltpu.CompilerParams(vmem_limit_bytes=16 * 1024 * 1024)
ANY_SPEC = pl.BlockSpec(memory_space=pl.ANY)
COST = pl.CostEstimate(flops=1000, bytes_accessed=1000, transcendentals=0)
TOKEN = jax.ShapeDtypeStruct((8, 128), jnp.float32)


def dot(a, b):
    return jnp.dot(a, b, preferred_element_type=jnp.float32)


def span(start, size):
    return pl.ds(pl.multiple_of(start, size), size)


def blocks(*frames):
    return [(frame, j) for frame in frames for j in range(FT // BK)]


def scores(q, kt, unit):
    frame, j = unit
    return dot(q, kt[frame, :, j * BK : (j + 1) * BK])


def accumulate(units, kt, values):
    def fetch(unit):
        lane, *unit = unit
        known = lane.pop("known", None)
        return scores(lane["q"], kt, unit) if known is None else known

    ahead = fetch(units[0])
    for n, (lane, frame, j) in enumerate(units):
        s = ahead
        if n + 1 < len(units):
            ahead = fetch(units[n + 1])
        shift = lane["shift"][frame]
        parts = [jnp.exp2(s[:, c : c + 128] * SCALE - shift) for c in range(0, BK, 128)]
        weights = jnp.concatenate([part.astype(jnp.bfloat16) for part in parts], axis=1)
        added = dot(weights, values[frame, j * BK : (j + 1) * BK, :])
        if lane["acc"] is None:
            lane["acc"], lane["l"] = added, sum(parts[1:], parts[0])
        else:
            lane["acc"], lane["l"] = lane["acc"] + added, sum(parts, lane["l"])


def interleaved(lanes, *frames):
    return [(lane, *unit) for unit in blocks(*frames) for lane in lanes]


def visible(info, slot, frame):
    return (frame >= 1) & (frame >= info[2 + slot]) & (frame <= info[4 + slot])


def shifts(m, seen):
    m = m.astype(jnp.float32)
    return [jnp.where(shown, m, HIDDEN) for shown in seen]


def load_frames(kt, values, keys, vals, columns):
    for frame, ((k, k_row), (v, v_row)) in enumerate(zip(keys, vals)):
        kt[frame] = k[pl.ds(k_row, FT), columns].T
        values[frame] = v[pl.ds(v_row, FT), columns]


def over_blocks(heads, offset, load, run):
    def head_turn(h, carry):
        wide = span((h + offset) * HD, HD)
        load(wide)

        def turn(i, carry):
            run(h, wide, [span(slot * FT + i * BQ, BQ) for slot in (0, 1)])
            return carry

        lax.fori_loop(0, FT // BQ, turn, 0)
        return carry

    lax.fori_loop(0, heads, head_turn, 0)


def local_kernel(offset, heads, info, q, k, v, m, acc, l, token, kt, values):
    first = info[0]
    token[...] = jnp.zeros_like(token)

    def run(h, wide, rows):
        column = span(h * HD, HD)
        lanes = []
        for slot in (0, 1):
            lane = dict(q=q[rows[slot], wide], acc=None, l=None)
            known = scores(lane["q"], kt, (slot, 0))
            peak = jnp.max(known, axis=1, keepdims=True) * SCALE
            shift = jnp.broadcast_to(peak, (BQ, HD)).astype(m.dtype)
            m[rows[slot], column] = shift
            seen = [visible(info, slot, first + frame) for frame in (0, 1)]
            lane.update(known=known, shift=shifts(shift, seen))
            lanes.append(lane)
        units = [
            (lane, slot ^ turn, j)
            for turn in (0, 1)
            for j in range(FT // BK)
            for slot, lane in enumerate(lanes)
        ]
        accumulate(units, kt, values)
        for slot, lane in enumerate(lanes):
            acc[rows[slot], column] = lane["acc"]
            l[rows[slot], column] = lane["l"]

    def load(wide):
        load_frames(kt, values, [(k, 0), (k, FT)], [(v, 0), (v, FT)], wide)

    over_blocks(heads, offset, load, run)


def near_kernel(offset, heads, info, q, k, v, m, acc_in, l_in, acc, l, token, kt, values):
    first = info[0]
    token[...] = jnp.zeros_like(token)

    def run(h, wide, rows):
        column = span(h * HD, HD)
        lanes = []
        for slot in (0, 1):
            seen = [visible(info, slot, first - 2 + frame) for frame in (0, 1)]
            r = rows[slot]
            lanes.append(
                dict(
                    q=q[r, wide], acc=acc_in[r, column], l=l_in[r, column],
                    shift=shifts(m[r, column], seen),
                )
            )
        accumulate(interleaved(lanes, 1, 0), kt, values)
        for slot, lane in enumerate(lanes):
            acc[rows[slot], column] = lane["acc"]
            l[rows[slot], column] = lane["l"]

    def load(wide):
        load_frames(kt, values, [(k, 0), (k, FT)], [(v, 0), (v, FT)], wide)

    over_blocks(heads, offset, load, run)


def final_kernel(
    offset, heads, info, q, sink_a, sink_b, far, relay_k, relay_v, m, acc_in, l_in,
    key_any, value_any, near_k, near_v, *refs,
):
    outs = refs[:-7]
    kt, values, acc, l, shift, largest, sem = refs[-7:]
    first = info[0]
    core = info[6]
    far_seen = visible(info, 0, first - 3)

    def load(wide):
        largest[0] = 0.0
        largest[1] = 0.0

        @pl.when(core == 0)
        def _():
            load_frames(kt, values, [(sink_a, 0), (far, 0)], [(sink_b, 0), (far, FT)], wide)

        @pl.when(core == 1)
        def _():
            load_frames(
                kt, values, [(sink_b, 0), (relay_k, FT)], [(sink_a, 0), (relay_v, FT)], wide
            )

    def write(slot, first_row, column, acc, l):
        total = jnp.sum(l, axis=1, keepdims=True)
        attended = (acc / total).astype(jnp.bfloat16)
        rows = span(first_row, BQ)
        if len(outs) == 1:
            outs[0][span(slot * FT + first_row, BQ), column] = attended
        else:

            @pl.when(info[1] == slot)
            def _():
                outs[0][rows, column] = attended

            @pl.when(info[1] != slot)
            def _():
                outs[1][rows, column] = attended

        return jnp.max(total)

    def run(h, wide, i):
        column = span(h * HD, HD)
        lanes = []
        for slot in (0, 1):
            r = span(slot * FT + i * BQ, BQ)
            lanes.append(
                dict(
                    q=q[r, wide], acc=acc_in[r, column], l=l_in[r, column],
                    shift=shifts(m[r, column], [True, far_seen & (slot == 0)]),
                )
            )
        accumulate(interleaved(lanes, 0) + interleaved(lanes[:1], 1), kt, values)
        for slot, lane in enumerate(lanes):
            most = write(slot, i * BQ, column, lane["acc"], lane["l"])
            largest[slot] = jnp.where(most < largest[slot], largest[slot], most)

    def again(slot, h, wide):
        column = span(h * HD, HD)
        here, there = core == 0, core == 1
        sources = [
            (here, sink_a, 0, sink_b, 0),
            (there, sink_b, 0, sink_a, 0),
        ]
        if slot == 0:
            sources += [
                (far_seen & here, far, 0, far, FT), (far_seen & there, relay_k, FT, relay_v, FT)
            ]
        for frame in (0, 1):
            row = frame * FT
            own = visible(info, slot, first + frame)
            sources.append((own, key_any, row, value_any, row))
            behind = visible(info, slot, first - 2 + frame)
            sources.append((behind, near_k, row, near_v, row))

        def sweep(step):
            def turn(t, carry):
                seen = False
                for n, (shown, k, k_row, v, v_row) in enumerate(sources):
                    chosen = (t == n) & shown
                    seen = seen | chosen

                    @pl.when(chosen)
                    def _():
                        for n, (ref, row) in enumerate(((k, k_row), (v, v_row))):
                            copy = pltpu.make_async_copy(
                                ref.at[pl.ds(row, FT), wide], values.at[n], sem.at[n]
                            )
                            copy.start()
                            copy.wait()

                @pl.when(seen)
                def _():
                    kt[0] = values[0].T
                    values[0] = values[1]

                    def block(i, carry):
                        step(span(i * BQ, BQ), span(slot * FT + i * BQ, BQ))
                        return carry

                    lax.fori_loop(0, FT // BQ, block, 0)

                return carry

            lax.fori_loop(0, len(sources), turn, 0)

        def peak(rows, q_rows):
            for unit in blocks(0):
                most = jnp.max(scores(q[q_rows, wide], kt, unit), axis=1, keepdims=True) * SCALE
                shift[rows, :] = jnp.maximum(shift[rows, :], most)

        def add(rows, q_rows):
            lane = dict(q=q[q_rows, wide], acc=acc[rows, :], l=l[rows, :], shift=[shift[rows, :]])
            accumulate(interleaved([lane], 0), kt, values)
            acc[rows, :] = lane["acc"]
            l[rows, :] = lane["l"]

        shift[...] = jnp.full((FT, HD), -jnp.inf, jnp.float32)
        acc[...] = jnp.zeros((FT, HD), jnp.float32)
        l[...] = jnp.zeros((FT, HD), jnp.float32)
        sweep(peak)
        sweep(add)
        for i in range(FT // BQ):
            rows = slice(i * BQ, (i + 1) * BQ)
            write(slot, i * BQ, column, acc[rows, :], l[rows, :])

    def head_turn(h, carry):
        wide = span((h + offset) * HD, HD)
        load(wide)

        def turn(i, carry):
            run(h, wide, i)
            return carry

        lax.fori_loop(0, FT // BQ, turn, 0)
        for slot in (0, 1):
            pl.when(jnp.logical_not(largest[slot] < LIMIT))(lambda slot=slot: again(slot, h, wide))
        return carry

    lax.fori_loop(0, heads, head_turn, 0)


VMEM_SPEC = pl.BlockSpec(memory_space=pltpu.VMEM)
SMEM_SPEC = pl.BlockSpec(memory_space=pltpu.SMEM)


def stage(kernel, info, group, arrays, outs, scratch=(), in_any=0, aliases=None):
    offset, heads = group

    def run(*refs):
        kernel(offset, heads, *refs)

    return pl.pallas_call(
        run,
        in_specs=[SMEM_SPEC] + [VMEM_SPEC] * (len(arrays) - in_any) + [ANY_SPEC] * in_any,
        out_specs=[VMEM_SPEC] * len(outs),
        scratch_shapes=[
            pltpu.VMEM((2, HD, FT), jnp.bfloat16), pltpu.VMEM((2, FT, HD), jnp.bfloat16)
        ] + list(scratch),
        out_shape=outs,
        input_output_aliases=aliases or {},
        compiler_params=PARAMS,
        cost_estimate=COST,
    )(info, *arrays)


def last_frames(keys, values):
    return jnp.concatenate([keys[FT:], values[FT:]], axis=0)


def sink_steps(size):
    bits = [1 << b for b in range(1, size.bit_length() - 1)]
    orders = (bits[::-1], bits[::-1])
    done = [0, 0]
    steps = []
    for step in range(len(bits)):
        pairs = []
        for which in (0, 1):
            bit = orders[which][step]
            holders = [i for i in range(0, size, 2) if i & ~done[which] == 0]
            pairs += [(i + which, (i | bit) + which) for i in holders]
            done[which] |= bit
        steps.append(pairs)
    return steps


def project(info, parts, weight):
    columns = weight.shape[1]
    turns = 6
    block = columns // turns
    rows, depth = parts[0][0].shape
    n = len(parts)

    def kernel(info, *refs):
        weight, out = refs[n:]
        column = span(pl.program_id(0) * block, block)
        total = None
        for a, (_, place, received) in zip(refs[:n], parts):
            owner = 1 - info[1] if received else info[1]
            first = owner * (weight.shape[0] // 2) + place * depth
            product = dot(a[...], weight[span(first, depth), column])
            total = product if total is None else total + product
        out[...] = total.astype(jnp.bfloat16)

    return pl.pallas_call(
        kernel,
        grid=(turns,),
        in_specs=[SMEM_SPEC] + [VMEM_SPEC] * (n + 1),
        out_specs=pl.BlockSpec((rows, block), lambda i: (0, i)),
        out_shape=jax.ShapeDtypeStruct((rows, columns), jnp.bfloat16),
        compiler_params=PARAMS,
        cost_estimate=COST,
    )(info, *[a for a, _, _ in parts], weight)


def local(query_states, key_states, value_states, win_start, group_end, out_weight):
    axis = "tm"
    size = lax.axis_size(axis)
    paired = lax.axis_size("head") == 2
    me = lax.axis_index(axis)
    core = me % 2
    heads = query_states.shape[1] // HD
    info = jnp.concatenate(
        [
            jnp.stack([me * 2, lax.axis_index("head")]).astype(jnp.int32),
            win_start.astype(jnp.int32),
            group_end.astype(jnp.int32),
            jnp.stack([core]).astype(jnp.int32),
        ]
    )
    groups = [(0, heads // 2), (heads // 2, heads // 2)] if heads % 2 == 0 else [(0, heads)]
    rows = 2 * FT
    width = groups[0][1] * HD
    sums = [jax.ShapeDtypeStruct((rows, width), jnp.float32)] * 2

    onward = [(i, i + 1) for i in range(size - 1)]
    near_k = lax.ppermute(key_states, axis, onward)
    near_v = lax.ppermute(value_states, axis, onward)
    moved = lax.ppermute(value_states, axis, [(0, 1)])
    held = jnp.where(core == 0, key_states[:FT], moved[:FT])
    on_chip = [(i, i + 1) for i in range(0, size, 2)]
    relay_k = lax.ppermute(near_k, axis, on_chip)
    relay_v = lax.ppermute(near_v, axis, on_chip)
    own_last = last_frames(key_states, value_states)
    far = lax.ppermute(own_last, axis, [(i, i + 2) for i in range(0, size - 2, 2)])

    def local_stage(group):
        return stage(
            local_kernel, info, group, [query_states, key_states, value_states],
            [jax.ShapeDtypeStruct((rows, width), jnp.bfloat16)] + sums + [TOKEN],
        )

    states = []
    for step, pairs in enumerate(sink_steps(size)):
        moved = lax.ppermute(held, axis, pairs)
        takes = jnp.zeros((), bool)
        for _, target in pairs:
            takes = takes | (me == target)
        if step < len(groups):
            *state, token = local_stage(groups[step])
            states.append(state)
            takes = takes & (token[0, 0] == 0)
        held = jnp.where(takes, moved, held)
    other = lax.ppermute(held, axis, [(i, i ^ 1) for i in range(size)])

    for g, group in enumerate(groups):
        m, acc, l = states[g]
        acc, l, _ = stage(
            near_kernel, info, group, [query_states, near_k, near_v, m, acc, l], sums + [TOKEN],
            aliases={5: 0, 6: 1},
        )
        states[g] = m, acc, l
    mine, theirs = [], []
    for g, group in enumerate(groups):
        part = jax.ShapeDtypeStruct((FT if paired else rows, width), jnp.bfloat16)
        results = stage(
            final_kernel, info, group,
            [query_states, held, other, far, relay_k, relay_v, *states[g],
             key_states, value_states, near_k, near_v],
            [part] * (2 if paired else 1),
            [pltpu.VMEM((FT, HD), jnp.float32)] * 3
            + [pltpu.SMEM((2,), jnp.float32), pltpu.SemaphoreType.DMA((2,))],
            in_any=4,
        )
        mine.append(results[0])
        if paired:
            theirs.append(lax.ppermute(results[1], "head", [(0, 1), (1, 0)]))
    if not paired:
        attended = jnp.concatenate(mine, axis=1)
        token_rows = lax.all_to_all(attended, "head", split_axis=0, concat_axis=1, tiled=True)
        return dot(token_rows, out_weight).astype(jnp.bfloat16)
    parts = [(array, g, False) for g, array in enumerate(mine)]
    parts += [(array, g, True) for g, array in enumerate(theirs)]
    return project(info, parts, out_weight)


def solution(mesh):
    in_specs = (P("tm", "head"), P("tm", "head"), P("tm", "head"), P("tm"), P("tm"), P())
    out_specs = P(("tm", "head"), None)
    return jax.shard_map(local, mesh=mesh, in_specs=in_specs, out_specs=out_specs, check_vma=False)
```

```python
import functools

import jax
import jax.numpy as jnp
from jax import lax
from jax.experimental import pallas as pl
from jax.experimental.pallas import tpu as pltpu
from jax.sharding import PartitionSpec as P

HD = 128
FT = 768
BK = 256
LOG2E = 1.4426950408889634
SCALE = HD ** -0.5 * LOG2E
LIMIT = 1e30
HIDDEN = 1e30
PARAMS = pltpu.CompilerParams(vmem_limit_bytes=24 * 1024 * 1024)
ANY_SPEC = pl.BlockSpec(memory_space=pl.ANY)
COST = pl.CostEstimate(flops=1000, bytes_accessed=1000, transcendentals=0)
TOKEN = jax.ShapeDtypeStruct((8, 128), jnp.float32)


def dot(a, b):
    return jnp.dot(a, b, preferred_element_type=jnp.float32)


def span(start, size):
    return pl.ds(pl.multiple_of(start, size), size)


def rows_of(slot):
    return slice(slot * FT, (slot + 1) * FT)


def extended_scores(q, kt, j):
    return dot(q, kt[:, j * BK : (j + 1) * BK])


def add_frame(lanes, kt, values):
    units = [(n, j) for n in range(len(lanes)) for j in range(FT // BK)]

    def fetch(unit):
        n, j = unit
        return extended_scores(lanes[n][0], kt, j)

    ahead = fetch(units[0])
    weights = []
    for at, (n, j) in enumerate(units):
        s = ahead
        if at + 1 < len(units):
            ahead = fetch(units[at + 1])
        _, shift, add = lanes[n]
        for c in range(0, BK, HD):
            weights.append(jnp.exp2(s[:, c : c + HD] * SCALE - shift).astype(jnp.bfloat16))
        if j == FT // BK - 1:
            add(dot(jnp.concatenate(weights, axis=1), values[...]))
            weights = []


def visible(info, slot, frame):
    return (frame >= 1) & (frame >= info[2 + slot]) & (frame <= info[4 + slot])


def lanes_of(h, heads):
    share = HD // heads
    lane = lax.broadcasted_iota(jnp.int32, (1, HD), 1)
    return (lane >= h * share) & (lane < (h + 1) * share)


def spread(packed, h, heads):
    row = lax.broadcasted_iota(jnp.int32, (HD, HD), 0)
    chosen = jnp.where(row == h * (HD // heads), 1.0, 0.0).astype(jnp.bfloat16)
    return dot(packed, chosen)


def spread_sum(packed, h, heads):
    high = packed.astype(jnp.bfloat16)
    low = (packed - high.astype(jnp.float32)).astype(jnp.bfloat16)
    return spread(high, h, heads) + spread(low, h, heads)


def sums_into(acc_from, acc, sums, rows, column, h, heads):
    def add(added):
        new = added[:, :HD]
        acc[rows, column] = new if acc_from is None else acc_from[rows, column] + new
        old = sums[rows, :]
        sums[rows, :] = jnp.where(lanes_of(h, heads), old + added[:, HD:], old)

    return add


def load_frame(kt, values, k, v, column):
    kt[...] = k[:, column].T
    values[:, :HD] = v[:, column]


def each_head(group, turn):
    offset, count = group

    def body(h, carry):
        turn(h, span(h * HD, HD), span((h + offset) * HD, HD))
        return carry

    lax.fori_loop(0, count, body, 0)


def own_kernel(group, info, q, k, v, *refs):
    m, acc, sums, token, kt, values = refs[-6:]
    if len(refs) > 6:
        refs[0][...] = v[...]
    heads = group[1]
    first = info[0]
    token[...] = jnp.zeros_like(token)
    values[:, HD:] = jnp.ones((FT, HD), jnp.bfloat16)
    ones = jnp.ones((HD, HD), jnp.bfloat16)
    m[...] = jnp.zeros_like(m)
    sums[...] = jnp.zeros_like(sums)

    def turn(h, column, wide):
        here = lanes_of(h, heads)
        for slot in (0, 1):
            rows = rows_of(slot)
            product = q[rows, wide].astype(jnp.float32) * k[rows, wide].astype(jnp.float32)
            own = (dot(product.astype(jnp.bfloat16), ones) * SCALE).astype(jnp.bfloat16)
            m[rows, :] = jnp.where(here, own, m[rows, :])
        for frame in (0, 1):
            load_frame(kt, values, k.at[rows_of(frame)], v.at[rows_of(frame)], wide)
            lanes = []
            for slot in (0, 1):
                rows = rows_of(slot)
                shift = spread(m[rows, :], h, heads)
                shift = jnp.where(visible(info, slot, first + frame), shift, HIDDEN)
                acc_from = acc if frame else None
                add = sums_into(acc_from, acc, sums, rows, column, h, heads)
                lanes.append((q[rows, wide], shift, add))
            add_frame(lanes, kt, values)

    each_head(group, turn)


def near_kernel(group, info, q, m, acc_in, sums_in, near_k, near_v, *refs):
    acc, sums, kt, values, k_buf, v_buf, sem = refs
    offset, heads = group
    first = info[0]
    order = (1, 0)
    copies = {
        frame: [
            pltpu.make_async_copy(
                source.at[pl.ds(frame * FT, FT), pl.ds(offset * HD, heads * HD)],
                buf.at[frame],
                sem.at[frame, n],
            )
            for n, (source, buf) in enumerate(((near_k, k_buf), (near_v, v_buf)))
        ]
        for frame in order
    }
    for frame in order:
        for copy in copies[frame]:
            copy.start()
    values[:, HD:] = jnp.ones((FT, HD), jnp.bfloat16)
    sums[...] = sums_in[...]
    for frame in order:
        for copy in copies[frame]:
            copy.wait()

        def turn(h, column, wide):
            load_frame(kt, values, k_buf.at[frame], v_buf.at[frame], column)
            acc_from = acc_in if frame == order[0] else acc
            lanes = []
            for slot in (0, 1):
                rows = rows_of(slot)
                shift = spread(m[rows, :], h, heads)
                shift = jnp.where(visible(info, slot, first - 2 + frame), shift, HIDDEN)
                add = sums_into(acc_from, acc, sums, rows, column, h, heads)
                lanes.append((q[rows, wide], shift, add))
            add_frame(lanes, kt, values)

        each_head(group, turn)


def final_kernel(
    group, info, q, m, acc_in, sums_in,
    sink_a, sink_b, far, relay_k, relay_v, key_any, value_any, near_k, near_v, *refs,
):
    outs = refs[:-8]
    kt, values, k_buf, v_buf, acc, shift, largest, sem = refs[-8:]
    first = info[0]
    core = info[6]
    far_seen = visible(info, 0, first - 3)
    offset, heads = group
    group_columns = pl.ds(offset * HD, heads * HD)
    values[:, HD:] = jnp.ones((FT, HD), jnp.bfloat16)

    def copies(frame, k, k_row, v, v_row, columns):
        return [
            pltpu.make_async_copy(
                source.at[pl.ds(row, FT), columns], buf.at[frame], sem.at[frame, n]
            )
            for n, (source, row, buf) in enumerate(((k, k_row, k_buf), (v, v_row, v_buf)))
        ]

    arriving = {
        0: [
            (0, sink_a, 0, sink_b, 0, group_columns),
            (1, far, 0, far, FT, group_columns),
        ],
        1: [
            (0, sink_b, 0, sink_a, 0, group_columns),
            (1, relay_k, FT, relay_v, FT, group_columns),
        ],
    }
    for which, listed in arriving.items():

        @pl.when(core == which)
        def _():
            started = [copies(*entry) for entry in listed]
            for act in (lambda copy: copy.start(), lambda copy: copy.wait()):
                for pair in started:
                    for copy in pair:
                        act(copy)

    def write(slot, h, acc, total):
        attended = (acc / total).astype(jnp.bfloat16)
        column = span(h * HD, HD)
        if len(outs) == 1:
            outs[0][rows_of(slot), column] = attended
        else:

            @pl.when(info[1] == slot)
            def _():
                outs[0][:, column] = attended

            @pl.when(info[1] != slot)
            def _():
                outs[1][:, column] = attended

    def turn(h, column, wide):
        results = {}

        def keep(slot):
            def add(added):
                results[slot] = results[slot] + added if slot in results else added

            return add

        shifts = [spread(m[rows_of(slot), :], h, heads) for slot in (0, 1)]
        load_frame(kt, values, k_buf.at[0], v_buf.at[0], column)
        add_frame(
            [(q[rows_of(slot), wide], shifts[slot], keep(slot)) for slot in (1, 0)], kt, values
        )
        load_frame(kt, values, k_buf.at[1], v_buf.at[1], column)
        shown = jnp.where(far_seen, shifts[0], HIDDEN)
        add_frame([(q[rows_of(0), wide], shown, keep(0))], kt, values)
        for slot in (0, 1):
            rows = rows_of(slot)
            total = spread_sum(sums_in[rows, :], h, heads) + results[slot][:, HD:]
            write(slot, h, acc_in[rows, column] + results[slot][:, :HD], total)
            largest[h, slot] = jnp.max(total)

    each_head(group, turn)

    def again(slot, h, wide):
        here, there = core == 0, core == 1
        sources = [(here, sink_a, 0, sink_b, 0), (there, sink_b, 0, sink_a, 0)]
        if slot == 0:
            sources += [
                (far_seen & here, far, 0, far, FT), (far_seen & there, relay_k, FT, relay_v, FT)
            ]
        for frame in (0, 1):
            row = frame * FT
            own = visible(info, slot, first + frame)
            sources.append((own, key_any, row, value_any, row))
            behind = visible(info, slot, first - 2 + frame)
            sources.append((behind, near_k, row, near_v, row))
        one = (k_buf.at[0, :, :HD], v_buf.at[0, :, :HD])

        def sweep(step):
            def visit(t, carry):
                seen = False
                for n, (shown, k, k_row, v, v_row) in enumerate(sources):
                    chosen = (t == n) & shown
                    seen = seen | chosen

                    @pl.when(chosen)
                    def _():
                        for n, (ref, row) in enumerate(((k, k_row), (v, v_row))):
                            copy = pltpu.make_async_copy(
                                ref.at[pl.ds(row, FT), wide], one[n], sem.at[0, n]
                            )
                            copy.start()
                            copy.wait()

                @pl.when(seen)
                def _():
                    load_frame(kt, values, k_buf.at[0], v_buf.at[0], slice(0, HD))
                    step()

                return carry

            lax.fori_loop(0, len(sources), visit, 0)

        queries = q[rows_of(slot), wide]

        def peak():
            for j in range(FT // BK):
                most = jnp.max(extended_scores(queries, kt, j), axis=1, keepdims=True) * SCALE
                shift[...] = jnp.maximum(shift[...], most)

        def more(added):
            acc[...] = acc[...] + added

        shift[...] = jnp.full((FT, HD), -jnp.inf, jnp.float32)
        acc[...] = jnp.zeros((FT, 2 * HD), jnp.float32)
        sweep(peak)
        sweep(lambda: add_frame([(queries, shift[...], more)], kt, values))
        write(slot, h, acc[:, :HD], acc[:, HD:])

    def check(h, column, wide):
        for slot in (0, 1):
            in_range = largest[h, slot] < LIMIT
            pl.when(jnp.logical_not(in_range))(lambda slot=slot: again(slot, h, wide))

    each_head(group, check)


VMEM_SPEC = pl.BlockSpec(memory_space=pltpu.VMEM)
SMEM_SPEC = pl.BlockSpec(memory_space=pltpu.SMEM)


def stage(kernel, arrays, in_any, outs, scratch):
    return pl.pallas_call(
        kernel,
        in_specs=[SMEM_SPEC] + [VMEM_SPEC] * (len(arrays) - in_any - 1) + [ANY_SPEC] * in_any,
        out_specs=[VMEM_SPEC] * len(outs),
        scratch_shapes=[
            pltpu.VMEM((HD, FT), jnp.bfloat16), pltpu.VMEM((FT, 2 * HD), jnp.bfloat16)
        ] + list(scratch),
        out_shape=outs,
        compiler_params=PARAMS,
        cost_estimate=COST,
    )(*arrays)


def last_frames(keys, values):
    return jnp.concatenate([keys[FT:], values[FT:]], axis=0)


def sink_steps(size):
    bits = [1 << b for b in range(1, size.bit_length() - 1)]
    orders = (bits[::-1], [bits[0]] + bits[:0:-1])
    done = [0, 0]
    steps = []
    for step in range(len(bits)):
        pairs = []
        for which in (0, 1):
            bit = orders[which][step]
            holders = [i for i in range(0, size, 2) if i & ~done[which] == 0]
            pairs += [(i + which, (i | bit) + which) for i in holders]
            done[which] |= bit
        steps.append(pairs)
    return steps


def project(info, parts, weight):
    columns = weight.shape[1]
    turns = 6
    block = columns // turns
    rows, depth = parts[0][0].shape
    n = len(parts)

    def kernel(info, *refs):
        weight, out = refs[n:]
        column = span(pl.program_id(0) * block, block)
        total = None
        for a, (_, place, received) in zip(refs[:n], parts):
            owner = 1 - info[1] if received else info[1]
            first = owner * (weight.shape[0] // 2) + place * depth
            product = dot(a[...], weight[span(first, depth), column])
            total = product if total is None else total + product
        out[...] = total.astype(jnp.bfloat16)

    return pl.pallas_call(
        kernel,
        grid=(turns,),
        in_specs=[SMEM_SPEC] + [VMEM_SPEC] * (n + 1),
        out_specs=pl.BlockSpec((rows, block), lambda i: (0, i)),
        out_shape=jax.ShapeDtypeStruct((rows, columns), jnp.bfloat16),
        compiler_params=PARAMS,
        cost_estimate=COST,
    )(info, *[a for a, _, _ in parts], weight)


def local(query_states, key_states, value_states, win_start, group_end, out_weight):
    axis = "tm"
    size = lax.axis_size(axis)
    paired = lax.axis_size("head") == 2
    me = lax.axis_index(axis)
    core = me % 2
    heads = query_states.shape[1] // HD
    info = jnp.concatenate(
        [
            jnp.stack([me * 2, lax.axis_index("head")]).astype(jnp.int32),
            win_start.astype(jnp.int32),
            group_end.astype(jnp.int32),
            jnp.stack([core]).astype(jnp.int32),
        ]
    )
    groups = [(0, heads // 2), (heads // 2, heads // 2)] if heads % 2 == 0 else [(0, heads)]
    rows, width = query_states.shape
    q_like = jax.ShapeDtypeStruct((rows, width), jnp.bfloat16)
    group_width = groups[0][1] * HD
    m_like = jax.ShapeDtypeStruct((rows, HD), jnp.bfloat16)
    acc_like = jax.ShapeDtypeStruct((rows, group_width), jnp.float32)
    sums_like = jax.ShapeDtypeStruct((rows, HD), jnp.float32)
    frame_buffers = [pltpu.VMEM((2, FT, group_width), jnp.bfloat16)] * 2
    dma_sems = pltpu.SemaphoreType.DMA((2, 2))

    onward = [(i, i + 1) for i in range(size - 1)]
    near_k = lax.ppermute(key_states, axis, onward)
    moved = lax.ppermute(value_states, axis, [(0, 1)])
    held = jnp.where(core == 0, key_states[:FT], moved[:FT])
    own_last = last_frames(key_states, value_states)
    far = lax.ppermute(own_last, axis, [(i, i + 2) for i in range(0, size - 2, 2)])

    states = []
    for step, pairs in enumerate(sink_steps(size)):
        moved = lax.ppermute(held, axis, pairs)
        takes = jnp.zeros((), bool)
        for _, target in pairs:
            takes = takes | (me == target)
        if step < len(groups):
            *passed, m, acc, sums, token = stage(
                functools.partial(own_kernel, groups[step]),
                [info, query_states, key_states, value_states], 0,
                [q_like] * (step == 0) + [m_like, acc_like, sums_like, TOKEN], [],
            )
            states.append((m, acc, sums))
            takes = takes & (token[0, 0] == 0)
            if step == 0:
                near_v = lax.ppermute(passed[0], axis, onward)
        held = jnp.where(takes, moved, held)
    other = lax.ppermute(held, axis, [(i, i ^ 1) for i in range(size)])
    on_chip = [(i, i + 1) for i in range(0, size, 2)]
    relay_k = lax.ppermute(near_k, axis, on_chip)
    relay_v = lax.ppermute(near_v, axis, on_chip)

    for g, group in enumerate(groups):
        m, acc, sums = states[g]
        acc, sums = stage(
            functools.partial(near_kernel, group),
            [info, query_states, m, acc, sums, near_k, near_v], 2, [acc_like, sums_like],
            frame_buffers + [dma_sems],
        )
        states[g] = m, acc, sums
    mine, theirs = [], []
    for g, group in enumerate(groups):
        part = jax.ShapeDtypeStruct((FT if paired else rows, group_width), jnp.bfloat16)
        results = stage(
            functools.partial(final_kernel, group),
            [info, query_states, *states[g], held, other, far, relay_k, relay_v,
             key_states, value_states, near_k, near_v], 9,
            [part] * (2 if paired else 1),
            frame_buffers + [
                pltpu.VMEM((FT, 2 * HD), jnp.float32),
                pltpu.VMEM((FT, HD), jnp.float32),
                pltpu.SMEM((group[1], 2), jnp.float32),
                dma_sems,
            ],
        )
        mine.append(results[0])
        if paired:
            theirs.append(lax.ppermute(results[1], "head", [(0, 1), (1, 0)]))
    if not paired:
        attended = jnp.concatenate(mine, axis=1)
        token_rows = lax.all_to_all(attended, "head", split_axis=0, concat_axis=1, tiled=True)
        return dot(token_rows, out_weight).astype(jnp.bfloat16)
    parts = [(array, g, False) for g, array in enumerate(mine)]
    parts += [(array, g, True) for g, array in enumerate(theirs)]
    return project(info, parts, out_weight)


def solution(mesh):
    in_specs = (P("tm", "head"), P("tm", "head"), P("tm", "head"), P("tm"), P("tm"), P())
    out_specs = P(("tm", "head"), None)
    return jax.shard_map(local, mesh=mesh, in_specs=in_specs, out_specs=out_specs, check_vma=False)
```

```python
import functools

import jax
import jax.numpy as jnp
from jax import lax
from jax.experimental import pallas as pl
from jax.experimental.pallas import tpu as pltpu
from jax.sharding import PartitionSpec as P

HD = 128
FT = 768
BK = 256
LOG2E = 1.4426950408889634
SCALE = HD ** -0.5 * LOG2E
LIMIT = 1e30
HIDDEN = 1e30
PARAMS = pltpu.CompilerParams(vmem_limit_bytes=12 * 1024 * 1024)
ANY_SPEC = pl.BlockSpec(memory_space=pl.ANY)
COST = pl.CostEstimate(flops=1000, bytes_accessed=1000, transcendentals=0)
TOKEN = jax.ShapeDtypeStruct((8, 128), jnp.float32)


def dot(a, b):
    return jnp.dot(a, b, preferred_element_type=jnp.float32)


def span(start, size):
    return pl.ds(pl.multiple_of(start, size), size)


def rows_of(slot):
    return slice(slot * FT, (slot + 1) * FT)


def extended_scores(q, kt, j):
    return dot(q, kt[:, j * BK : (j + 1) * BK])


def add_frame(lanes, kt, values):
    units = [(n, j) for n in range(len(lanes)) for j in range(FT // BK)]

    def fetch(unit):
        n, j = unit
        return extended_scores(lanes[n][0], kt, j)

    ahead = fetch(units[0])
    weights = []
    for at, (n, j) in enumerate(units):
        s = ahead
        if at + 1 < len(units):
            ahead = fetch(units[at + 1])
        _, shift, add = lanes[n]
        for c in range(0, BK, HD):
            weights.append(jnp.exp2(s[:, c : c + HD] * SCALE - shift).astype(jnp.bfloat16))
        if j == FT // BK - 1:
            add(dot(jnp.concatenate(weights, axis=1), values[...]))
            weights = []


def visible(info, slot, frame):
    return (frame >= 1) & (frame >= info[2 + slot]) & (frame <= info[4 + slot])


def lanes_of(h, heads):
    share = HD // heads
    lane = lax.broadcasted_iota(jnp.int32, (1, HD), 1)
    return (lane >= h * share) & (lane < (h + 1) * share)


def spread(packed, h, heads):
    row = lax.broadcasted_iota(jnp.int32, (HD, HD), 0)
    chosen = jnp.where(row == h * (HD // heads), 1.0, 0.0).astype(jnp.bfloat16)
    return dot(packed, chosen)


def spread_sum(packed, h, heads):
    high = packed.astype(jnp.bfloat16)
    low = (packed - high.astype(jnp.float32)).astype(jnp.bfloat16)
    return spread(high, h, heads) + spread(low, h, heads)


def sums_into(acc_from, acc, sums, rows, column, h, heads):
    def add(added):
        new = added[:, :HD]
        acc[rows, column] = new if acc_from is None else acc_from[rows, column] + new
        old = sums[rows, :]
        sums[rows, :] = jnp.where(lanes_of(h, heads), old + added[:, HD:], old)

    return add


def load_frame(kt, values, k, v, column):
    kt[...] = k[:, column].T
    values[:, :HD] = v[:, column]


def each_head(group, turn):
    offset, count = group

    def body(h, carry):
        turn(h, span(h * HD, HD), span((h + offset) * HD, HD))
        return carry

    lax.fori_loop(0, count, body, 0)


def own_kernel(group, info, q, k, v, *refs):
    m, acc, sums, token, kt, values = refs[-6:]
    if len(refs) > 6:
        refs[0][...] = v[...]
    heads = group[1]
    first = info[0]
    token[...] = jnp.zeros_like(token)
    values[:, HD:] = jnp.ones((FT, HD), jnp.bfloat16)
    ones = jnp.ones((HD, HD), jnp.bfloat16)
    m[...] = jnp.zeros_like(m)
    sums[...] = jnp.zeros_like(sums)

    def turn(h, column, wide):
        here = lanes_of(h, heads)
        for slot in (0, 1):
            rows = rows_of(slot)
            product = q[rows, wide].astype(jnp.float32) * k[rows, wide].astype(jnp.float32)
            own = (dot(product.astype(jnp.bfloat16), ones) * SCALE).astype(jnp.bfloat16)
            m[rows, :] = jnp.where(here, own, m[rows, :])
        for frame in (0, 1):
            load_frame(kt, values, k.at[rows_of(frame)], v.at[rows_of(frame)], wide)
            lanes = []
            for slot in (0, 1):
                rows = rows_of(slot)
                shift = spread(m[rows, :], h, heads)
                shift = jnp.where(visible(info, slot, first + frame), shift, HIDDEN)
                acc_from = acc if frame else None
                add = sums_into(acc_from, acc, sums, rows, column, h, heads)
                lanes.append((q[rows, wide], shift, add))
            add_frame(lanes, kt, values)

    each_head(group, turn)


def near_kernel(group, info, q, m, acc_in, sums_in, near_k, near_v, *refs):
    acc, sums, token, kt, values, k_buf, v_buf, sem = refs
    offset, heads = group
    token[...] = jnp.zeros_like(token)
    first = info[0]
    order = (1, 0)
    copies = {
        frame: [
            pltpu.make_async_copy(
                source.at[pl.ds(frame * FT, FT), pl.ds(offset * HD, heads * HD)],
                buf.at[frame],
                sem.at[frame, n],
            )
            for n, (source, buf) in enumerate(((near_k, k_buf), (near_v, v_buf)))
        ]
        for frame in order
    }
    for frame in order:
        for copy in copies[frame]:
            copy.start()
    values[:, HD:] = jnp.ones((FT, HD), jnp.bfloat16)
    sums[...] = sums_in[...]
    for frame in order:
        for copy in copies[frame]:
            copy.wait()

        def turn(h, column, wide):
            load_frame(kt, values, k_buf.at[frame], v_buf.at[frame], column)
            acc_from = acc_in if frame == order[0] else acc
            lanes = []
            for slot in (0, 1):
                rows = rows_of(slot)
                shift = spread(m[rows, :], h, heads)
                shift = jnp.where(visible(info, slot, first - 2 + frame), shift, HIDDEN)
                add = sums_into(acc_from, acc, sums, rows, column, h, heads)
                lanes.append((q[rows, wide], shift, add))
            add_frame(lanes, kt, values)

        each_head(group, turn)


def final_kernel(
    group, h, info, q, m, acc_in, sums_in,
    sink_a, sink_b, far, relay_k, relay_v, key_any, value_any, near_k, near_v, *refs,
):
    outs = refs[:-8]
    kt, values, k_buf, v_buf, acc, shift, too_large, sem = refs[-8:]
    first = info[0]
    core = info[6]
    far_seen = visible(info, 0, first - 3)
    offset, heads = group
    column = slice(h * HD, (h + 1) * HD)
    wide = slice((offset + h) * HD, (offset + h + 1) * HD)
    values[:, HD:] = jnp.ones((FT, HD), jnp.bfloat16)

    def copies(frame, k, k_row, v, v_row):
        return [
            pltpu.make_async_copy(
                source.at[pl.ds(row, FT), wide], buf.at[frame], sem.at[frame, n]
            )
            for n, (source, row, buf) in enumerate(((k, k_row, k_buf), (v, v_row, v_buf)))
        ]

    arriving = {
        0: [
            (0, sink_a, 0, sink_b, 0),
            (1, far, 0, far, FT),
        ],
        1: [
            (0, sink_b, 0, sink_a, 0),
            (1, relay_k, FT, relay_v, FT),
        ],
    }
    for which, listed in arriving.items():

        @pl.when(core == which)
        def _():
            started = [copies(*entry) for entry in listed]
            for act in (lambda copy: copy.start(), lambda copy: copy.wait()):
                for pair in started:
                    for copy in pair:
                        act(copy)

    def write(slot, acc, total):
        attended = (acc / total).astype(jnp.bfloat16)
        if len(outs) == 1:
            outs[0][rows_of(slot), :] = attended
        else:

            @pl.when(info[1] == slot)
            def _():
                outs[0][...] = attended

            @pl.when(info[1] != slot)
            def _():
                outs[1][...] = attended

    results = {}

    def keep(slot):
        def add(added):
            results[slot] = results[slot] + added if slot in results else added

        return add

    shifts = [spread(m[rows_of(slot), :], h, heads) for slot in (0, 1)]
    load_frame(kt, values, k_buf.at[0], v_buf.at[0], slice(0, HD))
    add_frame(
        [(q[rows_of(slot), wide], shifts[slot], keep(slot)) for slot in (1, 0)], kt, values
    )
    load_frame(kt, values, k_buf.at[1], v_buf.at[1], slice(0, HD))
    shown = jnp.where(far_seen, shifts[0], HIDDEN)
    add_frame([(q[rows_of(0), wide], shown, keep(0))], kt, values)
    for slot in (0, 1):
        rows = rows_of(slot)
        total = spread_sum(sums_in[rows, :], h, heads) + results[slot][:, HD:]
        write(slot, acc_in[rows, column] + results[slot][:, :HD], total)
        too_large[slot] = jnp.max(jnp.where(total < LIMIT, 0.0, 1.0))

    def again(slot):
        here, there = core == 0, core == 1
        sources = [(here, sink_a, 0, sink_b, 0), (there, sink_b, 0, sink_a, 0)]
        if slot == 0:
            sources += [
                (far_seen & here, far, 0, far, FT), (far_seen & there, relay_k, FT, relay_v, FT)
            ]
        for frame in (0, 1):
            row = frame * FT
            own = visible(info, slot, first + frame)
            sources.append((own, key_any, row, value_any, row))
            behind = visible(info, slot, first - 2 + frame)
            sources.append((behind, near_k, row, near_v, row))
        one = (k_buf.at[0], v_buf.at[0])

        def sweep(step):
            def visit(t, carry):
                seen = False
                for n, (shown, k, k_row, v, v_row) in enumerate(sources):
                    chosen = (t == n) & shown
                    seen = seen | chosen

                    @pl.when(chosen)
                    def _():
                        for n, (ref, row) in enumerate(((k, k_row), (v, v_row))):
                            copy = pltpu.make_async_copy(
                                ref.at[pl.ds(row, FT), wide], one[n], sem.at[0, n]
                            )
                            copy.start()
                            copy.wait()

                @pl.when(seen)
                def _():
                    load_frame(kt, values, k_buf.at[0], v_buf.at[0], slice(0, HD))
                    step()

                return carry

            lax.fori_loop(0, len(sources), visit, 0)

        queries = q[rows_of(slot), wide]

        def peak():
            for j in range(FT // BK):
                most = jnp.max(extended_scores(queries, kt, j), axis=1, keepdims=True) * SCALE
                shift[...] = jnp.maximum(shift[...], most)

        def more(added):
            acc[...] = acc[...] + added

        shift[...] = jnp.full((FT, HD), -jnp.inf, jnp.float32)
        acc[...] = jnp.zeros((FT, 2 * HD), jnp.float32)
        sweep(peak)
        sweep(lambda: add_frame([(queries, shift[...], more)], kt, values))
        write(slot, acc[:, :HD], acc[:, HD:])

    for slot in (0, 1):
        pl.when(too_large[slot] > 0.0)(lambda slot=slot: again(slot))


VMEM_SPEC = pl.BlockSpec(memory_space=pltpu.VMEM)
SMEM_SPEC = pl.BlockSpec(memory_space=pltpu.SMEM)


def stage(kernel, arrays, in_any, outs, scratch):
    return pl.pallas_call(
        kernel,
        in_specs=[SMEM_SPEC] + [VMEM_SPEC] * (len(arrays) - in_any - 1) + [ANY_SPEC] * in_any,
        out_specs=[VMEM_SPEC] * len(outs),
        scratch_shapes=[
            pltpu.VMEM((HD, FT), jnp.bfloat16), pltpu.VMEM((FT, 2 * HD), jnp.bfloat16)
        ] + list(scratch),
        out_shape=outs,
        compiler_params=PARAMS,
        cost_estimate=COST,
    )(*arrays)


def last_frames(keys, values):
    return jnp.concatenate([keys[FT:], values[FT:]], axis=0)


def sink_steps(size):
    bits = [1 << b for b in range(1, size.bit_length() - 1)]
    orders = (bits[::-1], [bits[0]] + bits[:0:-1])
    done = [0, 0]
    steps = []
    for step in range(len(bits)):
        pairs = []
        for which in (0, 1):
            bit = orders[which][step]
            holders = [i for i in range(0, size, 2) if i & ~done[which] == 0]
            pairs += [(i + which, (i | bit) + which) for i in holders]
            done[which] |= bit
        steps.append(pairs)
    return steps


def project(info, parts, weight):
    columns = weight.shape[1]
    turns = 6
    block = columns // turns
    rows, depth = parts[0][0].shape
    n = len(parts)

    def kernel(info, *refs):
        weight, out = refs[n:]
        column = span(pl.program_id(0) * block, block)
        total = None
        for a, (_, place, received) in zip(refs[:n], parts):
            owner = 1 - info[1] if received else info[1]
            first = owner * (weight.shape[0] // 2) + place * depth
            product = dot(a[...], weight[span(first, depth), column])
            total = product if total is None else total + product
        out[...] = total.astype(jnp.bfloat16)

    return pl.pallas_call(
        kernel,
        grid=(turns,),
        in_specs=[SMEM_SPEC] + [VMEM_SPEC] * (n + 1),
        out_specs=pl.BlockSpec((rows, block), lambda i: (0, i)),
        out_shape=jax.ShapeDtypeStruct((rows, columns), jnp.bfloat16),
        compiler_params=PARAMS,
        cost_estimate=COST,
    )(info, *[a for a, _, _ in parts], weight)


def local(query_states, key_states, value_states, win_start, group_end, out_weight):
    axis = "tm"
    size = lax.axis_size(axis)
    paired = lax.axis_size("head") == 2
    me = lax.axis_index(axis)
    core = me % 2
    heads = query_states.shape[1] // HD
    info = jnp.concatenate(
        [
            jnp.stack([me * 2, lax.axis_index("head")]).astype(jnp.int32),
            win_start.astype(jnp.int32),
            group_end.astype(jnp.int32),
            jnp.stack([core]).astype(jnp.int32),
        ]
    )
    groups = [(0, heads // 2), (heads // 2, heads // 2)] if heads % 2 == 0 else [(0, heads)]
    rows, width = query_states.shape
    q_like = jax.ShapeDtypeStruct((rows, width), jnp.bfloat16)
    group_width = groups[0][1] * HD
    m_like = jax.ShapeDtypeStruct((rows, HD), jnp.bfloat16)
    acc_like = jax.ShapeDtypeStruct((rows, group_width), jnp.float32)
    sums_like = jax.ShapeDtypeStruct((rows, HD), jnp.float32)

    def frame_buffers(columns):
        return [pltpu.VMEM((2, FT, columns), jnp.bfloat16)] * 2

    dma_sems = pltpu.SemaphoreType.DMA((2, 2))

    onward = [(i, i + 1) for i in range(size - 1)]
    near_k = lax.ppermute(key_states, axis, onward)
    moved = lax.ppermute(value_states, axis, [(0, 1)])
    held = jnp.where(core == 0, key_states[:FT], moved[:FT])
    own_last = last_frames(key_states, value_states)
    far = lax.ppermute(own_last, axis, [(i, i + 2) for i in range(0, size - 2, 2)])

    def arrived(array):
        return array[0, 0] == array[0, 0]

    def near_stage(group, state):
        return stage(
            functools.partial(near_kernel, group),
            [info, query_states, *state, near_k, near_v], 2, [acc_like, sums_like, TOKEN],
            frame_buffers(group_width) + [dma_sems],
        )

    states = []
    steps = sink_steps(size)
    for step, pairs in enumerate(steps):
        moved = lax.ppermute(held, axis, pairs)
        takes = jnp.zeros((), bool)
        for _, target in pairs:
            takes = takes | (me == target)
        if step < len(groups):
            *passed, m, acc, sums, token = stage(
                functools.partial(own_kernel, groups[step]),
                [info, query_states, key_states, value_states], 0,
                [q_like] * (step == 0) + [m_like, acc_like, sums_like, TOKEN], [],
            )
            states.append((m, acc, sums))
            takes = takes & (token[0, 0] == 0)
            if step == 0:
                near_v = lax.ppermute(passed[0], axis, onward)
        if step == len(steps) - 2:
            takes = takes & arrived(near_k)
        if step == len(steps) - 1:
            *sums_now, token = near_stage(groups[0], states[0])
            states[0] = states[0][0], *sums_now
            takes = takes & (token[0, 0] == 0) & arrived(far)
        held = jnp.where(takes, moved, held)
    other = lax.ppermute(held, axis, [(i, i ^ 1) for i in range(size)])
    on_chip = [(i, i + 1) for i in range(0, size, 2)]
    relay_k = lax.ppermute(near_k, axis, on_chip)
    relay_v = lax.ppermute(near_v, axis, on_chip)

    for g, group in enumerate(groups[1:], 1):
        *sums_now, _ = near_stage(group, states[g])
        states[g] = states[g][0], *sums_now
    mine, theirs = [], []
    for g, group in enumerate(groups):
        for h in range(group[1]):
            part = jax.ShapeDtypeStruct((FT if paired else rows, HD), jnp.bfloat16)
            results = stage(
                functools.partial(final_kernel, group, h),
                [info, query_states, *states[g], held, other, far, relay_k, relay_v,
                 key_states, value_states, near_k, near_v], 9,
                [part] * (2 if paired else 1),
                frame_buffers(HD) + [
                    pltpu.VMEM((FT, 2 * HD), jnp.float32),
                    pltpu.VMEM((FT, HD), jnp.float32),
                    pltpu.SMEM((2,), jnp.float32),
                    dma_sems,
                ],
            )
            mine.append(results[0])
            if paired:
                theirs.append(lax.ppermute(results[1], "head", [(0, 1), (1, 0)]))
    if not paired:
        attended = jnp.concatenate(mine, axis=1)
        token_rows = lax.all_to_all(attended, "head", split_axis=0, concat_axis=1, tiled=True)
        return dot(token_rows, out_weight).astype(jnp.bfloat16)
    parts = [(array, g, False) for g, array in enumerate(mine)]
    parts += [(array, g, True) for g, array in enumerate(theirs)]
    return project(info, parts, out_weight)


def solution(mesh):
    in_specs = (P("tm", "head"), P("tm", "head"), P("tm", "head"), P("tm"), P("tm"), P())
    out_specs = P(("tm", "head"), None)
    return jax.shard_map(local, mesh=mesh, in_specs=in_specs, out_specs=out_specs, check_vma=False)
```

```python
import functools

import jax
import jax.numpy as jnp
from jax import lax
from jax.experimental import pallas as pl
from jax.experimental.pallas import tpu as pltpu
from jax.sharding import PartitionSpec as P

HD = 128
FT = 768
BK = 256
LOG2E = 1.4426950408889634
SCALE = HD ** -0.5 * LOG2E
LIMIT = 1e30
HIDDEN = 1e30
PARAMS = pltpu.CompilerParams(vmem_limit_bytes=12 * 1024 * 1024)
ANY_SPEC = pl.BlockSpec(memory_space=pl.ANY)
NEAR_COST = pl.CostEstimate(flops=8_000_000_000, bytes_accessed=1000, transcendentals=0)
COST = pl.CostEstimate(flops=1000, bytes_accessed=1000, transcendentals=0)
TOKEN = jax.ShapeDtypeStruct((8, 128), jnp.float32)


def dot(a, b):
    return jnp.dot(a, b, preferred_element_type=jnp.float32)


def span(start, size):
    return pl.ds(pl.multiple_of(start, size), size)


def rows_of(slot):
    return slice(slot * FT, (slot + 1) * FT)


def extended_scores(q, kt, j):
    return dot(q, kt[:, j * BK : (j + 1) * BK])


def add_frame(lanes, kt, values):
    units = [(n, j) for n in range(len(lanes)) for j in range(FT // BK)]

    def fetch(unit):
        n, j = unit
        return extended_scores(lanes[n][0], kt, j)

    ahead = fetch(units[0])
    weights = []
    for at, (n, j) in enumerate(units):
        s = ahead
        if at + 1 < len(units):
            ahead = fetch(units[at + 1])
        _, shift, add = lanes[n]
        for c in range(0, BK, HD):
            weights.append(jnp.exp2(s[:, c : c + HD] * SCALE - shift).astype(jnp.bfloat16))
        if j == FT // BK - 1:
            add(dot(jnp.concatenate(weights, axis=1), values[...]))
            weights = []


def visible(info, slot, frame):
    return (frame >= 1) & (frame >= info[2 + slot]) & (frame <= info[4 + slot])


def lanes_of(h, heads):
    share = HD // heads
    lane = lax.broadcasted_iota(jnp.int32, (1, HD), 1)
    return (lane >= h * share) & (lane < (h + 1) * share)


def spread(packed, h, heads):
    row = lax.broadcasted_iota(jnp.int32, (HD, HD), 0)
    chosen = jnp.where(row == h * (HD // heads), 1.0, 0.0).astype(jnp.bfloat16)
    return dot(packed, chosen)


def spread_sum(packed, h, heads):
    high = packed.astype(jnp.bfloat16)
    low = (packed - high.astype(jnp.float32)).astype(jnp.bfloat16)
    return spread(high, h, heads) + spread(low, h, heads)


def sums_into(acc_from, acc, sums, rows, column, h, heads):
    def add(added):
        new = added[:, :HD]
        acc[rows, column] = new if acc_from is None else acc_from[rows, column] + new
        old = sums[rows, :]
        sums[rows, :] = jnp.where(lanes_of(h, heads), old + added[:, HD:], old)

    return add


def load_frame(kt, values, k, v, column):
    kt[...] = k[:, column].T
    values[:, :HD] = v[:, column]


def each_head(group, turn):
    offset, count = group

    def body(h, carry):
        turn(h, span(h * HD, HD), span((h + offset) * HD, HD))
        return carry

    lax.fori_loop(0, count, body, 0)


def own_kernel(group, info, q, k, v, *refs):
    m, acc, sums, token, kt, values = refs[-6:]
    if len(refs) > 6:
        refs[0][...] = v[...]
    heads = group[1]
    first = info[0]
    token[...] = jnp.zeros_like(token)
    values[:, HD:] = jnp.ones((FT, HD), jnp.bfloat16)
    ones = jnp.ones((HD, HD), jnp.bfloat16)
    m[...] = jnp.zeros_like(m)
    sums[...] = jnp.zeros_like(sums)

    def turn(h, column, wide):
        here = lanes_of(h, heads)
        for slot in (0, 1):
            rows = rows_of(slot)
            product = q[rows, wide].astype(jnp.float32) * k[rows, wide].astype(jnp.float32)
            own = (dot(product.astype(jnp.bfloat16), ones) * SCALE).astype(jnp.bfloat16)
            m[rows, :] = jnp.where(here, own, m[rows, :])
        for frame in (0, 1):
            load_frame(kt, values, k.at[rows_of(frame)], v.at[rows_of(frame)], wide)
            lanes = []
            for slot in (0, 1):
                rows = rows_of(slot)
                shift = spread(m[rows, :], h, heads)
                shift = jnp.where(visible(info, slot, first + frame), shift, HIDDEN)
                acc_from = acc if frame else None
                add = sums_into(acc_from, acc, sums, rows, column, h, heads)
                lanes.append((q[rows, wide], shift, add))
            add_frame(lanes, kt, values)

    each_head(group, turn)


def near_kernel(group, info, q, m, acc_in, sums_in, near_k, near_v, *refs):
    acc, sums, token, kt, values, k_buf, v_buf, sem = refs
    offset, heads = group
    token[...] = jnp.zeros_like(token)
    first = info[0]
    order = (1, 0)
    copies = {
        frame: [
            pltpu.make_async_copy(
                source.at[pl.ds(frame * FT, FT), pl.ds(offset * HD, heads * HD)],
                buf.at[frame],
                sem.at[frame, n],
            )
            for n, (source, buf) in enumerate(((near_k, k_buf), (near_v, v_buf)))
        ]
        for frame in order
    }
    for frame in order:
        for copy in copies[frame]:
            copy.start()
    values[:, HD:] = jnp.ones((FT, HD), jnp.bfloat16)
    sums[...] = sums_in[...]
    for frame in order:
        for copy in copies[frame]:
            copy.wait()

        def turn(h, column, wide):
            load_frame(kt, values, k_buf.at[frame], v_buf.at[frame], column)
            acc_from = acc_in if frame == order[0] else acc
            lanes = []
            for slot in (0, 1):
                rows = rows_of(slot)
                shift = spread(m[rows, :], h, heads)
                shift = jnp.where(visible(info, slot, first - 2 + frame), shift, HIDDEN)
                add = sums_into(acc_from, acc, sums, rows, column, h, heads)
                lanes.append((q[rows, wide], shift, add))
            add_frame(lanes, kt, values)

        each_head(group, turn)


def final_kernel(
    group, info, q, m, acc_in, sums_in,
    sink_a, sink_b, far, relay_k, relay_v, key_any, value_any, near_k, near_v, *refs,
):
    outs = refs[:-8]
    kt, values, k_buf, v_buf, acc, shift, too_large, sem = refs[-8:]
    first = info[0]
    core = info[6]
    far_seen = visible(info, 0, first - 3)
    offset, heads = group
    group_columns = pl.ds(offset * HD, heads * HD)
    values[:, HD:] = jnp.ones((FT, HD), jnp.bfloat16)

    def copies(frame, k, k_row, v, v_row, columns):
        return [
            pltpu.make_async_copy(
                source.at[pl.ds(row, FT), columns], buf.at[frame], sem.at[frame, n]
            )
            for n, (source, row, buf) in enumerate(((k, k_row, k_buf), (v, v_row, v_buf)))
        ]

    arriving = {
        0: [
            (0, sink_a, 0, sink_b, 0, group_columns),
            (1, far, 0, far, FT, group_columns),
        ],
        1: [
            (0, sink_b, 0, sink_a, 0, group_columns),
            (1, relay_k, FT, relay_v, FT, group_columns),
        ],
    }
    for which, listed in arriving.items():

        @pl.when(core == which)
        def _():
            started = [copies(*entry) for entry in listed]
            for act in (lambda copy: copy.start(), lambda copy: copy.wait()):
                for pair in started:
                    for copy in pair:
                        act(copy)

    def write(slot, h, acc, total):
        attended = (acc / total).astype(jnp.bfloat16)
        column = span(h * HD, HD)
        if len(outs) == 1:
            outs[0][rows_of(slot), column] = attended
        else:

            @pl.when(info[1] == slot)
            def _():
                outs[0][:, column] = attended

            @pl.when(info[1] != slot)
            def _():
                outs[1][:, column] = attended

    def turn(h, column, wide):
        results = {}

        def keep(slot):
            def add(added):
                results[slot] = results[slot] + added if slot in results else added

            return add

        shifts = [spread(m[rows_of(slot), :], h, heads) for slot in (0, 1)]
        load_frame(kt, values, k_buf.at[0], v_buf.at[0], column)
        add_frame(
            [(q[rows_of(slot), wide], shifts[slot], keep(slot)) for slot in (1, 0)], kt, values
        )
        load_frame(kt, values, k_buf.at[1], v_buf.at[1], column)
        shown = jnp.where(far_seen, shifts[0], HIDDEN)
        add_frame([(q[rows_of(0), wide], shown, keep(0))], kt, values)
        for slot in (0, 1):
            rows = rows_of(slot)
            total = spread_sum(sums_in[rows, :], h, heads) + results[slot][:, HD:]
            write(slot, h, acc_in[rows, column] + results[slot][:, :HD], total)
            too_large[h, slot] = jnp.max(jnp.where(total < LIMIT, 0.0, 1.0))

    each_head(group, turn)

    def again(slot, h, wide):
        here, there = core == 0, core == 1
        sources = [(here, sink_a, 0, sink_b, 0), (there, sink_b, 0, sink_a, 0)]
        if slot == 0:
            sources += [
                (far_seen & here, far, 0, far, FT), (far_seen & there, relay_k, FT, relay_v, FT)
            ]
        for frame in (0, 1):
            row = frame * FT
            own = visible(info, slot, first + frame)
            sources.append((own, key_any, row, value_any, row))
            behind = visible(info, slot, first - 2 + frame)
            sources.append((behind, near_k, row, near_v, row))
        one = (k_buf.at[0, :, :HD], v_buf.at[0, :, :HD])

        def sweep(step):
            def visit(t, carry):
                seen = False
                for n, (shown, k, k_row, v, v_row) in enumerate(sources):
                    chosen = (t == n) & shown
                    seen = seen | chosen

                    @pl.when(chosen)
                    def _():
                        for n, (ref, row) in enumerate(((k, k_row), (v, v_row))):
                            copy = pltpu.make_async_copy(
                                ref.at[pl.ds(row, FT), wide], one[n], sem.at[0, n]
                            )
                            copy.start()
                            copy.wait()

                @pl.when(seen)
                def _():
                    load_frame(kt, values, k_buf.at[0], v_buf.at[0], slice(0, HD))
                    step()

                return carry

            lax.fori_loop(0, len(sources), visit, 0)

        queries = q[rows_of(slot), wide]

        def peak():
            for j in range(FT // BK):
                most = jnp.max(extended_scores(queries, kt, j), axis=1, keepdims=True) * SCALE
                shift[...] = jnp.maximum(shift[...], most)

        def more(added):
            acc[...] = acc[...] + added

        shift[...] = jnp.full((FT, HD), -jnp.inf, jnp.float32)
        acc[...] = jnp.zeros((FT, 2 * HD), jnp.float32)
        sweep(peak)
        sweep(lambda: add_frame([(queries, shift[...], more)], kt, values))
        write(slot, h, acc[:, :HD], acc[:, HD:])

    def check(h, column, wide):
        for slot in (0, 1):
            pl.when(too_large[h, slot] > 0.0)(lambda slot=slot: again(slot, h, wide))

    each_head(group, check)


VMEM_SPEC = pl.BlockSpec(memory_space=pltpu.VMEM)
SMEM_SPEC = pl.BlockSpec(memory_space=pltpu.SMEM)


def stage(kernel, arrays, in_any, outs, scratch, cost=None):
    return pl.pallas_call(
        kernel,
        in_specs=[SMEM_SPEC] + [VMEM_SPEC] * (len(arrays) - in_any - 1) + [ANY_SPEC] * in_any,
        out_specs=[VMEM_SPEC] * len(outs),
        scratch_shapes=[
            pltpu.VMEM((HD, FT), jnp.bfloat16), pltpu.VMEM((FT, 2 * HD), jnp.bfloat16)
        ] + list(scratch),
        out_shape=outs,
        compiler_params=PARAMS,
        cost_estimate=cost or COST,
    )(*arrays)


def last_frames(keys, values):
    return jnp.concatenate([keys[FT:], values[FT:]], axis=0)


def sink_steps(size):
    bits = [1 << b for b in range(1, size.bit_length() - 1)]
    orders = (bits[::-1], bits[::-1])
    done = [0, 0]
    steps = []
    for step in range(len(bits)):
        pairs = []
        for which in (0, 1):
            bit = orders[which][step]
            holders = [i for i in range(0, size, 2) if i & ~done[which] == 0]
            pairs += [(i + which, (i | bit) + which) for i in holders]
            done[which] |= bit
        steps.append(pairs)
    return steps


def project(info, parts, weight):
    columns = weight.shape[1]
    turns = 6
    block = columns // turns
    rows, depth = parts[0][0].shape
    n = len(parts)

    def kernel(info, *refs):
        weight, out = refs[n:]
        column = span(pl.program_id(0) * block, block)
        total = None
        for a, (_, place, received) in zip(refs[:n], parts):
            owner = 1 - info[1] if received else info[1]
            first = owner * (weight.shape[0] // 2) + place * depth
            product = dot(a[...], weight[span(first, depth), column])
            total = product if total is None else total + product
        out[...] = total.astype(jnp.bfloat16)

    return pl.pallas_call(
        kernel,
        grid=(turns,),
        in_specs=[SMEM_SPEC] + [VMEM_SPEC] * (n + 1),
        out_specs=pl.BlockSpec((rows, block), lambda i: (0, i)),
        out_shape=jax.ShapeDtypeStruct((rows, columns), jnp.bfloat16),
        compiler_params=PARAMS,
        cost_estimate=COST,
    )(info, *[a for a, _, _ in parts], weight)


def local(query_states, key_states, value_states, win_start, group_end, out_weight):
    axis = "tm"
    size = lax.axis_size(axis)
    paired = lax.axis_size("head") == 2
    me = lax.axis_index(axis)
    core = me % 2
    heads = query_states.shape[1] // HD
    info = jnp.concatenate(
        [
            jnp.stack([me * 2, lax.axis_index("head")]).astype(jnp.int32),
            win_start.astype(jnp.int32),
            group_end.astype(jnp.int32),
            jnp.stack([core]).astype(jnp.int32),
        ]
    )
    groups = [(0, heads // 2), (heads // 2, heads // 2)] if heads % 2 == 0 else [(0, heads)]
    rows, width = query_states.shape
    q_like = jax.ShapeDtypeStruct((rows, width), jnp.bfloat16)
    group_width = groups[0][1] * HD
    m_like = jax.ShapeDtypeStruct((rows, HD), jnp.bfloat16)
    acc_like = jax.ShapeDtypeStruct((rows, group_width), jnp.float32)
    sums_like = jax.ShapeDtypeStruct((rows, HD), jnp.float32)
    frame_buffers = [pltpu.VMEM((2, FT, group_width), jnp.bfloat16)] * 2
    dma_sems = pltpu.SemaphoreType.DMA((2, 2))

    onward = [(i, i + 1) for i in range(size - 1)]
    near_k = lax.ppermute(key_states, axis, onward)
    moved = lax.ppermute(value_states, axis, [(0, 1)])
    held = jnp.where(core == 0, key_states[:FT], moved[:FT])

    def arrived(array):
        return array[0, 0] == array[0, 0]

    def near_stage(group, state):
        return stage(
            functools.partial(near_kernel, group),
            [info, query_states, *state, near_k, near_v], 2, [acc_like, sums_like, TOKEN],
            frame_buffers + [dma_sems], NEAR_COST,
        )

    states = []
    steps = sink_steps(size)
    for step, pairs in enumerate(steps):
        moved = lax.ppermute(held, axis, pairs)
        takes = jnp.zeros((), bool)
        for _, target in pairs:
            takes = takes | (me == target)
        if step < len(groups):
            *passed, m, acc, sums, token = stage(
                functools.partial(own_kernel, groups[step]),
                [info, query_states, key_states, value_states], 0,
                [q_like] * (step == 0) + [m_like, acc_like, sums_like, TOKEN], [],
            )
            states.append((m, acc, sums))
            takes = takes & (token[0, 0] == 0)
            if step == 0:
                near_v = lax.ppermute(passed[0], axis, onward)
                takes = takes & arrived(near_k)
            if step == len(groups) - 1:
                own_last = jnp.where(token[0, 0] == 0, last_frames(key_states, value_states), 0)
                far = lax.ppermute(own_last, axis, [(i, i + 2) for i in range(0, size - 2, 2)])
        if step == len(steps) - 1:
            *sums_now, token = near_stage(groups[0], states[0])
            states[0] = states[0][0], *sums_now
            takes = takes & (token[0, 0] == 0) & arrived(far)
        held = jnp.where(takes, moved, held)
    other = lax.ppermute(held, axis, [(i, i ^ 1) for i in range(size)])
    on_chip = [(i, i + 1) for i in range(0, size, 2)]
    relay_k = lax.ppermute(near_k, axis, on_chip)
    relay_v = lax.ppermute(near_v, axis, on_chip)

    for g, group in enumerate(groups[1:], 1):
        *sums_now, _ = near_stage(group, states[g])
        states[g] = states[g][0], *sums_now
    mine, theirs = [], []
    for g, group in enumerate(groups):
        part = jax.ShapeDtypeStruct((FT if paired else rows, group_width), jnp.bfloat16)
        results = stage(
            functools.partial(final_kernel, group),
            [info, query_states, *states[g], held, other, far, relay_k, relay_v,
             key_states, value_states, near_k, near_v], 9,
            [part] * (2 if paired else 1),
            frame_buffers + [
                pltpu.VMEM((FT, 2 * HD), jnp.float32),
                pltpu.VMEM((FT, HD), jnp.float32),
                pltpu.SMEM((group[1], 2), jnp.float32),
                dma_sems,
            ],
        )
        mine.append(results[0])
        if paired:
            theirs.append(lax.ppermute(results[1], "head", [(0, 1), (1, 0)]))
    if not paired:
        attended = jnp.concatenate(mine, axis=1)
        token_rows = lax.all_to_all(attended, "head", split_axis=0, concat_axis=1, tiled=True)
        return dot(token_rows, out_weight).astype(jnp.bfloat16)
    parts = [(array, g, False) for g, array in enumerate(mine)]
    parts += [(array, g, True) for g, array in enumerate(theirs)]
    return project(info, parts, out_weight)


def solution(mesh):
    in_specs = (P("tm", "head"), P("tm", "head"), P("tm", "head"), P("tm"), P("tm"), P())
    out_specs = P(("tm", "head"), None)
    return jax.shard_map(local, mesh=mesh, in_specs=in_specs, out_specs=out_specs, check_vma=False)
```

```python
import functools

import jax
import jax.numpy as jnp
from jax import lax
from jax.experimental import pallas as pl
from jax.experimental.pallas import tpu as pltpu
from jax.sharding import PartitionSpec as P

HD = 128
FT = 768
BK = 256
LOG2E = 1.4426950408889634
SCALE = HD ** -0.5 * LOG2E
LIMIT = 1e30
HIDDEN = 1e30
PARAMS = pltpu.CompilerParams(vmem_limit_bytes=12 * 1024 * 1024)
ANY_SPEC = pl.BlockSpec(memory_space=pl.ANY)
NEAR_COST = pl.CostEstimate(flops=8_000_000_000, bytes_accessed=1000, transcendentals=0)
COST = pl.CostEstimate(flops=1000, bytes_accessed=1000, transcendentals=0)
TOKEN = jax.ShapeDtypeStruct((8, 128), jnp.float32)


def dot(a, b):
    return jnp.dot(a, b, preferred_element_type=jnp.float32)


def span(start, size):
    return pl.ds(pl.multiple_of(start, size), size)


def rows_of(slot):
    return slice(slot * FT, (slot + 1) * FT)


def add_frame(lanes, kt, values):
    units = [(n, j) for n in range(len(lanes)) for j in range(FT // BK)]

    def scores(unit):
        n, j = unit
        return dot(lanes[n][0], kt[:, j * BK : (j + 1) * BK])

    ahead = scores(units[0])
    weights = []
    for at, (n, j) in enumerate(units):
        s = ahead
        if at + 1 < len(units):
            ahead = scores(units[at + 1])
        weights.append(jnp.exp2(s * SCALE).astype(jnp.bfloat16))
        if j == FT // BK - 1:
            lanes[n][1](dot(jnp.concatenate(weights, axis=1), values[...]))
            weights = []


def visible(info, slot, frame):
    return (frame >= 1) & (frame >= info[2 + slot]) & (frame <= info[4 + slot])


def lanes_of(h, heads):
    share = HD // heads
    lane = lax.broadcasted_iota(jnp.int32, (1, HD), 1)
    return (lane >= h * share) & (lane < (h + 1) * share)


def spread(packed, h, heads):
    row = lax.broadcasted_iota(jnp.int32, (HD, HD), 0)
    chosen = jnp.where(row == h * (HD // heads), 1.0, 0.0).astype(jnp.bfloat16)
    high = packed.astype(jnp.bfloat16)
    low = (packed - high.astype(jnp.float32)).astype(jnp.bfloat16)
    return dot(high, chosen) + dot(low, chosen)


def more_columns(own, slot):
    lane = lax.broadcasted_iota(jnp.int32, (1, HD), 1)
    flag = jnp.where(lane == 1 + slot, 1.0, 0.0)
    return jnp.where(lane == 0, -own, flag).astype(jnp.bfloat16)


def set_more_rows(kt, seen):
    row = lax.broadcasted_iota(jnp.int32, (HD, FT), 0)
    more = jnp.where(row == 0, 1.0, 0.0)
    for slot, shown in enumerate(seen):
        more = jnp.where(row == 1 + slot, jnp.where(shown, 0.0, -HIDDEN), more)
    kt[HD:, :] = more.astype(jnp.bfloat16)


def sums_into(acc_from, acc, sums, rows, column, h, heads):
    def add(added):
        new = added[:, :HD]
        acc[rows, column] = new if acc_from is None else acc_from[rows, column] + new
        old = sums[rows, :]
        sums[rows, :] = jnp.where(lanes_of(h, heads), old + added[:, HD:], old)

    return add


def load_frame(kt, values, k, v, column):
    kt[:HD, :] = k[:, column].T
    values[:, :HD] = v[:, column]


def each_head(group, turn):
    offset, count = group

    def body(h, carry):
        turn(h, span(h * HD, HD), span((h + offset) * HD, HD))
        return carry

    lax.fori_loop(0, count, body, 0)


def own_kernel(group, info, q, k, v, *refs):
    more, acc, sums, token, kt, values = refs[-6:]
    if len(refs) > 6:
        refs[0][...] = v[...]
    heads = group[1]
    first = info[0]
    token[...] = jnp.zeros_like(token)
    values[:, HD:] = jnp.ones((FT, HD), jnp.bfloat16)
    ones = jnp.ones((HD, HD), jnp.bfloat16)
    sums[...] = jnp.zeros_like(sums)

    def shifts(h, column, wide):
        for slot in (0, 1):
            rows = rows_of(slot)
            product = q[rows, wide].astype(jnp.float32) * k[rows, wide].astype(jnp.float32)
            more[rows, column] = more_columns(dot(product.astype(jnp.bfloat16), ones), slot)

    each_head(group, shifts)
    for frame in (0, 1):
        set_more_rows(kt, [visible(info, slot, first + frame) for slot in (0, 1)])

        def turn(h, column, wide):
            load_frame(kt, values, k.at[rows_of(frame)], v.at[rows_of(frame)], wide)
            lanes = []
            for slot in (0, 1):
                rows = rows_of(slot)
                add = sums_into(acc if frame else None, acc, sums, rows, column, h, heads)
                queries = jnp.concatenate([q[rows, wide], more[rows, column]], axis=1)
                lanes.append((queries, add))
            add_frame(lanes, kt, values)

        each_head(group, turn)


def near_kernel(group, info, q, more, acc_in, sums_in, near_k, near_v, *refs):
    acc, sums, token, kt, values, k_buf, v_buf, sem = refs
    offset, heads = group
    token[...] = jnp.zeros_like(token)
    first = info[0]
    order = (1, 0)
    copies = {
        frame: [
            pltpu.make_async_copy(
                source.at[pl.ds(frame * FT, FT), pl.ds(offset * HD, heads * HD)],
                buf.at[frame],
                sem.at[frame, n],
            )
            for n, (source, buf) in enumerate(((near_k, k_buf), (near_v, v_buf)))
        ]
        for frame in order
    }
    for frame in order:
        for copy in copies[frame]:
            copy.start()
    values[:, HD:] = jnp.ones((FT, HD), jnp.bfloat16)
    sums[...] = sums_in[...]
    for frame in order:
        set_more_rows(kt, [visible(info, slot, first - 2 + frame) for slot in (0, 1)])
        for copy in copies[frame]:
            copy.wait()

        def turn(h, column, wide):
            load_frame(kt, values, k_buf.at[frame], v_buf.at[frame], column)
            acc_from = acc_in if frame == order[0] else acc
            lanes = []
            for slot in (0, 1):
                rows = rows_of(slot)
                add = sums_into(acc_from, acc, sums, rows, column, h, heads)
                queries = jnp.concatenate([q[rows, wide], more[rows, column]], axis=1)
                lanes.append((queries, add))
            add_frame(lanes, kt, values)

        each_head(group, turn)


def final_kernel(
    group, info, q, more, acc_in, sums_in,
    sink_a, sink_b, far, relay_k, relay_v, key_any, value_any, near_k, near_v, *refs,
):
    outs = refs[:-8]
    kt, values, k_buf, v_buf, acc, shift, too_large, sem = refs[-8:]
    first = info[0]
    core = info[6]
    far_seen = visible(info, 0, first - 3)
    offset, heads = group
    group_columns = pl.ds(offset * HD, heads * HD)
    values[:, HD:] = jnp.ones((FT, HD), jnp.bfloat16)

    def copies(frame, k, k_row, v, v_row, columns):
        return [
            pltpu.make_async_copy(
                source.at[pl.ds(row, FT), columns], buf.at[frame], sem.at[frame, n]
            )
            for n, (source, row, buf) in enumerate(((k, k_row, k_buf), (v, v_row, v_buf)))
        ]

    arriving = {
        0: [
            (0, sink_a, 0, sink_b, 0, group_columns),
            (1, far, 0, far, FT, group_columns),
        ],
        1: [
            (0, sink_b, 0, sink_a, 0, group_columns),
            (1, relay_k, FT, relay_v, FT, group_columns),
        ],
    }
    for which, listed in arriving.items():

        @pl.when(core == which)
        def _():
            started = [copies(*entry) for entry in listed]
            for act in (lambda copy: copy.start(), lambda copy: copy.wait()):
                for pair in started:
                    for copy in pair:
                        act(copy)

    def write(slot, h, acc, total):
        attended = (acc / total).astype(jnp.bfloat16)
        column = span(h * HD, HD)
        if len(outs) == 1:
            outs[0][rows_of(slot), column] = attended
        else:

            @pl.when(info[1] == slot)
            def _():
                outs[0][:, column] = attended

            @pl.when(info[1] != slot)
            def _():
                outs[1][:, column] = attended

    def turn(h, column, wide):
        results = {}

        def keep(slot):
            def add(added):
                results[slot] = results[slot] + added if slot in results else added

            return add

        queries = [
            jnp.concatenate([q[rows_of(slot), wide], more[rows_of(slot), column]], axis=1)
            for slot in (0, 1)
        ]
        load_frame(kt, values, k_buf.at[0], v_buf.at[0], column)
        set_more_rows(kt, [True, True])
        add_frame([(queries[slot], keep(slot)) for slot in (1, 0)], kt, values)
        load_frame(kt, values, k_buf.at[1], v_buf.at[1], column)
        set_more_rows(kt, [far_seen, False])
        add_frame([(queries[0], keep(0))], kt, values)
        for slot in (0, 1):
            rows = rows_of(slot)
            total = spread(sums_in[rows, :], h, heads) + results[slot][:, HD:]
            write(slot, h, acc_in[rows, column] + results[slot][:, :HD], total)
            too_large[h, slot] = jnp.max(jnp.where(total < LIMIT, 0.0, 1.0))

    each_head(group, turn)

    def again(slot, h, wide):
        here, there = core == 0, core == 1
        sources = [(here, sink_a, 0, sink_b, 0), (there, sink_b, 0, sink_a, 0)]
        if slot == 0:
            sources += [
                (far_seen & here, far, 0, far, FT), (far_seen & there, relay_k, FT, relay_v, FT)
            ]
        for frame in (0, 1):
            row = frame * FT
            own = visible(info, slot, first + frame)
            sources.append((own, key_any, row, value_any, row))
            behind = visible(info, slot, first - 2 + frame)
            sources.append((behind, near_k, row, near_v, row))
        one = (k_buf.at[0, :, :HD], v_buf.at[0, :, :HD])

        def sweep(step):
            def visit(t, carry):
                seen = False
                for n, (shown, k, k_row, v, v_row) in enumerate(sources):
                    chosen = (t == n) & shown
                    seen = seen | chosen

                    @pl.when(chosen)
                    def _():
                        for n, (ref, row) in enumerate(((k, k_row), (v, v_row))):
                            copy = pltpu.make_async_copy(
                                ref.at[pl.ds(row, FT), wide], one[n], sem.at[0, n]
                            )
                            copy.start()
                            copy.wait()

                @pl.when(seen)
                def _():
                    load_frame(kt, values, k_buf.at[0], v_buf.at[0], slice(0, HD))
                    step()

                return carry

            lax.fori_loop(0, len(sources), visit, 0)

        queries = q[rows_of(slot), wide]

        def scores(j):
            return dot(queries, kt[:HD, j * BK : (j + 1) * BK]) * SCALE

        def peak():
            for j in range(FT // BK):
                shift[...] = jnp.maximum(shift[...], jnp.max(scores(j), axis=1, keepdims=True))

        def more_sums():
            for j in range(FT // BK):
                s = scores(j)
                weights = jnp.concatenate(
                    [jnp.exp2(s[:, c : c + HD] - shift[...]) for c in range(0, BK, HD)], axis=1
                )
                keys = values[j * BK : (j + 1) * BK, :]
                acc[...] = acc[...] + dot(weights.astype(jnp.bfloat16), keys)

        shift[...] = jnp.full((FT, HD), -jnp.inf, jnp.float32)
        acc[...] = jnp.zeros((FT, 2 * HD), jnp.float32)
        sweep(peak)
        sweep(more_sums)
        write(slot, h, acc[:, :HD], acc[:, HD:])

    def check(h, column, wide):
        for slot in (0, 1):
            pl.when(too_large[h, slot] > 0.0)(lambda slot=slot: again(slot, h, wide))

    each_head(group, check)


VMEM_SPEC = pl.BlockSpec(memory_space=pltpu.VMEM)
SMEM_SPEC = pl.BlockSpec(memory_space=pltpu.SMEM)


def stage(kernel, arrays, in_any, outs, scratch, cost=None, tokens=()):
    n = len(arrays)

    def run(*refs):
        kernel(*refs[:n], *refs[n + len(tokens) :])

    return pl.pallas_call(
        run,
        in_specs=[SMEM_SPEC] + [VMEM_SPEC] * (n - in_any - 1)
        + [ANY_SPEC] * (in_any + len(tokens)),
        out_specs=[VMEM_SPEC] * len(outs),
        scratch_shapes=[
            pltpu.VMEM((2 * HD, FT), jnp.bfloat16), pltpu.VMEM((FT, 2 * HD), jnp.bfloat16)
        ] + list(scratch),
        out_shape=outs,
        compiler_params=PARAMS,
        cost_estimate=cost or COST,
    )(*arrays, *tokens)


def small(kernel, scalars, arrays, tokens, rows):
    width = arrays[0].shape[1]
    n = len(arrays)

    def run(scalars, *refs):
        kernel(scalars, *refs[:n], refs[-1])

    return pl.pallas_call(
        run,
        in_specs=[SMEM_SPEC] + [VMEM_SPEC] * n + [ANY_SPEC] * len(tokens),
        out_specs=VMEM_SPEC,
        out_shape=jax.ShapeDtypeStruct((rows, width), jnp.bfloat16),
        compiler_params=PARAMS,
        cost_estimate=COST,
    )(jnp.reshape(scalars, (1,)).astype(jnp.int32), *arrays, *tokens)


def pick(flag, taken, kept, tokens=()):
    def kernel(flag, taken, kept, out):
        @pl.when(flag[0] == 1)
        def _():
            out[...] = taken[:FT, :]

        @pl.when(flag[0] == 0)
        def _():
            out[...] = kept[:FT, :]

    return small(kernel, flag, [taken, kept], tokens, FT)


def last_frames(keys, values, tokens=()):
    def kernel(_, keys, values, out):
        out[:FT, :] = keys[FT:, :]
        out[FT:, :] = values[FT:, :]

    return small(kernel, jnp.zeros((), jnp.int32), [keys, values], tokens, 2 * FT)


def sink_steps(size):
    bits = [1 << b for b in range(1, size.bit_length() - 1)]
    orders = (bits[::-1], bits[::-1])
    done = [0, 0]
    steps = []
    for step in range(len(bits)):
        pairs = []
        for which in (0, 1):
            bit = orders[which][step]
            holders = [i for i in range(0, size, 2) if i & ~done[which] == 0]
            pairs += [(i + which, (i | bit) + which) for i in holders]
            done[which] |= bit
        steps.append(pairs)
    return steps


def project(info, parts, weight):
    columns = weight.shape[1]
    turns = 6
    block = columns // turns
    rows, depth = parts[0][0].shape
    n = len(parts)

    def kernel(info, *refs):
        weight, out = refs[n:]
        column = span(pl.program_id(0) * block, block)
        total = None
        for a, (_, place, received) in zip(refs[:n], parts):
            owner = 1 - info[1] if received else info[1]
            first = owner * (weight.shape[0] // 2) + place * depth
            product = dot(a[...], weight[span(first, depth), column])
            total = product if total is None else total + product
        out[...] = total.astype(jnp.bfloat16)

    return pl.pallas_call(
        kernel,
        grid=(turns,),
        in_specs=[SMEM_SPEC] + [VMEM_SPEC] * (n + 1),
        out_specs=pl.BlockSpec((rows, block), lambda i: (0, i)),
        out_shape=jax.ShapeDtypeStruct((rows, columns), jnp.bfloat16),
        compiler_params=PARAMS,
        cost_estimate=COST,
    )(info, *[a for a, _, _ in parts], weight)


def local(query_states, key_states, value_states, win_start, group_end, out_weight):
    axis = "tm"
    size = lax.axis_size(axis)
    paired = lax.axis_size("head") == 2
    me = lax.axis_index(axis)
    core = me % 2
    heads = query_states.shape[1] // HD
    info = jnp.concatenate(
        [
            jnp.stack([me * 2, lax.axis_index("head")]).astype(jnp.int32),
            win_start.astype(jnp.int32),
            group_end.astype(jnp.int32),
            jnp.stack([core]).astype(jnp.int32),
        ]
    )
    groups = [(0, heads // 2), (heads // 2, heads // 2)] if heads % 2 == 0 else [(0, heads)]
    rows, width = query_states.shape
    q_like = jax.ShapeDtypeStruct((rows, width), jnp.bfloat16)
    group_width = groups[0][1] * HD
    more_like = jax.ShapeDtypeStruct((rows, group_width), jnp.bfloat16)
    acc_like = jax.ShapeDtypeStruct((rows, group_width), jnp.float32)
    sums_like = jax.ShapeDtypeStruct((rows, HD), jnp.float32)
    frame_buffers = [pltpu.VMEM((2, FT, group_width), jnp.bfloat16)] * 2
    dma_sems = pltpu.SemaphoreType.DMA((2, 2))

    onward = [(i, i + 1) for i in range(size - 1)]
    near_k = lax.ppermute(key_states, axis, onward)
    moved = lax.ppermute(value_states, axis, [(0, 1)])
    held = pick(core, moved, key_states)

    def near_stage(group, state):
        return stage(
            functools.partial(near_kernel, group),
            [info, query_states, *state, near_k, near_v], 2, [acc_like, sums_like, TOKEN],
            frame_buffers + [dma_sems], NEAR_COST,
        )

    states = []
    steps = sink_steps(size)
    for step, pairs in enumerate(steps):
        moved = lax.ppermute(held, axis, pairs)
        takes = jnp.zeros((), bool)
        tokens = []
        for _, target in pairs:
            takes = takes | (me == target)
        if step < len(groups):
            *passed, more, acc, sums, token = stage(
                functools.partial(own_kernel, groups[step]),
                [info, query_states, key_states, value_states], 0,
                [q_like] * (step == 0) + [more_like, acc_like, sums_like, TOKEN], [],
                tokens=[held] * (step > 0),
            )
            states.append((more, acc, sums))
            tokens.append(token)
            if step == 0:
                near_v = lax.ppermute(passed[0], axis, onward)
                tokens.append(near_k)
            if step == len(groups) - 1:
                own_last = last_frames(key_states, value_states, [token])
                far = lax.ppermute(own_last, axis, [(i, i + 2) for i in range(0, size - 2, 2)])
        if step == len(steps) - 1:
            *sums_now, token = near_stage(groups[0], states[0])
            states[0] = states[0][0], *sums_now
            tokens += [token, far]
        held = pick(takes, moved, held, tokens)
    other = lax.ppermute(held, axis, [(i, i ^ 1) for i in range(size)])
    on_chip = [(i, i + 1) for i in range(0, size, 2)]
    relay_k = lax.ppermute(near_k, axis, on_chip)
    relay_v = lax.ppermute(near_v, axis, on_chip)

    for g, group in enumerate(groups[1:], 1):
        *sums_now, _ = near_stage(group, states[g])
        states[g] = states[g][0], *sums_now
    mine, theirs = [], []
    for g, group in enumerate(groups):
        part = jax.ShapeDtypeStruct((FT if paired else rows, group_width), jnp.bfloat16)
        results = stage(
            functools.partial(final_kernel, group),
            [info, query_states, *states[g], held, other, far, relay_k, relay_v,
             key_states, value_states, near_k, near_v], 9,
            [part] * (2 if paired else 1),
            frame_buffers + [
                pltpu.VMEM((FT, 2 * HD), jnp.float32),
                pltpu.VMEM((FT, HD), jnp.float32),
                pltpu.SMEM((group[1], 2), jnp.float32),
                dma_sems,
            ],
        )
        mine.append(results[0])
        if paired:
            theirs.append(lax.ppermute(results[1], "head", [(0, 1), (1, 0)]))
    if not paired:
        attended = jnp.concatenate(mine, axis=1)
        token_rows = lax.all_to_all(attended, "head", split_axis=0, concat_axis=1, tiled=True)
        return dot(token_rows, out_weight).astype(jnp.bfloat16)
    parts = [(array, g, False) for g, array in enumerate(mine)]
    parts += [(array, g, True) for g, array in enumerate(theirs)]
    return project(info, parts, out_weight)


def solution(mesh):
    in_specs = (P("tm", "head"), P("tm", "head"), P("tm", "head"), P("tm"), P("tm"), P())
    out_specs = P(("tm", "head"), None)
    return jax.shard_map(local, mesh=mesh, in_specs=in_specs, out_specs=out_specs, check_vma=False)
```

```python
import functools

import jax
import jax.numpy as jnp
from jax import lax
from jax.experimental import pallas as pl
from jax.experimental.pallas import tpu as pltpu
from jax.sharding import PartitionSpec as P

HD = 128
FT = 768
BK = 256
LOG2E = 1.4426950408889634
SCALE = HD ** -0.5 * LOG2E
LIMIT = 1e30
HIDDEN = 1e30
PARAMS = pltpu.CompilerParams(vmem_limit_bytes=12 * 1024 * 1024)
ANY_SPEC = pl.BlockSpec(memory_space=pl.ANY)
NEAR_COST = pl.CostEstimate(flops=8_000_000_000, bytes_accessed=1000, transcendentals=0)
COST = pl.CostEstimate(flops=1000, bytes_accessed=1000, transcendentals=0)
TOKEN = jax.ShapeDtypeStruct((8, 128), jnp.float32)


def dot(a, b):
    return jnp.dot(a, b, preferred_element_type=jnp.float32)


def span(start, size):
    return pl.ds(pl.multiple_of(start, size), size)


def rows_of(slot):
    return slice(slot * FT, (slot + 1) * FT)


def add_frame(lanes, kt, values, block):
    units = [(n, row) for n in range(len(lanes)) for row in range(0, FT, block)]

    def scores(unit):
        n, row = unit
        return dot(lanes[n][0][row : row + block, :], kt[...])

    ahead = scores(units[0])
    for at, (n, row) in enumerate(units):
        s = ahead
        if at + 1 < len(units):
            ahead = scores(units[at + 1])
        weights = jnp.exp2(s * SCALE).astype(jnp.bfloat16)
        lanes[n][1](row, dot(weights, values[...]))


def visible(info, slot, frame):
    return (frame >= 1) & (frame >= info[2 + slot]) & (frame <= info[4 + slot])


def lanes_of(h, heads):
    share = HD // heads
    lane = lax.broadcasted_iota(jnp.int32, (1, HD), 1)
    return (lane >= h * share) & (lane < (h + 1) * share)


def spread(packed, h, heads):
    row = lax.broadcasted_iota(jnp.int32, (HD, HD), 0)
    chosen = jnp.where(row == h * (HD // heads), 1.0, 0.0).astype(jnp.bfloat16)
    high = packed.astype(jnp.bfloat16)
    low = (packed - high.astype(jnp.float32)).astype(jnp.bfloat16)
    return dot(high, chosen) + dot(low, chosen)


def more_columns(own, slot):
    lane = lax.broadcasted_iota(jnp.int32, (1, HD), 1)
    flag = jnp.where(lane == 1 + slot, 1.0, 0.0)
    return jnp.where(lane == 0, -own, flag).astype(jnp.bfloat16)


def set_more_rows(kt, seen):
    row = lax.broadcasted_iota(jnp.int32, (HD, FT), 0)
    more = jnp.where(row == 0, 1.0, 0.0)
    for slot, shown in enumerate(seen):
        more = jnp.where(row == 1 + slot, jnp.where(shown, 0.0, -HIDDEN), more)
    kt[HD:, :] = more.astype(jnp.bfloat16)


def sums_into(acc_from, acc, sums, slot, column, h, heads):
    def add(row, added):
        rows = slice(slot * FT + row, slot * FT + row + added.shape[0])
        new = added[:, :HD]
        acc[rows, column] = new if acc_from is None else acc_from[rows, column] + new
        old = sums[rows, :]
        sums[rows, :] = jnp.where(lanes_of(h, heads), old + added[:, HD:], old)

    return add


def load_frame(kt, values, k, v, column):
    kt[:HD, :] = k[:, column].T
    values[:, :HD] = v[:, column]


def each_head(group, turn):
    offset, count = group

    def body(h, carry):
        turn(h, span(h * HD, HD), span((h + offset) * HD, HD))
        return carry

    lax.fori_loop(0, count, body, 0)


def own_kernel(group, info, q, k, v, *refs):
    more, acc, sums, token, kt, values = refs
    heads = group[1]
    first = info[0]
    token[...] = jnp.zeros_like(token)
    values[:, HD:] = jnp.ones((FT, HD), jnp.bfloat16)
    ones = jnp.ones((HD, HD), jnp.bfloat16)
    sums[...] = jnp.zeros_like(sums)

    def shifts(h, column, wide):
        for slot in (0, 1):
            rows = rows_of(slot)
            product = q[rows, wide].astype(jnp.float32) * k[rows, wide].astype(jnp.float32)
            more[rows, column] = more_columns(dot(product.astype(jnp.bfloat16), ones), slot)

    each_head(group, shifts)
    for frame in (0, 1):
        set_more_rows(kt, [visible(info, slot, first + frame) for slot in (0, 1)])

        def turn(h, column, wide):
            load_frame(kt, values, k.at[rows_of(frame)], v.at[rows_of(frame)], wide)
            lanes = []
            for slot in (0, 1):
                rows = rows_of(slot)
                add = sums_into(acc if frame else None, acc, sums, slot, column, h, heads)
                queries = jnp.concatenate([q[rows, wide], more[rows, column]], axis=1)
                lanes.append((queries, add))
            add_frame(lanes, kt, values, 768)

        each_head(group, turn)


def near_kernel(group, info, q, more, acc_in, sums_in, near_k, near_v, *refs):
    acc, sums, token, kt, values, k_buf, v_buf, sem = refs
    offset, heads = group
    token[...] = jnp.zeros_like(token)
    first = info[0]
    order = (1, 0)
    copies = {
        frame: [
            pltpu.make_async_copy(
                source.at[pl.ds(frame * FT, FT), pl.ds(offset * HD, heads * HD)],
                buf.at[frame],
                sem.at[frame, n],
            )
            for n, (source, buf) in enumerate(((near_k, k_buf), (near_v, v_buf)))
        ]
        for frame in order
    }
    for frame in order:
        for copy in copies[frame]:
            copy.start()
    values[:, HD:] = jnp.ones((FT, HD), jnp.bfloat16)
    sums[...] = sums_in[...]
    for frame in order:
        set_more_rows(kt, [visible(info, slot, first - 2 + frame) for slot in (0, 1)])
        for copy in copies[frame]:
            copy.wait()

        def turn(h, column, wide):
            load_frame(kt, values, k_buf.at[frame], v_buf.at[frame], column)
            acc_from = acc_in if frame == order[0] else acc
            lanes = []
            for slot in (0, 1):
                rows = rows_of(slot)
                add = sums_into(acc_from, acc, sums, slot, column, h, heads)
                queries = jnp.concatenate([q[rows, wide], more[rows, column]], axis=1)
                lanes.append((queries, add))
            add_frame(lanes, kt, values, 384)

        each_head(group, turn)


def final_kernel(
    group, info, q, more, acc_in, sums_in,
    sink_a, sink_b, far, relay_k, relay_v, key_any, value_any, near_k, near_v, *refs,
):
    outs = refs[:-9]
    kt, values, k_buf, v_buf, results, acc, shift, too_large, sem = refs[-9:]
    first = info[0]
    core = info[6]
    far_seen = visible(info, 0, first - 3)
    offset, heads = group
    group_columns = pl.ds(offset * HD, heads * HD)
    values[:, HD:] = jnp.ones((FT, HD), jnp.bfloat16)

    def copies(frame, k, k_row, v, v_row, columns):
        return [
            pltpu.make_async_copy(
                source.at[pl.ds(row, FT), columns], buf.at[frame], sem.at[frame, n]
            )
            for n, (source, row, buf) in enumerate(((k, k_row, k_buf), (v, v_row, v_buf)))
        ]

    arriving = {
        0: [
            (0, sink_a, 0, sink_b, 0, group_columns),
            (1, far, 0, far, FT, group_columns),
        ],
        1: [
            (0, sink_b, 0, sink_a, 0, group_columns),
            (1, relay_k, FT, relay_v, FT, group_columns),
        ],
    }
    for which, listed in arriving.items():

        @pl.when(core == which)
        def _():
            started = [copies(*entry) for entry in listed]
            for act in (lambda copy: copy.start(), lambda copy: copy.wait()):
                for pair in started:
                    for copy in pair:
                        act(copy)

    def write(slot, h, acc, total):
        attended = (acc / total).astype(jnp.bfloat16)
        column = span(h * HD, HD)
        if len(outs) == 1:
            outs[0][rows_of(slot), column] = attended
        else:

            @pl.when(info[1] == slot)
            def _():
                outs[0][:, column] = attended

            @pl.when(info[1] != slot)
            def _():
                outs[1][:, column] = attended

    def turn(h, column, wide):
        def into(ref, slot, old=None):
            def add(row, added):
                rows = slice(slot * FT + row, slot * FT + row + added.shape[0])
                ref[rows, :] = added if old is None else old[rows, :] + added

            return add

        queries = [
            jnp.concatenate([q[rows_of(slot), wide], more[rows_of(slot), column]], axis=1)
            for slot in (0, 1)
        ]
        load_frame(kt, values, k_buf.at[0], v_buf.at[0], column)
        set_more_rows(kt, [True, True])
        add_frame([(queries[slot], into(results, slot)) for slot in (1, 0)], kt, values, 256)
        load_frame(kt, values, k_buf.at[1], v_buf.at[1], column)
        set_more_rows(kt, [far_seen, False])
        add_frame([(queries[0], into(results, 0, results))], kt, values, 256)
        for slot in (0, 1):
            rows = rows_of(slot)
            total = spread(sums_in[rows, :], h, heads) + results[rows, HD:]
            write(slot, h, acc_in[rows, column] + results[rows, :HD], total)
            too_large[h, slot] = jnp.max(jnp.where(total < LIMIT, 0.0, 1.0))

    each_head(group, turn)

    def again(slot, h, wide):
        here, there = core == 0, core == 1
        sources = [(here, sink_a, 0, sink_b, 0), (there, sink_b, 0, sink_a, 0)]
        if slot == 0:
            sources += [
                (far_seen & here, far, 0, far, FT), (far_seen & there, relay_k, FT, relay_v, FT)
            ]
        for frame in (0, 1):
            row = frame * FT
            own = visible(info, slot, first + frame)
            sources.append((own, key_any, row, value_any, row))
            behind = visible(info, slot, first - 2 + frame)
            sources.append((behind, near_k, row, near_v, row))
        one = (k_buf.at[0, :, :HD], v_buf.at[0, :, :HD])

        def sweep(step):
            def visit(t, carry):
                seen = False
                for n, (shown, k, k_row, v, v_row) in enumerate(sources):
                    chosen = (t == n) & shown
                    seen = seen | chosen

                    @pl.when(chosen)
                    def _():
                        for n, (ref, row) in enumerate(((k, k_row), (v, v_row))):
                            copy = pltpu.make_async_copy(
                                ref.at[pl.ds(row, FT), wide], one[n], sem.at[0, n]
                            )
                            copy.start()
                            copy.wait()

                @pl.when(seen)
                def _():
                    load_frame(kt, values, k_buf.at[0], v_buf.at[0], slice(0, HD))
                    step()

                return carry

            lax.fori_loop(0, len(sources), visit, 0)

        queries = q[rows_of(slot), wide]

        def scores(j):
            return dot(queries, kt[:HD, j * BK : (j + 1) * BK]) * SCALE

        def peak():
            for j in range(FT // BK):
                shift[...] = jnp.maximum(shift[...], jnp.max(scores(j), axis=1, keepdims=True))

        def more_sums():
            for j in range(FT // BK):
                s = scores(j)
                weights = jnp.concatenate(
                    [jnp.exp2(s[:, c : c + HD] - shift[...]) for c in range(0, BK, HD)], axis=1
                )
                keys = values[j * BK : (j + 1) * BK, :]
                acc[...] = acc[...] + dot(weights.astype(jnp.bfloat16), keys)

        shift[...] = jnp.full((FT, HD), -jnp.inf, jnp.float32)
        acc[...] = jnp.zeros((FT, 2 * HD), jnp.float32)
        sweep(peak)
        sweep(more_sums)
        write(slot, h, acc[:, :HD], acc[:, HD:])

    def check(h, column, wide):
        for slot in (0, 1):
            pl.when(too_large[h, slot] > 0.0)(lambda slot=slot: again(slot, h, wide))

    each_head(group, check)


VMEM_SPEC = pl.BlockSpec(memory_space=pltpu.VMEM)
SMEM_SPEC = pl.BlockSpec(memory_space=pltpu.SMEM)


def stage(kernel, arrays, in_any, outs, scratch, cost=None, tokens=()):
    n = len(arrays)

    def run(*refs):
        kernel(*refs[:n], *refs[n + len(tokens) :])

    return pl.pallas_call(
        run,
        in_specs=[SMEM_SPEC] + [VMEM_SPEC] * (n - in_any - 1)
        + [ANY_SPEC] * (in_any + len(tokens)),
        out_specs=[VMEM_SPEC] * len(outs),
        scratch_shapes=[
            pltpu.VMEM((2 * HD, FT), jnp.bfloat16), pltpu.VMEM((FT, 2 * HD), jnp.bfloat16)
        ] + list(scratch),
        out_shape=outs,
        compiler_params=PARAMS,
        cost_estimate=cost or COST,
    )(*arrays, *tokens)


def small(kernel, scalars, arrays, tokens, rows):
    width = arrays[0].shape[1]
    n = len(arrays)

    def run(scalars, *refs):
        kernel(scalars, *refs[:n], refs[-1])

    return pl.pallas_call(
        run,
        in_specs=[SMEM_SPEC] + [VMEM_SPEC] * n + [ANY_SPEC] * len(tokens),
        out_specs=VMEM_SPEC,
        out_shape=jax.ShapeDtypeStruct((rows, width), jnp.bfloat16),
        compiler_params=PARAMS,
        cost_estimate=COST,
    )(jnp.reshape(scalars, (1,)).astype(jnp.int32), *arrays, *tokens)


def pick(flag, taken, kept, tokens=()):
    width = kept.shape[1]

    def kernel(flag, taken, kept, *refs):
        out, sem = refs[-2:]
        for value, source in ((1, taken), (0, kept)):

            @pl.when(flag[0] == value)
            def _():
                copy = pltpu.make_async_copy(source.at[pl.ds(0, FT)], out, sem)
                copy.start()
                copy.wait()

    return pl.pallas_call(
        kernel,
        in_specs=[SMEM_SPEC] + [ANY_SPEC] * (2 + len(tokens)),
        out_specs=VMEM_SPEC,
        out_shape=jax.ShapeDtypeStruct((FT, width), jnp.bfloat16),
        scratch_shapes=[pltpu.SemaphoreType.DMA],
        compiler_params=PARAMS,
        cost_estimate=COST,
    )(jnp.reshape(flag, (1,)).astype(jnp.int32), taken, kept, *tokens)


def last_frames(keys, values, tokens=()):
    def kernel(_, keys, values, out):
        out[:FT, :] = keys[FT:, :]
        out[FT:, :] = values[FT:, :]

    return small(kernel, jnp.zeros((), jnp.int32), [keys, values], tokens, 2 * FT)


def sink_steps(size):
    bits = [1 << b for b in range(1, size.bit_length() - 1)]
    orders = (bits[::-1], bits[::-1])
    done = [0, 0]
    steps = []
    for step in range(len(bits)):
        pairs = []
        for which in (0, 1):
            bit = orders[which][step]
            holders = [i for i in range(0, size, 2) if i & ~done[which] == 0]
            pairs += [(i + which, (i | bit) + which) for i in holders]
            done[which] |= bit
        steps.append(pairs)
    return steps


def project(info, parts, weight):
    columns = weight.shape[1]
    turns = 6
    block = columns // turns
    rows, depth = parts[0][0].shape
    n = len(parts)

    def kernel(info, *refs):
        weight, out = refs[n:]
        column = span(pl.program_id(0) * block, block)
        total = None
        for a, (_, place, received) in zip(refs[:n], parts):
            owner = 1 - info[1] if received else info[1]
            first = owner * (weight.shape[0] // 2) + place * depth
            product = dot(a[...], weight[span(first, depth), column])
            total = product if total is None else total + product
        out[...] = total.astype(jnp.bfloat16)

    return pl.pallas_call(
        kernel,
        grid=(turns,),
        in_specs=[SMEM_SPEC] + [VMEM_SPEC] * (n + 1),
        out_specs=pl.BlockSpec((rows, block), lambda i: (0, i)),
        out_shape=jax.ShapeDtypeStruct((rows, columns), jnp.bfloat16),
        compiler_params=PARAMS,
        cost_estimate=COST,
    )(info, *[a for a, _, _ in parts], weight)


def local(query_states, key_states, value_states, win_start, group_end, out_weight):
    axis = "tm"
    size = lax.axis_size(axis)
    paired = lax.axis_size("head") == 2
    me = lax.axis_index(axis)
    core = me % 2
    heads = query_states.shape[1] // HD
    info = jnp.concatenate(
        [
            jnp.stack([me * 2, lax.axis_index("head")]).astype(jnp.int32),
            win_start.astype(jnp.int32),
            group_end.astype(jnp.int32),
            jnp.stack([core]).astype(jnp.int32),
        ]
    )
    groups = [(0, heads // 2), (heads // 2, heads // 2)] if heads % 2 == 0 else [(0, heads)]
    rows = query_states.shape[0]
    group_width = groups[0][1] * HD
    more_like = jax.ShapeDtypeStruct((rows, group_width), jnp.bfloat16)
    acc_like = jax.ShapeDtypeStruct((rows, group_width), jnp.float32)
    sums_like = jax.ShapeDtypeStruct((rows, HD), jnp.float32)
    frame_buffers = [pltpu.VMEM((2, FT, group_width), jnp.bfloat16)] * 2
    dma_sems = pltpu.SemaphoreType.DMA((2, 2))

    onward = [(i, i + 1) for i in range(size - 1)]
    near_k = lax.ppermute(key_states, axis, onward)
    near_v = lax.ppermute(value_states, axis, onward)
    moved = lax.ppermute(value_states, axis, [(0, 1)])
    held = pick(core, moved, key_states)

    def near_stage(group, state):
        return stage(
            functools.partial(near_kernel, group),
            [info, query_states, *state, near_k, near_v], 2, [acc_like, sums_like, TOKEN],
            frame_buffers + [dma_sems], NEAR_COST,
        )

    states = []
    steps = sink_steps(size)
    for step, pairs in enumerate(steps):
        moved = lax.ppermute(held, axis, pairs)
        takes = jnp.zeros((), bool)
        tokens = []
        for _, target in pairs:
            takes = takes | (me == target)
        if step < len(groups):
            more, acc, sums, token = stage(
                functools.partial(own_kernel, groups[step]),
                [info, query_states, key_states, value_states], 0,
                [more_like, acc_like, sums_like, TOKEN], [],
                tokens=[held] * (step > 0),
            )
            states.append((more, acc, sums))
            tokens.append(token)
            if step == 1:
                tokens += [near_k, near_v]
            if step == len(groups) - 1:
                own_last = last_frames(key_states, value_states, [token])
                far = lax.ppermute(own_last, axis, [(i, i + 2) for i in range(0, size - 2, 2)])
        if step == len(steps) - 1:
            *sums_now, token = near_stage(groups[0], states[0])
            states[0] = states[0][0], *sums_now
            tokens += [token, far]
        held = pick(takes, moved, held, tokens)
    other = lax.ppermute(held, axis, [(i, i ^ 1) for i in range(size)])
    on_chip = [(i, i + 1) for i in range(0, size, 2)]
    relay_k = lax.ppermute(near_k, axis, on_chip)
    relay_v = lax.ppermute(near_v, axis, on_chip)

    for g, group in enumerate(groups[1:], 1):
        *sums_now, _ = near_stage(group, states[g])
        states[g] = states[g][0], *sums_now
    mine, theirs = [], []
    for g, group in enumerate(groups):
        part = jax.ShapeDtypeStruct((FT if paired else rows, group_width), jnp.bfloat16)
        results = stage(
            functools.partial(final_kernel, group),
            [info, query_states, *states[g], held, other, far, relay_k, relay_v,
             key_states, value_states, near_k, near_v], 9,
            [part] * (2 if paired else 1),
            frame_buffers + [
                pltpu.VMEM((rows, 2 * HD), jnp.float32),
                pltpu.VMEM((FT, 2 * HD), jnp.float32),
                pltpu.VMEM((FT, HD), jnp.float32),
                pltpu.SMEM((group[1], 2), jnp.float32),
                dma_sems,
            ],
        )
        mine.append(results[0])
        if paired:
            theirs.append(lax.ppermute(results[1], "head", [(0, 1), (1, 0)]))
    if not paired:
        attended = jnp.concatenate(mine, axis=1)
        token_rows = lax.all_to_all(attended, "head", split_axis=0, concat_axis=1, tiled=True)
        return dot(token_rows, out_weight).astype(jnp.bfloat16)
    parts = [(array, g, False) for g, array in enumerate(mine)]
    parts += [(array, g, True) for g, array in enumerate(theirs)]
    return project(info, parts, out_weight)


def solution(mesh):
    in_specs = (P("tm", "head"), P("tm", "head"), P("tm", "head"), P("tm"), P("tm"), P())
    out_specs = P(("tm", "head"), None)
    return jax.shard_map(local, mesh=mesh, in_specs=in_specs, out_specs=out_specs, check_vma=False)
```

```python
import functools

import jax
import jax.numpy as jnp
from jax import lax
from jax.experimental import pallas as pl
from jax.experimental.pallas import tpu as pltpu
from jax.sharding import PartitionSpec as P

HD = 128
FT = 768
BK = 256
LOG2E = 1.4426950408889634
SCALE = HD ** -0.5 * LOG2E
LIMIT = 1e30
HIDDEN = 1e30
PARAMS = pltpu.CompilerParams(vmem_limit_bytes=12 * 1024 * 1024)
ANY_SPEC = pl.BlockSpec(memory_space=pl.ANY)
NEAR_COST = pl.CostEstimate(flops=8_000_000_000, bytes_accessed=1000, transcendentals=0)
COST = pl.CostEstimate(flops=1000, bytes_accessed=1000, transcendentals=0)
TOKEN = jax.ShapeDtypeStruct((8, 128), jnp.float32)


def dot(a, b):
    return jnp.dot(a, b, preferred_element_type=jnp.float32)


def span(start, size):
    return pl.ds(pl.multiple_of(start, size), size)


def rows_of(slot):
    return slice(slot * FT, (slot + 1) * FT)


def add_frame(lanes, kt, values, block):
    units = [(n, row) for n in range(len(lanes)) for row in range(0, FT, block)]

    def scores(unit):
        n, row = unit
        return dot(lanes[n][0][row : row + block, :], kt[...])

    ahead = scores(units[0])
    for at, (n, row) in enumerate(units):
        s = ahead
        if at + 1 < len(units):
            ahead = scores(units[at + 1])
        weights = jnp.exp2(s * SCALE).astype(jnp.bfloat16)
        lanes[n][1](row, dot(weights, values[...]))


def visible(info, slot, frame):
    return (frame >= 1) & (frame >= info[2 + slot]) & (frame <= info[4 + slot])


def lanes_of(h, heads):
    share = HD // heads
    lane = lax.broadcasted_iota(jnp.int32, (1, HD), 1)
    return (lane >= h * share) & (lane < (h + 1) * share)


def spread(packed, h, heads):
    row = lax.broadcasted_iota(jnp.int32, (HD, HD), 0)
    chosen = jnp.where(row == h * (HD // heads), 1.0, 0.0).astype(jnp.bfloat16)
    high = packed.astype(jnp.bfloat16)
    low = (packed - high.astype(jnp.float32)).astype(jnp.bfloat16)
    return dot(high, chosen) + dot(low, chosen)


def more_columns(own, slot):
    lane = lax.broadcasted_iota(jnp.int32, (1, HD), 1)
    flag = jnp.where(lane == 1 + slot, 1.0, 0.0)
    return jnp.where(lane == 0, -own, flag).astype(jnp.bfloat16)


def set_more_rows(kt, seen):
    row = lax.broadcasted_iota(jnp.int32, (HD, FT), 0)
    more = jnp.where(row == 0, 1.0, 0.0)
    for slot, shown in enumerate(seen):
        more = jnp.where(row == 1 + slot, jnp.where(shown, 0.0, -HIDDEN), more)
    kt[HD:, :] = more.astype(jnp.bfloat16)


def sums_into(acc_from, acc, sums, slot, column, h, heads):
    def add(row, added):
        rows = slice(slot * FT + row, slot * FT + row + added.shape[0])
        new = added[:, :HD]
        acc[rows, column] = new if acc_from is None else acc_from[rows, column] + new
        old = sums[rows, :]
        sums[rows, :] = jnp.where(lanes_of(h, heads), old + added[:, HD:], old)

    return add


def load_frame(kt, values, k, v, column):
    kt[:HD, :] = k[:, column].T
    values[:, :HD] = v[:, column]


def each_head(group, turn):
    offset, count = group

    def body(h, carry):
        turn(h, span(h * HD, HD), span((h + offset) * HD, HD))
        return carry

    lax.fori_loop(0, count, body, 0)


def own_kernel(group, info, q, k, v, *refs):
    more, acc, sums, token, kt, values = refs
    heads = group[1]
    first = info[0]
    token[...] = jnp.zeros_like(token)
    values[:, HD:] = jnp.ones((FT, HD), jnp.bfloat16)
    ones = jnp.ones((HD, HD), jnp.bfloat16)
    sums[...] = jnp.zeros_like(sums)

    def shifts(h, column, wide):
        for slot in (0, 1):
            rows = rows_of(slot)
            product = q[rows, wide].astype(jnp.float32) * k[rows, wide].astype(jnp.float32)
            more[rows, column] = more_columns(dot(product.astype(jnp.bfloat16), ones), slot)

    each_head(group, shifts)
    for frame in (0, 1):
        set_more_rows(kt, [visible(info, slot, first + frame) for slot in (0, 1)])

        def turn(h, column, wide):
            load_frame(kt, values, k.at[rows_of(frame)], v.at[rows_of(frame)], wide)
            lanes = []
            for slot in (0, 1):
                rows = rows_of(slot)
                add = sums_into(acc if frame else None, acc, sums, slot, column, h, heads)
                queries = jnp.concatenate([q[rows, wide], more[rows, column]], axis=1)
                lanes.append((queries, add))
            add_frame(lanes, kt, values, 256)

        each_head(group, turn)


def near_kernel(group, info, q, more, acc_in, sums_in, near_k, near_v, *refs):
    acc, sums, token, kt, values, k_buf, v_buf, sem = refs
    offset, heads = group
    token[...] = jnp.zeros_like(token)
    first = info[0]
    order = (1, 0)
    copies = {
        frame: [
            pltpu.make_async_copy(
                source.at[pl.ds(frame * FT, FT), pl.ds(offset * HD, heads * HD)],
                buf.at[frame],
                sem.at[frame, n],
            )
            for n, (source, buf) in enumerate(((near_k, k_buf), (near_v, v_buf)))
        ]
        for frame in order
    }
    for frame in order:
        for copy in copies[frame]:
            copy.start()
    values[:, HD:] = jnp.ones((FT, HD), jnp.bfloat16)
    sums[...] = sums_in[...]
    for frame in order:
        set_more_rows(kt, [visible(info, slot, first - 2 + frame) for slot in (0, 1)])
        for copy in copies[frame]:
            copy.wait()

        def turn(h, column, wide):
            load_frame(kt, values, k_buf.at[frame], v_buf.at[frame], column)
            acc_from = acc_in if frame == order[0] else acc
            lanes = []
            for slot in (0, 1):
                rows = rows_of(slot)
                add = sums_into(acc_from, acc, sums, slot, column, h, heads)
                queries = jnp.concatenate([q[rows, wide], more[rows, column]], axis=1)
                lanes.append((queries, add))
            add_frame(lanes, kt, values, 256)

        each_head(group, turn)


def final_kernel(
    group, info, q, more, acc_in, sums_in,
    sink_a, sink_b, far, relay_k, relay_v, key_any, value_any, near_k, near_v, *refs,
):
    outs = refs[:-9]
    kt, values, k_buf, v_buf, results, acc, shift, too_large, sem = refs[-9:]
    first = info[0]
    core = info[6]
    far_seen = visible(info, 0, first - 3)
    offset, heads = group
    group_columns = pl.ds(offset * HD, heads * HD)
    values[:, HD:] = jnp.ones((FT, HD), jnp.bfloat16)

    own_columns = pl.ds(0, heads * HD)

    def copies(frame, k, k_row, v, v_row, columns):
        return [
            pltpu.make_async_copy(
                source.at[pl.ds(row, FT), columns], buf.at[frame], sem.at[frame, n]
            )
            for n, (source, row, buf) in enumerate(((k, k_row, k_buf), (v, v_row, v_buf)))
        ]

    arriving = {
        0: [
            (0, sink_a, 0, sink_b, 0, own_columns),
            (1, far, 0, far, FT, own_columns),
        ],
        1: [
            (0, sink_b, 0, sink_a, 0, own_columns),
            (1, relay_k, FT, relay_v, FT, group_columns),
        ],
    }
    for which, listed in arriving.items():

        @pl.when(core == which)
        def _():
            started = [copies(*entry) for entry in listed]
            for act in (lambda copy: copy.start(), lambda copy: copy.wait()):
                for pair in started:
                    for copy in pair:
                        act(copy)

    def write(slot, h, acc, total):
        attended = (acc / total).astype(jnp.bfloat16)
        column = span(h * HD, HD)
        if len(outs) == 1:
            outs[0][rows_of(slot), column] = attended
        else:

            @pl.when(info[1] == slot)
            def _():
                outs[0][:, column] = attended

            @pl.when(info[1] != slot)
            def _():
                outs[1][:, column] = attended

    def turn(h, column, wide):
        def into(ref, slot, old=None):
            def add(row, added):
                rows = slice(slot * FT + row, slot * FT + row + added.shape[0])
                ref[rows, :] = added if old is None else old[rows, :] + added

            return add

        queries = [
            jnp.concatenate([q[rows_of(slot), wide], more[rows_of(slot), column]], axis=1)
            for slot in (0, 1)
        ]
        load_frame(kt, values, k_buf.at[0], v_buf.at[0], column)
        set_more_rows(kt, [True, True])
        add_frame([(queries[slot], into(results, slot)) for slot in (1, 0)], kt, values, 256)
        load_frame(kt, values, k_buf.at[1], v_buf.at[1], column)
        set_more_rows(kt, [far_seen, False])
        add_frame([(queries[0], into(results, 0, results))], kt, values, 256)
        for slot in (0, 1):
            rows = rows_of(slot)
            total = spread(sums_in[rows, :], h, heads) + results[rows, HD:]
            write(slot, h, acc_in[rows, column] + results[rows, :HD], total)
            too_large[h, slot] = jnp.max(jnp.where(total < LIMIT, 0.0, 1.0))

    each_head(group, turn)

    def again(slot, h, column, wide):
        here, there = core == 0, core == 1
        sources = [
            (here, sink_a, 0, sink_b, 0, column), (there, sink_b, 0, sink_a, 0, column)
        ]
        if slot == 0:
            sources += [
                (far_seen & here, far, 0, far, FT, column),
                (far_seen & there, relay_k, FT, relay_v, FT, wide),
            ]
        for frame in (0, 1):
            row = frame * FT
            own = visible(info, slot, first + frame)
            sources.append((own, key_any, row, value_any, row, wide))
            behind = visible(info, slot, first - 2 + frame)
            sources.append((behind, near_k, row, near_v, row, wide))
        one = (k_buf.at[0, :, :HD], v_buf.at[0, :, :HD])

        def sweep(step):
            def visit(t, carry):
                seen = False
                for n, (shown, k, k_row, v, v_row, where) in enumerate(sources):
                    chosen = (t == n) & shown
                    seen = seen | chosen

                    @pl.when(chosen)
                    def _():
                        for n, (ref, row) in enumerate(((k, k_row), (v, v_row))):
                            copy = pltpu.make_async_copy(
                                ref.at[pl.ds(row, FT), where], one[n], sem.at[0, n]
                            )
                            copy.start()
                            copy.wait()

                @pl.when(seen)
                def _():
                    load_frame(kt, values, k_buf.at[0], v_buf.at[0], slice(0, HD))
                    step()

                return carry

            lax.fori_loop(0, len(sources), visit, 0)

        queries = q[rows_of(slot), wide]

        def scores(j):
            return dot(queries, kt[:HD, j * BK : (j + 1) * BK]) * SCALE

        def peak():
            for j in range(FT // BK):
                shift[...] = jnp.maximum(shift[...], jnp.max(scores(j), axis=1, keepdims=True))

        def more_sums():
            for j in range(FT // BK):
                s = scores(j)
                weights = jnp.concatenate(
                    [jnp.exp2(s[:, c : c + HD] - shift[...]) for c in range(0, BK, HD)], axis=1
                )
                keys = values[j * BK : (j + 1) * BK, :]
                acc[...] = acc[...] + dot(weights.astype(jnp.bfloat16), keys)

        shift[...] = jnp.full((FT, HD), -jnp.inf, jnp.float32)
        acc[...] = jnp.zeros((FT, 2 * HD), jnp.float32)
        sweep(peak)
        sweep(more_sums)
        write(slot, h, acc[:, :HD], acc[:, HD:])

    def check(h, column, wide):
        for slot in (0, 1):
            pl.when(too_large[h, slot] > 0.0)(lambda slot=slot: again(slot, h, column, wide))

    each_head(group, check)


VMEM_SPEC = pl.BlockSpec(memory_space=pltpu.VMEM)
SMEM_SPEC = pl.BlockSpec(memory_space=pltpu.SMEM)


def stage(kernel, arrays, in_any, outs, scratch, cost=None, tokens=()):
    n = len(arrays)

    def run(*refs):
        kernel(*refs[:n], *refs[n + len(tokens) :])

    return pl.pallas_call(
        run,
        in_specs=[SMEM_SPEC] + [VMEM_SPEC] * (n - in_any - 1)
        + [ANY_SPEC] * (in_any + len(tokens)),
        out_specs=[VMEM_SPEC] * len(outs),
        scratch_shapes=[
            pltpu.VMEM((2 * HD, FT), jnp.bfloat16), pltpu.VMEM((FT, 2 * HD), jnp.bfloat16)
        ] + list(scratch),
        out_shape=outs,
        compiler_params=PARAMS,
        cost_estimate=cost or COST,
    )(*arrays, *tokens)


def pick(flag, taken, kept, tokens=(), columns=None):
    column, width = columns or (0, kept.shape[1])

    def kernel(flag, taken, kept, *refs):
        out, sem = refs[-2:]
        for value, source in ((1, taken), (0, kept)):

            @pl.when(flag[0] == value)
            def _():
                rows = source.at[pl.ds(0, FT), pl.ds(column, width)]
                copy = pltpu.make_async_copy(rows, out, sem)
                copy.start()
                copy.wait()

    return pl.pallas_call(
        kernel,
        in_specs=[SMEM_SPEC] + [ANY_SPEC] * (2 + len(tokens)),
        out_specs=VMEM_SPEC,
        out_shape=jax.ShapeDtypeStruct((FT, width), jnp.bfloat16),
        scratch_shapes=[pltpu.SemaphoreType.DMA],
        compiler_params=PARAMS,
        cost_estimate=COST,
    )(jnp.reshape(flag, (1,)).astype(jnp.int32), taken, kept, *tokens)


def last_frames(group, keys, values, tokens=()):
    columns = pl.ds(group[0] * HD, group[1] * HD)
    n = len(tokens)

    def kernel(keys, values, *refs):
        out, sem = refs[n:]
        started = [
            pltpu.make_async_copy(
                source.at[pl.ds(FT, FT), columns], out.at[pl.ds(i * FT, FT)], sem.at[i]
            )
            for i, source in enumerate((keys, values))
        ]
        for copy in started:
            copy.start()
        for copy in started:
            copy.wait()

    return pl.pallas_call(
        kernel,
        in_specs=[ANY_SPEC] * (2 + n),
        out_specs=VMEM_SPEC,
        out_shape=jax.ShapeDtypeStruct((2 * FT, group[1] * HD), jnp.bfloat16),
        scratch_shapes=[pltpu.SemaphoreType.DMA((2,))],
        compiler_params=PARAMS,
        cost_estimate=COST,
    )(keys, values, *tokens)


def sink_steps(size):
    bits = [1 << b for b in range(1, size.bit_length() - 1)]
    orders = (bits[::-1], bits[::-1])
    done = [0, 0]
    steps = []
    for step in range(len(bits)):
        pairs = []
        for which in (0, 1):
            bit = orders[which][step]
            holders = [i for i in range(0, size, 2) if i & ~done[which] == 0]
            pairs += [(i + which, (i | bit) + which) for i in holders]
            done[which] |= bit
        steps.append(pairs)
    return steps


def project(info, parts, weight):
    columns = weight.shape[1]
    turns = 6
    block = columns // turns
    rows, depth = parts[0][0].shape
    n = len(parts)

    def kernel(info, *refs):
        weight, out = refs[n:]
        column = span(pl.program_id(0) * block, block)
        total = None
        for a, (_, place, received) in zip(refs[:n], parts):
            owner = 1 - info[1] if received else info[1]
            first = owner * (weight.shape[0] // 2) + place * depth
            product = dot(a[...], weight[span(first, depth), column])
            total = product if total is None else total + product
        out[...] = total.astype(jnp.bfloat16)

    return pl.pallas_call(
        kernel,
        grid=(turns,),
        in_specs=[SMEM_SPEC] + [VMEM_SPEC] * (n + 1),
        out_specs=pl.BlockSpec((rows, block), lambda i: (0, i)),
        out_shape=jax.ShapeDtypeStruct((rows, columns), jnp.bfloat16),
        compiler_params=PARAMS,
        cost_estimate=COST,
    )(info, *[a for a, _, _ in parts], weight)


def local(query_states, key_states, value_states, win_start, group_end, out_weight):
    axis = "tm"
    size = lax.axis_size(axis)
    paired = lax.axis_size("head") == 2
    me = lax.axis_index(axis)
    core = me % 2
    heads = query_states.shape[1] // HD
    info = jnp.concatenate(
        [
            jnp.stack([me * 2, lax.axis_index("head")]).astype(jnp.int32),
            win_start.astype(jnp.int32),
            group_end.astype(jnp.int32),
            jnp.stack([core]).astype(jnp.int32),
        ]
    )
    groups = [(0, heads // 2), (heads // 2, heads // 2)] if heads % 2 == 0 else [(0, heads)]
    rows = query_states.shape[0]
    group_width = groups[0][1] * HD
    more_like = jax.ShapeDtypeStruct((rows, group_width), jnp.bfloat16)
    acc_like = jax.ShapeDtypeStruct((rows, group_width), jnp.float32)
    sums_like = jax.ShapeDtypeStruct((rows, HD), jnp.float32)
    frame_buffers = [pltpu.VMEM((2, FT, group_width), jnp.bfloat16)] * 2
    dma_sems = pltpu.SemaphoreType.DMA((2, 2))

    onward = [(i, i + 1) for i in range(size - 1)]
    near_k = lax.ppermute(key_states, axis, onward)
    near_v = lax.ppermute(value_states, axis, onward)
    moved = lax.ppermute(value_states, axis, [(0, 1)])
    held = pick(core, moved, key_states)

    def near_stage(group, state):
        return stage(
            functools.partial(near_kernel, group),
            [info, query_states, *state, near_k, near_v], 2, [acc_like, sums_like, TOKEN],
            frame_buffers + [dma_sems], NEAR_COST,
        )

    def flag_of(pairs):
        takes = jnp.zeros((), bool)
        for _, target in pairs:
            takes = takes | (me == target)
        return takes

    states = []
    *steps, last_step = sink_steps(size)
    for step, pairs in enumerate(steps):
        moved = lax.ppermute(held, axis, pairs)
        tokens = []
        if step < len(groups):
            *state, token = stage(
                functools.partial(own_kernel, groups[step]),
                [info, query_states, key_states, value_states], 0,
                [more_like, acc_like, sums_like, TOKEN], [], tokens=[held] * (step > 0),
            )
            states.append(state)
            tokens.append(token)
        if step < len(steps) - 1:
            held = pick(flag_of(pairs), moved, held, tokens)

    on_chip = [(i, i + 1) for i in range(0, size, 2)]
    relay_k = lax.ppermute(near_k, axis, on_chip)
    relay_v = lax.ppermute(near_v, axis, on_chip)
    own_done, arrivals = tokens, [near_k, near_v]
    mine, theirs = [], []
    for g, group in enumerate(groups):
        columns = group[0] * HD, group[1] * HD
        own_last = last_frames(group, key_states, value_states, own_done)
        far = lax.ppermute(own_last, axis, [(i, i + 2) for i in range(0, size - 2, 2)])
        part = pick(flag_of(steps[-1]), moved, held, own_done + arrivals, columns)
        arriving = lax.ppermute(part, axis, last_step)
        more = states[g][0]
        *sums_now, token = near_stage(group, states[g])
        states[g] = more, *sums_now
        part = pick(flag_of(last_step), arriving, part, [token, far] + mine)
        own_done, arrivals = [part], []
        other = lax.ppermute(part, axis, [(i, i ^ 1) for i in range(size)])
        out = jax.ShapeDtypeStruct((FT if paired else rows, group_width), jnp.bfloat16)
        results = stage(
            functools.partial(final_kernel, group),
            [info, query_states, *states[g], part, other, far, relay_k, relay_v,
             key_states, value_states, near_k, near_v], 9,
            [out] * (2 if paired else 1),
            frame_buffers + [
                pltpu.VMEM((rows, 2 * HD), jnp.float32),
                pltpu.VMEM((FT, 2 * HD), jnp.float32),
                pltpu.VMEM((FT, HD), jnp.float32),
                pltpu.SMEM((group[1], 2), jnp.float32),
                dma_sems,
            ],
        )
        mine.append(results[0])
        if paired:
            theirs.append(lax.ppermute(results[1], "head", [(0, 1), (1, 0)]))
    if not paired:
        attended = jnp.concatenate(mine, axis=1)
        token_rows = lax.all_to_all(attended, "head", split_axis=0, concat_axis=1, tiled=True)
        return dot(token_rows, out_weight).astype(jnp.bfloat16)
    parts = [(array, g, False) for g, array in enumerate(mine)]
    parts += [(array, g, True) for g, array in enumerate(theirs)]
    return project(info, parts, out_weight)


def solution(mesh):
    in_specs = (P("tm", "head"), P("tm", "head"), P("tm", "head"), P("tm"), P("tm"), P())
    out_specs = P(("tm", "head"), None)
    return jax.shard_map(local, mesh=mesh, in_specs=in_specs, out_specs=out_specs, check_vma=False)
```

```python
import functools

import jax
import jax.numpy as jnp
from jax import lax
from jax.experimental import pallas as pl
from jax.experimental.pallas import tpu as pltpu
from jax.sharding import PartitionSpec as P

HD = 128
FT = 768
BK = 256
LOG2E = 1.4426950408889634
SCALE = HD ** -0.5 * LOG2E
LIMIT = 1e30
HIDDEN = 1e30
PARAMS = pltpu.CompilerParams(vmem_limit_bytes=12 * 1024 * 1024)
ANY_SPEC = pl.BlockSpec(memory_space=pl.ANY)
NEAR_COST = pl.CostEstimate(flops=8_000_000_000, bytes_accessed=1000, transcendentals=0)
COST = pl.CostEstimate(flops=1000, bytes_accessed=1000, transcendentals=0)
TOKEN = jax.ShapeDtypeStruct((8, 128), jnp.float32)


def dot(a, b):
    return jnp.dot(a, b, preferred_element_type=jnp.float32)


def span(start, size):
    return pl.ds(pl.multiple_of(start, size), size)


def rows_of(slot):
    return slice(slot * FT, (slot + 1) * FT)


def add_frame(lanes, kt, values, block):
    units = [(n, row) for n in range(len(lanes)) for row in range(0, FT, block)]

    def scores(unit):
        n, row = unit
        return dot(lanes[n][0][row : row + block, :], kt[...])

    ahead = scores(units[0])
    for at, (n, row) in enumerate(units):
        s = ahead
        if at + 1 < len(units):
            ahead = scores(units[at + 1])
        weights = jnp.exp2(s * SCALE).astype(jnp.bfloat16)
        lanes[n][1](row, dot(weights, values[...]))


def visible(info, slot, frame):
    return (frame >= 1) & (frame >= info[2 + slot]) & (frame <= info[4 + slot])


def lanes_of(h, heads):
    share = HD // heads
    lane = lax.broadcasted_iota(jnp.int32, (1, HD), 1)
    return (lane >= h * share) & (lane < (h + 1) * share)


def spread(packed, h, heads):
    row = lax.broadcasted_iota(jnp.int32, (HD, HD), 0)
    chosen = jnp.where(row == h * (HD // heads), 1.0, 0.0).astype(jnp.bfloat16)
    high = packed.astype(jnp.bfloat16)
    low = (packed - high.astype(jnp.float32)).astype(jnp.bfloat16)
    return dot(high, chosen) + dot(low, chosen)


def more_columns(own, slot):
    lane = lax.broadcasted_iota(jnp.int32, (1, HD), 1)
    flag = jnp.where(lane == 1 + slot, 1.0, 0.0)
    return jnp.where(lane == 0, -own, flag).astype(jnp.bfloat16)


def set_more_rows(kt, seen):
    row = lax.broadcasted_iota(jnp.int32, (HD, FT), 0)
    more = jnp.where(row == 0, 1.0, 0.0)
    for slot, shown in enumerate(seen):
        more = jnp.where(row == 1 + slot, jnp.where(shown, 0.0, -HIDDEN), more)
    kt[HD:, :] = more.astype(jnp.bfloat16)


def sums_into(acc_from, acc, sums, slot, column, h, heads):
    def add(row, added):
        rows = slice(slot * FT + row, slot * FT + row + added.shape[0])
        new = added[:, :HD]
        acc[rows, column] = new if acc_from is None else acc_from[rows, column] + new
        old = sums[rows, :]
        sums[rows, :] = jnp.where(lanes_of(h, heads), old + added[:, HD:], old)

    return add


def load_frame(kt, values, k, v, column):
    kt[:HD, :] = k[:, column].T
    values[:, :HD] = v[:, column]


def each_head(group, turn, part=None):
    offset, heads = group
    first, count = part or (0, heads)

    def body(h, carry):
        turn(h, span(h * HD, HD), span((h + offset) * HD, HD))
        return carry

    lax.fori_loop(first, first + count, body, 0)


def own_kernel(group, info, q, k, v, *refs):
    more, acc, sums, token, kt, values = refs
    heads = group[1]
    first = info[0]
    token[...] = jnp.zeros_like(token)
    values[:, HD:] = jnp.ones((FT, HD), jnp.bfloat16)
    ones = jnp.ones((HD, HD), jnp.bfloat16)
    sums[...] = jnp.zeros_like(sums)

    def shifts(h, column, wide):
        for slot in (0, 1):
            rows = rows_of(slot)
            product = q[rows, wide].astype(jnp.float32) * k[rows, wide].astype(jnp.float32)
            more[rows, column] = more_columns(dot(product.astype(jnp.bfloat16), ones), slot)

    each_head(group, shifts)
    for frame in (0, 1):
        set_more_rows(kt, [visible(info, slot, first + frame) for slot in (0, 1)])

        def turn(h, column, wide):
            load_frame(kt, values, k.at[rows_of(frame)], v.at[rows_of(frame)], wide)
            lanes = []
            for slot in (0, 1):
                rows = rows_of(slot)
                add = sums_into(acc if frame else None, acc, sums, slot, column, h, heads)
                queries = jnp.concatenate([q[rows, wide], more[rows, column]], axis=1)
                lanes.append((queries, add))
            add_frame(lanes, kt, values, 256)

        each_head(group, turn)


def near_kernel(group, info, q, more, acc_in, sums_in, near_k, near_v, *refs):
    acc, sums, token, kt, values, k_buf, v_buf, sem = refs
    offset, heads = group
    token[...] = jnp.zeros_like(token)
    first = info[0]
    order = (1, 0)
    copies = {
        frame: [
            pltpu.make_async_copy(
                source.at[pl.ds(frame * FT, FT), pl.ds(offset * HD, heads * HD)],
                buf.at[frame],
                sem.at[frame, n],
            )
            for n, (source, buf) in enumerate(((near_k, k_buf), (near_v, v_buf)))
        ]
        for frame in order
    }
    for frame in order:
        for copy in copies[frame]:
            copy.start()
    values[:, HD:] = jnp.ones((FT, HD), jnp.bfloat16)
    sums[...] = sums_in[...]
    for frame in order:
        set_more_rows(kt, [visible(info, slot, first - 2 + frame) for slot in (0, 1)])
        for copy in copies[frame]:
            copy.wait()

        def turn(h, column, wide):
            load_frame(kt, values, k_buf.at[frame], v_buf.at[frame], column)
            acc_from = acc_in if frame == order[0] else acc
            lanes = []
            for slot in (0, 1):
                rows = rows_of(slot)
                add = sums_into(acc_from, acc, sums, slot, column, h, heads)
                queries = jnp.concatenate([q[rows, wide], more[rows, column]], axis=1)
                lanes.append((queries, add))
            add_frame(lanes, kt, values, 256)

        each_head(group, turn)


def final_kernel(
    group, part, info, q, more, acc_in, sums_in,
    sink_a, sink_b, far, relay, key_any, value_any, near_k, near_v, *refs,
):
    outs = refs[:-9]
    kt, values, k_buf, v_buf, results, acc, shift, too_large, sem = refs[-9:]
    first = info[0]
    core = info[6]
    far_seen = visible(info, 0, first - 3)
    offset, heads = group
    group_columns = pl.ds(offset * HD, heads * HD)
    part_first, part_heads = part
    values[:, HD:] = jnp.ones((FT, HD), jnp.bfloat16)

    own_columns = pl.ds(0, heads * HD)

    def copies(frame, k, k_row, v, v_row, columns):
        return [
            pltpu.make_async_copy(
                source.at[pl.ds(row, FT), columns], buf.at[frame], sem.at[frame, n]
            )
            for n, (source, row, buf) in enumerate(((k, k_row, k_buf), (v, v_row, v_buf)))
        ]

    arriving = {
        0: [
            (0, sink_a, 0, sink_b, 0, own_columns),
            (1, far, 0, far, FT, own_columns),
        ],
        1: [
            (0, sink_b, 0, sink_a, 0, own_columns),
            (1, relay, 0, relay, FT, group_columns),
        ],
    }
    for which, listed in arriving.items():

        @pl.when(core == which)
        def _():
            started = [copies(*entry) for entry in listed]
            for act in (lambda copy: copy.start(), lambda copy: copy.wait()):
                for pair in started:
                    for copy in pair:
                        act(copy)

    def write(slot, h, acc, total):
        attended = (acc / total).astype(jnp.bfloat16)
        column = span((h - part_first) * HD, HD)
        if len(outs) == 1:
            outs[0][rows_of(slot), column] = attended
        else:

            @pl.when(info[1] == slot)
            def _():
                outs[0][:, column] = attended

            @pl.when(info[1] != slot)
            def _():
                outs[1][:, column] = attended

    def turn(h, column, wide):
        def into(ref, slot, old=None):
            def add(row, added):
                rows = slice(slot * FT + row, slot * FT + row + added.shape[0])
                ref[rows, :] = added if old is None else old[rows, :] + added

            return add

        queries = [
            jnp.concatenate([q[rows_of(slot), wide], more[rows_of(slot), column]], axis=1)
            for slot in (0, 1)
        ]
        load_frame(kt, values, k_buf.at[0], v_buf.at[0], column)
        set_more_rows(kt, [True, True])
        add_frame([(queries[slot], into(results, slot)) for slot in (1, 0)], kt, values, 256)
        load_frame(kt, values, k_buf.at[1], v_buf.at[1], column)
        set_more_rows(kt, [far_seen, False])
        add_frame([(queries[0], into(results, 0, results))], kt, values, 256)
        for slot in (0, 1):
            rows = rows_of(slot)
            total = spread(sums_in[rows, :], h, heads) + results[rows, HD:]
            write(slot, h, acc_in[rows, column] + results[rows, :HD], total)
            too_large[h, slot] = jnp.max(jnp.where(total < LIMIT, 0.0, 1.0))

    each_head(group, turn, part)

    def again(slot, h, column, wide):
        here, there = core == 0, core == 1
        sources = [
            (here, sink_a, 0, sink_b, 0, column), (there, sink_b, 0, sink_a, 0, column)
        ]
        if slot == 0:
            sources += [
                (far_seen & here, far, 0, far, FT, column),
                (far_seen & there, relay, 0, relay, FT, wide),
            ]
        for frame in (0, 1):
            row = frame * FT
            own = visible(info, slot, first + frame)
            sources.append((own, key_any, row, value_any, row, wide))
            behind = visible(info, slot, first - 2 + frame)
            sources.append((behind, near_k, row, near_v, row, wide))
        one = (k_buf.at[0, :, :HD], v_buf.at[0, :, :HD])

        def sweep(step):
            def visit(t, carry):
                seen = False
                for n, (shown, k, k_row, v, v_row, where) in enumerate(sources):
                    chosen = (t == n) & shown
                    seen = seen | chosen

                    @pl.when(chosen)
                    def _():
                        for n, (ref, row) in enumerate(((k, k_row), (v, v_row))):
                            copy = pltpu.make_async_copy(
                                ref.at[pl.ds(row, FT), where], one[n], sem.at[0, n]
                            )
                            copy.start()
                            copy.wait()

                @pl.when(seen)
                def _():
                    load_frame(kt, values, k_buf.at[0], v_buf.at[0], slice(0, HD))
                    step()

                return carry

            lax.fori_loop(0, len(sources), visit, 0)

        queries = q[rows_of(slot), wide]

        def scores(j):
            return dot(queries, kt[:HD, j * BK : (j + 1) * BK]) * SCALE

        def peak():
            for j in range(FT // BK):
                shift[...] = jnp.maximum(shift[...], jnp.max(scores(j), axis=1, keepdims=True))

        def more_sums():
            for j in range(FT // BK):
                s = scores(j)
                weights = jnp.concatenate(
                    [jnp.exp2(s[:, c : c + HD] - shift[...]) for c in range(0, BK, HD)], axis=1
                )
                keys = values[j * BK : (j + 1) * BK, :]
                acc[...] = acc[...] + dot(weights.astype(jnp.bfloat16), keys)

        shift[...] = jnp.full((FT, HD), -jnp.inf, jnp.float32)
        acc[...] = jnp.zeros((FT, 2 * HD), jnp.float32)
        sweep(peak)
        sweep(more_sums)
        write(slot, h, acc[:, :HD], acc[:, HD:])

    def check(h, column, wide):
        for slot in (0, 1):
            pl.when(too_large[h, slot] > 0.0)(lambda slot=slot: again(slot, h, column, wide))

    each_head(group, check, part)


VMEM_SPEC = pl.BlockSpec(memory_space=pltpu.VMEM)
SMEM_SPEC = pl.BlockSpec(memory_space=pltpu.SMEM)


def stage(kernel, arrays, in_any, outs, scratch, cost=None, tokens=()):
    n = len(arrays)

    def run(*refs):
        kernel(*refs[:n], *refs[n + len(tokens) :])

    return pl.pallas_call(
        run,
        in_specs=[SMEM_SPEC] + [VMEM_SPEC] * (n - in_any - 1)
        + [ANY_SPEC] * (in_any + len(tokens)),
        out_specs=[VMEM_SPEC] * len(outs),
        scratch_shapes=[
            pltpu.VMEM((2 * HD, FT), jnp.bfloat16), pltpu.VMEM((FT, 2 * HD), jnp.bfloat16)
        ] + list(scratch),
        out_shape=outs,
        compiler_params=PARAMS,
        cost_estimate=cost or COST,
    )(*arrays, *tokens)


def pick(flag, taken, kept, tokens=(), columns=None):
    column, width = columns or (0, kept.shape[1])

    def kernel(flag, taken, kept, *refs):
        out, sem = refs[-2:]
        for value, source in ((1, taken), (0, kept)):

            @pl.when(flag[0] == value)
            def _():
                rows = source.at[pl.ds(0, FT), pl.ds(column, width)]
                copy = pltpu.make_async_copy(rows, out, sem)
                copy.start()
                copy.wait()

    return pl.pallas_call(
        kernel,
        in_specs=[SMEM_SPEC] + [ANY_SPEC] * (2 + len(tokens)),
        out_specs=VMEM_SPEC,
        out_shape=jax.ShapeDtypeStruct((FT, width), jnp.bfloat16),
        scratch_shapes=[pltpu.SemaphoreType.DMA],
        compiler_params=PARAMS,
        cost_estimate=COST,
    )(jnp.reshape(flag, (1,)).astype(jnp.int32), taken, kept, *tokens)


def last_frames(group, keys, values, tokens=()):
    columns = pl.ds(group[0] * HD, group[1] * HD)
    n = len(tokens)

    def kernel(keys, values, *refs):
        out, sem = refs[n:]
        started = [
            pltpu.make_async_copy(
                source.at[pl.ds(FT, FT), columns], out.at[pl.ds(i * FT, FT)], sem.at[i]
            )
            for i, source in enumerate((keys, values))
        ]
        for copy in started:
            copy.start()
        for copy in started:
            copy.wait()

    return pl.pallas_call(
        kernel,
        in_specs=[ANY_SPEC] * (2 + n),
        out_specs=VMEM_SPEC,
        out_shape=jax.ShapeDtypeStruct((2 * FT, group[1] * HD), jnp.bfloat16),
        scratch_shapes=[pltpu.SemaphoreType.DMA((2,))],
        compiler_params=PARAMS,
        cost_estimate=COST,
    )(keys, values, *tokens)


def sink_steps(size):
    bits = [1 << b for b in range(1, size.bit_length() - 1)]
    orders = (bits[::-1], bits[::-1])
    done = [0, 0]
    steps = []
    for step in range(len(bits)):
        pairs = []
        for which in (0, 1):
            bit = orders[which][step]
            holders = [i for i in range(0, size, 2) if i & ~done[which] == 0]
            pairs += [(i + which, (i | bit) + which) for i in holders]
            done[which] |= bit
        steps.append(pairs)
    return steps


def project(info, parts, weight, base=None, dtype=jnp.bfloat16):
    columns = weight.shape[1]
    turns = 6
    block = columns // turns
    rows = parts[0][0].shape[0]
    n = len(parts)
    bases = [] if base is None else [base]

    def kernel(info, *refs):
        weight, out = refs[n], refs[-1]
        column = span(pl.program_id(0) * block, block)
        total = None if base is None else refs[n + 1][:, column]
        for a, (array, place, received) in zip(refs[:n], parts):
            owner = 1 - info[1] if received else info[1]
            first = owner * (weight.shape[0] // 2) + place
            product = dot(a[...], weight[pl.ds(pl.multiple_of(first, HD), array.shape[1]), column])
            total = product if total is None else total + product
        out[...] = total.astype(dtype)

    return pl.pallas_call(
        kernel,
        grid=(turns,),
        in_specs=[SMEM_SPEC] + [VMEM_SPEC] * (n + 1 + len(bases)),
        out_specs=pl.BlockSpec((rows, block), lambda i: (0, i)),
        out_shape=jax.ShapeDtypeStruct((rows, columns), dtype),
        compiler_params=PARAMS,
        cost_estimate=COST,
    )(info, *[a for a, _, _ in parts], weight, *bases)


def local(query_states, key_states, value_states, win_start, group_end, out_weight):
    axis = "tm"
    size = lax.axis_size(axis)
    paired = lax.axis_size("head") == 2
    me = lax.axis_index(axis)
    core = me % 2
    heads = query_states.shape[1] // HD
    info = jnp.concatenate(
        [
            jnp.stack([me * 2, lax.axis_index("head")]).astype(jnp.int32),
            win_start.astype(jnp.int32),
            group_end.astype(jnp.int32),
            jnp.stack([core]).astype(jnp.int32),
        ]
    )
    groups = [(0, heads // 2), (heads // 2, heads // 2)] if heads % 2 == 0 else [(0, heads)]
    rows = query_states.shape[0]
    group_width = groups[0][1] * HD
    more_like = jax.ShapeDtypeStruct((rows, group_width), jnp.bfloat16)
    acc_like = jax.ShapeDtypeStruct((rows, group_width), jnp.float32)
    sums_like = jax.ShapeDtypeStruct((rows, HD), jnp.float32)
    frame_buffers = [pltpu.VMEM((2, FT, group_width), jnp.bfloat16)] * 2
    dma_sems = pltpu.SemaphoreType.DMA((2, 2))

    onward = [(i, i + 1) for i in range(size - 1)]
    near_k = lax.ppermute(key_states, axis, onward)
    near_v = lax.ppermute(value_states, axis, onward)
    moved = lax.ppermute(value_states, axis, [(0, 1)])
    held = pick(core, moved, key_states)

    def near_stage(group, state, tokens):
        return stage(
            functools.partial(near_kernel, group),
            [info, query_states, *state, near_k, near_v], 2, [acc_like, sums_like, TOKEN],
            frame_buffers + [dma_sems], NEAR_COST, tokens,
        )

    def flag_of(pairs):
        takes = jnp.zeros((), bool)
        for _, target in pairs:
            takes = takes | (me == target)
        return takes

    states = []
    *steps, last_step = sink_steps(size)
    for step, pairs in enumerate(steps):
        moved = lax.ppermute(held, axis, pairs)
        tokens = []
        if step < len(groups):
            *state, token = stage(
                functools.partial(own_kernel, groups[step]),
                [info, query_states, key_states, value_states], 0,
                [more_like, acc_like, sums_like, TOKEN], [], tokens=[held] * (step > 0),
            )
            states.append(state)
            tokens.append(token)
        if step < len(steps) - 1:
            held = pick(flag_of(pairs), moved, held, tokens)

    on_chip = [(i, i + 1) for i in range(0, size, 2)]
    near_last = last_frames((0, heads), near_k, near_v, tokens)
    relay = lax.ppermute(near_last, axis, on_chip)
    own_done, arrivals = tokens, [near_last]
    sends = []
    for g, group in enumerate(groups):
        columns = group[0] * HD, group[1] * HD
        own_last = last_frames(group, key_states, value_states, own_done)
        far = lax.ppermute(own_last, axis, [(i, i + 2) for i in range(0, size - 2, 2)])
        part = pick(flag_of(steps[-1]), moved, held, own_done + arrivals, columns)
        arriving = lax.ppermute(part, axis, last_step)
        if g == 0:
            tokens = []
            for n, state in enumerate(states):
                *sums_now, token = near_stage(groups[n], state, [part])
                states[n] = state[0], *sums_now
                tokens.append(token)
        part = pick(flag_of(last_step), arriving, part, [far] + tokens)
        other = lax.ppermute(part, axis, [(i, i ^ 1) for i in range(size)])
        own_done, arrivals = [part], []
        last = g == len(groups) - 1
        for first, count in [(h, 1) for h in range(group[1])] if last else [(0, group[1])]:
            out = jax.ShapeDtypeStruct((FT if paired else rows, count * HD), jnp.bfloat16)
            results = stage(
                functools.partial(final_kernel, group, (first, count)),
                [info, query_states, *states[g], part, other, far, relay,
                 key_states, value_states, near_k, near_v], 8,
                [out] * (2 if paired else 1),
                frame_buffers + [
                    pltpu.VMEM((rows, 2 * HD), jnp.float32),
                    pltpu.VMEM((FT, 2 * HD), jnp.float32),
                    pltpu.VMEM((FT, HD), jnp.float32),
                    pltpu.SMEM((group[1], 2), jnp.float32),
                    dma_sems,
                ],
            )
            received = None
            if paired:
                received = lax.ppermute(results[1], "head", [(0, 1), (1, 0)])
            sends.append((columns[0] + first * HD, results[0], received))
        tokens = [sends[0][1]]
    if not paired:
        attended = jnp.concatenate([mine for _, mine, _ in sends], axis=1)
        token_rows = lax.all_to_all(attended, "head", split_axis=0, concat_axis=1, tiled=True)
        return dot(token_rows, out_weight).astype(jnp.bfloat16)
    early = [(mine, place, False) for place, mine, _ in sends]
    early.append((sends[0][2], sends[0][0], True))
    late = [(received, place, True) for place, _, received in sends[1:]]
    base = project(info, early, out_weight, dtype=jnp.float32)
    return project(info, late, out_weight, base)


def solution(mesh):
    in_specs = (P("tm", "head"), P("tm", "head"), P("tm", "head"), P("tm"), P("tm"), P())
    out_specs = P(("tm", "head"), None)
    return jax.shard_map(local, mesh=mesh, in_specs=in_specs, out_specs=out_specs, check_vma=False)
```

```python
import functools

import jax
import jax.numpy as jnp
from jax import lax
from jax.experimental import pallas as pl
from jax.experimental.pallas import tpu as pltpu
from jax.sharding import PartitionSpec as P

HD = 128
FT = 768
BK = 256
LOG2E = 1.4426950408889634
SCALE = HD ** -0.5 * LOG2E
LIMIT = 1e30
HIDDEN = 1e30
PARAMS = pltpu.CompilerParams(vmem_limit_bytes=12 * 1024 * 1024)
ANY_SPEC = pl.BlockSpec(memory_space=pl.ANY)
NEAR_COST = pl.CostEstimate(flops=8_000_000_000, bytes_accessed=1000, transcendentals=0)
COST = pl.CostEstimate(flops=1000, bytes_accessed=1000, transcendentals=0)
TOKEN = jax.ShapeDtypeStruct((8, 128), jnp.float32)


def dot(a, b):
    return jnp.dot(a, b, preferred_element_type=jnp.float32)


def span(start, size):
    return pl.ds(pl.multiple_of(start, size), size)


def rows_of(slot):
    return slice(slot * FT, (slot + 1) * FT)


def add_frame(lanes, kt, values, block):
    units = [(n, row) for n in range(len(lanes)) for row in range(0, FT, block)]

    def scores(unit):
        n, row = unit
        queries = lanes[n][0]
        return dot(queries[row : row + block, :], kt[: queries.shape[1], :])

    ahead = scores(units[0])
    for at, (n, row) in enumerate(units):
        s = ahead
        if at + 1 < len(units):
            ahead = scores(units[at + 1])
        if len(lanes[n]) == 2:
            weights = jnp.exp2(s * SCALE).astype(jnp.bfloat16)
        else:
            shift = lanes[n][2][row : row + block, :]
            columns = [s[:, c : c + HD] * SCALE - shift for c in range(0, FT, HD)]
            weights = jnp.concatenate([jnp.exp2(c).astype(jnp.bfloat16) for c in columns], axis=1)
        lanes[n][1](row, dot(weights, values[...]))


def visible(info, slot, frame):
    return (frame >= 1) & (frame >= info[2 + slot]) & (frame <= info[4 + slot])


def lanes_of(h, heads):
    share = HD // heads
    lane = lax.broadcasted_iota(jnp.int32, (1, HD), 1)
    return (lane >= h * share) & (lane < (h + 1) * share)


def spread(packed, h, heads):
    row = lax.broadcasted_iota(jnp.int32, (HD, HD), 0)
    chosen = jnp.where(row == h * (HD // heads), 1.0, 0.0).astype(jnp.bfloat16)
    high = packed.astype(jnp.bfloat16)
    low = (packed - high.astype(jnp.float32)).astype(jnp.bfloat16)
    return dot(high, chosen) + dot(low, chosen)


def more_columns(own, slot):
    lane = lax.broadcasted_iota(jnp.int32, (1, HD), 1)
    flag = jnp.where(lane == 1 + slot, 1.0, 0.0)
    return jnp.where(lane == 0, -own, flag).astype(jnp.bfloat16)


def set_more_rows(kt, seen):
    row = lax.broadcasted_iota(jnp.int32, (HD, FT), 0)
    more = jnp.where(row == 0, 1.0, 0.0)
    for slot, shown in enumerate(seen):
        more = jnp.where(row == 1 + slot, jnp.where(shown, 0.0, -HIDDEN), more)
    kt[HD:, :] = more.astype(jnp.bfloat16)


def sums_into(acc_from, acc, sums, slot, column, h, heads):
    def add(row, added):
        rows = slice(slot * FT + row, slot * FT + row + added.shape[0])
        new = added[:, :HD]
        acc[rows, column] = new if acc_from is None else acc_from[rows, column] + new
        old = sums[rows, :]
        sums[rows, :] = jnp.where(lanes_of(h, heads), old + added[:, HD:], old)

    return add


def load_frame(kt, values, k, v, column):
    kt[:HD, :] = k[:, column].T
    values[:, :HD] = v[:, column]


def each_head(group, turn, part=None):
    offset, heads = group
    first, count = part or (0, heads)

    def body(h, carry):
        turn(h, span(h * HD, HD), span((h + offset) * HD, HD))
        return carry

    lax.fori_loop(first, first + count, body, 0)


def own_kernel(group, info, q, k, v, *refs):
    more, acc, sums, token, kt, values = refs
    heads = group[1]
    first = info[0]
    token[...] = jnp.zeros_like(token)
    values[:, HD:] = jnp.ones((FT, HD), jnp.bfloat16)
    ones = jnp.ones((HD, HD), jnp.bfloat16)
    sums[...] = jnp.zeros_like(sums)

    def turn(h, column, wide):
        shifts = []
        for slot in (0, 1):
            rows = rows_of(slot)
            product = q[rows, wide].astype(jnp.float32) * k[rows, wide].astype(jnp.float32)
            own = dot(product.astype(jnp.bfloat16), ones).astype(jnp.bfloat16).astype(jnp.float32)
            more[rows, column] = more_columns(own, slot)
            shifts.append(own * SCALE)
        for frame in (0, 1):
            load_frame(kt, values, k.at[rows_of(frame)], v.at[rows_of(frame)], wide)
            lanes = []
            for slot in (0, 1):
                add = sums_into(acc if frame else None, acc, sums, slot, column, h, heads)
                shift = jnp.where(visible(info, slot, first + frame), shifts[slot], HIDDEN)
                lanes.append((q[rows_of(slot), wide], add, shift))
            add_frame(lanes, kt, values, 256)

    each_head(group, turn)


def near_kernel(group, info, q, more, acc_in, sums_in, near_k, near_v, *refs):
    acc, sums, token, kt, values, k_buf, v_buf, sem = refs
    offset, heads = group
    token[...] = jnp.zeros_like(token)
    first = info[0]
    order = (1, 0)
    copies = {
        frame: [
            pltpu.make_async_copy(
                source.at[pl.ds(frame * FT, FT), pl.ds(offset * HD, heads * HD)],
                buf.at[frame],
                sem.at[frame, n],
            )
            for n, (source, buf) in enumerate(((near_k, k_buf), (near_v, v_buf)))
        ]
        for frame in order
    }
    for frame in order:
        for copy in copies[frame]:
            copy.start()
    values[:, HD:] = jnp.ones((FT, HD), jnp.bfloat16)
    sums[...] = sums_in[...]
    for frame in order:
        set_more_rows(kt, [visible(info, slot, first - 2 + frame) for slot in (0, 1)])
        for copy in copies[frame]:
            copy.wait()

        def turn(h, column, wide):
            load_frame(kt, values, k_buf.at[frame], v_buf.at[frame], column)
            acc_from = acc_in if frame == order[0] else acc
            lanes = []
            for slot in (0, 1):
                rows = rows_of(slot)
                add = sums_into(acc_from, acc, sums, slot, column, h, heads)
                queries = jnp.concatenate([q[rows, wide], more[rows, column]], axis=1)
                lanes.append((queries, add))
            add_frame(lanes, kt, values, 256)

        each_head(group, turn)


def final_kernel(
    group, part, info, q, more, acc_in, sums_in,
    sink_a, sink_b, far, relay, key_any, value_any, near_k, near_v, *refs,
):
    outs = refs[:-9]
    kt, values, k_buf, v_buf, results, acc, shift, too_large, sem = refs[-9:]
    first = info[0]
    core = info[6]
    far_seen = visible(info, 0, first - 3)
    offset, heads = group
    group_columns = pl.ds(offset * HD, heads * HD)
    part_first, part_heads = part
    values[:, HD:] = jnp.ones((FT, HD), jnp.bfloat16)

    own_columns = pl.ds(0, heads * HD)

    def copies(frame, k, k_row, v, v_row, columns):
        return [
            pltpu.make_async_copy(
                source.at[pl.ds(row, FT), columns], buf.at[frame], sem.at[frame, n]
            )
            for n, (source, row, buf) in enumerate(((k, k_row, k_buf), (v, v_row, v_buf)))
        ]

    arriving = {
        0: [
            (0, sink_a, 0, sink_b, 0, own_columns),
            (1, far, 0, far, FT, own_columns),
        ],
        1: [
            (0, sink_b, 0, sink_a, 0, own_columns),
            (1, relay, 0, relay, FT, group_columns),
        ],
    }
    for which, listed in arriving.items():

        @pl.when(core == which)
        def _():
            started = [copies(*entry) for entry in listed]
            for act in (lambda copy: copy.start(), lambda copy: copy.wait()):
                for pair in started:
                    for copy in pair:
                        act(copy)

    def write(slot, h, acc, total):
        attended = (acc / total).astype(jnp.bfloat16)
        column = span((h - part_first) * HD, HD)
        if len(outs) == 1:
            outs[0][rows_of(slot), column] = attended
        else:

            @pl.when(info[1] == slot)
            def _():
                outs[0][:, column] = attended

            @pl.when(info[1] != slot)
            def _():
                outs[1][:, column] = attended

    def turn(h, column, wide):
        def into(ref, slot, old=None):
            def add(row, added):
                rows = slice(slot * FT + row, slot * FT + row + added.shape[0])
                ref[rows, :] = added if old is None else old[rows, :] + added

            return add

        queries = [
            jnp.concatenate([q[rows_of(slot), wide], more[rows_of(slot), column]], axis=1)
            for slot in (0, 1)
        ]
        load_frame(kt, values, k_buf.at[0], v_buf.at[0], column)
        set_more_rows(kt, [True, True])
        add_frame([(queries[slot], into(results, slot)) for slot in (1, 0)], kt, values, 256)
        load_frame(kt, values, k_buf.at[1], v_buf.at[1], column)
        set_more_rows(kt, [far_seen, False])
        add_frame([(queries[0], into(results, 0, results))], kt, values, 256)
        for slot in (0, 1):
            rows = rows_of(slot)
            total = spread(sums_in[rows, :], h, heads) + results[rows, HD:]
            write(slot, h, acc_in[rows, column] + results[rows, :HD], total)
            too_large[h, slot] = jnp.max(jnp.where(total < LIMIT, 0.0, 1.0))

    each_head(group, turn, part)

    def again(slot, h, column, wide):
        here, there = core == 0, core == 1
        sources = [
            (here, sink_a, 0, sink_b, 0, column), (there, sink_b, 0, sink_a, 0, column)
        ]
        if slot == 0:
            sources += [
                (far_seen & here, far, 0, far, FT, column),
                (far_seen & there, relay, 0, relay, FT, wide),
            ]
        for frame in (0, 1):
            row = frame * FT
            own = visible(info, slot, first + frame)
            sources.append((own, key_any, row, value_any, row, wide))
            behind = visible(info, slot, first - 2 + frame)
            sources.append((behind, near_k, row, near_v, row, wide))
        one = (k_buf.at[0, :, :HD], v_buf.at[0, :, :HD])

        def sweep(step):
            def visit(t, carry):
                seen = False
                for n, (shown, k, k_row, v, v_row, where) in enumerate(sources):
                    chosen = (t == n) & shown
                    seen = seen | chosen

                    @pl.when(chosen)
                    def _():
                        for n, (ref, row) in enumerate(((k, k_row), (v, v_row))):
                            copy = pltpu.make_async_copy(
                                ref.at[pl.ds(row, FT), where], one[n], sem.at[0, n]
                            )
                            copy.start()
                            copy.wait()

                @pl.when(seen)
                def _():
                    load_frame(kt, values, k_buf.at[0], v_buf.at[0], slice(0, HD))
                    step()

                return carry

            lax.fori_loop(0, len(sources), visit, 0)

        queries = q[rows_of(slot), wide]

        def scores(j):
            return dot(queries, kt[:HD, j * BK : (j + 1) * BK]) * SCALE

        def peak():
            for j in range(FT // BK):
                shift[...] = jnp.maximum(shift[...], jnp.max(scores(j), axis=1, keepdims=True))

        def more_sums():
            for j in range(FT // BK):
                s = scores(j)
                weights = jnp.concatenate(
                    [jnp.exp2(s[:, c : c + HD] - shift[...]) for c in range(0, BK, HD)], axis=1
                )
                keys = values[j * BK : (j + 1) * BK, :]
                acc[...] = acc[...] + dot(weights.astype(jnp.bfloat16), keys)

        shift[...] = jnp.full((FT, HD), -jnp.inf, jnp.float32)
        acc[...] = jnp.zeros((FT, 2 * HD), jnp.float32)
        sweep(peak)
        sweep(more_sums)
        write(slot, h, acc[:, :HD], acc[:, HD:])

    def check(h, column, wide):
        for slot in (0, 1):
            pl.when(too_large[h, slot] > 0.0)(lambda slot=slot: again(slot, h, column, wide))

    each_head(group, check, part)


VMEM_SPEC = pl.BlockSpec(memory_space=pltpu.VMEM)
SMEM_SPEC = pl.BlockSpec(memory_space=pltpu.SMEM)


def stage(kernel, arrays, in_any, outs, scratch, cost=None, tokens=()):
    n = len(arrays)

    def run(*refs):
        kernel(*refs[:n], *refs[n + len(tokens) :])

    return pl.pallas_call(
        run,
        in_specs=[SMEM_SPEC] + [VMEM_SPEC] * (n - in_any - 1)
        + [ANY_SPEC] * (in_any + len(tokens)),
        out_specs=[VMEM_SPEC] * len(outs),
        scratch_shapes=[
            pltpu.VMEM((2 * HD, FT), jnp.bfloat16), pltpu.VMEM((FT, 2 * HD), jnp.bfloat16)
        ] + list(scratch),
        out_shape=outs,
        compiler_params=PARAMS,
        cost_estimate=cost or COST,
    )(*arrays, *tokens)


def pick(flag, taken, kept, tokens=(), columns=None):
    column, width = columns or (0, kept.shape[1])

    def kernel(flag, taken, kept, *refs):
        out, sem = refs[-2:]
        for value, source in ((1, taken), (0, kept)):

            @pl.when(flag[0] == value)
            def _():
                rows = source.at[pl.ds(0, FT), pl.ds(column, width)]
                copy = pltpu.make_async_copy(rows, out, sem)
                copy.start()
                copy.wait()

    return pl.pallas_call(
        kernel,
        in_specs=[SMEM_SPEC] + [ANY_SPEC] * (2 + len(tokens)),
        out_specs=VMEM_SPEC,
        out_shape=jax.ShapeDtypeStruct((FT, width), jnp.bfloat16),
        scratch_shapes=[pltpu.SemaphoreType.DMA],
        compiler_params=PARAMS,
        cost_estimate=COST,
    )(jnp.reshape(flag, (1,)).astype(jnp.int32), taken, kept, *tokens)


def last_frames(group, keys, values, tokens=()):
    columns = pl.ds(group[0] * HD, group[1] * HD)
    n = len(tokens)

    def kernel(keys, values, *refs):
        out, sem = refs[n:]
        started = [
            pltpu.make_async_copy(
                source.at[pl.ds(FT, FT), columns], out.at[pl.ds(i * FT, FT)], sem.at[i]
            )
            for i, source in enumerate((keys, values))
        ]
        for copy in started:
            copy.start()
        for copy in started:
            copy.wait()

    return pl.pallas_call(
        kernel,
        in_specs=[ANY_SPEC] * (2 + n),
        out_specs=VMEM_SPEC,
        out_shape=jax.ShapeDtypeStruct((2 * FT, group[1] * HD), jnp.bfloat16),
        scratch_shapes=[pltpu.SemaphoreType.DMA((2,))],
        compiler_params=PARAMS,
        cost_estimate=COST,
    )(keys, values, *tokens)


def sink_steps(size):
    bits = [1 << b for b in range(1, size.bit_length() - 1)]
    orders = (bits[::-1], bits[::-1])
    done = [0, 0]
    steps = []
    for step in range(len(bits)):
        pairs = []
        for which in (0, 1):
            bit = orders[which][step]
            holders = [i for i in range(0, size, 2) if i & ~done[which] == 0]
            pairs += [(i + which, (i | bit) + which) for i in holders]
            done[which] |= bit
        steps.append(pairs)
    return steps


def project(info, parts, weight, base=None, dtype=jnp.bfloat16):
    columns = weight.shape[1]
    turns = 6
    block = columns // turns
    rows = parts[0][0].shape[0]
    n = len(parts)
    bases = [] if base is None else [base]

    def kernel(info, *refs):
        weight, out = refs[n], refs[-1]
        column = span(pl.program_id(0) * block, block)
        total = None if base is None else refs[n + 1][:, column]
        for a, (array, place, received) in zip(refs[:n], parts):
            owner = 1 - info[1] if received else info[1]
            first = owner * (weight.shape[0] // 2) + place
            product = dot(a[...], weight[pl.ds(pl.multiple_of(first, HD), array.shape[1]), column])
            total = product if total is None else total + product
        out[...] = total.astype(dtype)

    return pl.pallas_call(
        kernel,
        grid=(turns,),
        in_specs=[SMEM_SPEC] + [VMEM_SPEC] * (n + 1 + len(bases)),
        out_specs=pl.BlockSpec((rows, block), lambda i: (0, i)),
        out_shape=jax.ShapeDtypeStruct((rows, columns), dtype),
        compiler_params=PARAMS,
        cost_estimate=COST,
    )(info, *[a for a, _, _ in parts], weight, *bases)


def local(query_states, key_states, value_states, win_start, group_end, out_weight):
    axis = "tm"
    size = lax.axis_size(axis)
    paired = lax.axis_size("head") == 2
    me = lax.axis_index(axis)
    core = me % 2
    heads = query_states.shape[1] // HD
    info = jnp.concatenate(
        [
            jnp.stack([me * 2, lax.axis_index("head")]).astype(jnp.int32),
            win_start.astype(jnp.int32),
            group_end.astype(jnp.int32),
            jnp.stack([core]).astype(jnp.int32),
        ]
    )
    groups = [(0, heads // 2), (heads // 2, heads // 2)] if heads % 2 == 0 else [(0, heads)]
    rows = query_states.shape[0]
    group_width = groups[0][1] * HD
    more_like = jax.ShapeDtypeStruct((rows, group_width), jnp.bfloat16)
    acc_like = jax.ShapeDtypeStruct((rows, group_width), jnp.float32)
    sums_like = jax.ShapeDtypeStruct((rows, HD), jnp.float32)
    frame_buffers = [pltpu.VMEM((2, FT, group_width), jnp.bfloat16)] * 2
    dma_sems = pltpu.SemaphoreType.DMA((2, 2))

    onward = [(i, i + 1) for i in range(size - 1)]
    near_k = lax.ppermute(key_states, axis, onward)
    near_v = lax.ppermute(value_states, axis, onward)
    moved = lax.ppermute(value_states, axis, [(0, 1)])
    held = pick(core, moved, key_states)

    def near_stage(group, state, tokens):
        return stage(
            functools.partial(near_kernel, group),
            [info, query_states, *state, near_k, near_v], 2, [acc_like, sums_like, TOKEN],
            frame_buffers + [dma_sems], NEAR_COST, tokens,
        )

    def flag_of(pairs):
        takes = jnp.zeros((), bool)
        for _, target in pairs:
            takes = takes | (me == target)
        return takes

    states = []
    *steps, last_step = sink_steps(size)
    for step, pairs in enumerate(steps):
        moved = lax.ppermute(held, axis, pairs)
        tokens = []
        if step < len(groups):
            *state, token = stage(
                functools.partial(own_kernel, groups[step]),
                [info, query_states, key_states, value_states], 0,
                [more_like, acc_like, sums_like, TOKEN], [], tokens=[held] * (step > 0),
            )
            states.append(state)
            tokens.append(token)
        if step < len(steps) - 1:
            held = pick(flag_of(pairs), moved, held, tokens)

    on_chip = [(i, i + 1) for i in range(0, size, 2)]
    near_last = last_frames((0, heads), near_k, near_v, tokens)
    relay = lax.ppermute(near_last, axis, on_chip)
    own_done, arrivals = tokens, [near_last]
    sends = []
    for g, group in enumerate(groups):
        columns = group[0] * HD, group[1] * HD
        own_last = last_frames(group, key_states, value_states, own_done)
        far = lax.ppermute(own_last, axis, [(i, i + 2) for i in range(0, size - 2, 2)])
        part = pick(flag_of(steps[-1]), moved, held, own_done + arrivals, columns)
        arriving = lax.ppermute(part, axis, last_step)
        if g == 0:
            tokens = []
            for n, state in enumerate(states):
                *sums_now, token = near_stage(groups[n], state, [part] * (n > 0))
                states[n] = state[0], *sums_now
                tokens.append(token)
        part = pick(flag_of(last_step), arriving, part, [far] + tokens)
        other = lax.ppermute(part, axis, [(i, i ^ 1) for i in range(size)])
        own_done, arrivals = [part], []
        last = g == len(groups) - 1
        for first, count in [(h, 1) for h in range(group[1])] if last else [(0, group[1])]:
            out = jax.ShapeDtypeStruct((FT if paired else rows, count * HD), jnp.bfloat16)
            results = stage(
                functools.partial(final_kernel, group, (first, count)),
                [info, query_states, *states[g], part, other, far, relay,
                 key_states, value_states, near_k, near_v], 8,
                [out] * (2 if paired else 1),
                frame_buffers + [
                    pltpu.VMEM((rows, 2 * HD), jnp.float32),
                    pltpu.VMEM((FT, 2 * HD), jnp.float32),
                    pltpu.VMEM((FT, HD), jnp.float32),
                    pltpu.SMEM((group[1], 2), jnp.float32),
                    dma_sems,
                ],
            )
            received = None
            if paired:
                received = lax.ppermute(results[1], "head", [(0, 1), (1, 0)])
            sends.append((columns[0] + first * HD, results[0], received))
        tokens = [sends[0][1]]
    if not paired:
        attended = jnp.concatenate([mine for _, mine, _ in sends], axis=1)
        token_rows = lax.all_to_all(attended, "head", split_axis=0, concat_axis=1, tiled=True)
        return dot(token_rows, out_weight).astype(jnp.bfloat16)
    early = [(mine, place, False) for place, mine, _ in sends]
    early.append((sends[0][2], sends[0][0], True))
    late = [(received, place, True) for place, _, received in sends[1:]]
    base = project(info, early, out_weight, dtype=jnp.float32)
    return project(info, late, out_weight, base)


def solution(mesh):
    in_specs = (P("tm", "head"), P("tm", "head"), P("tm", "head"), P("tm"), P("tm"), P())
    out_specs = P(("tm", "head"), None)
    return jax.shard_map(local, mesh=mesh, in_specs=in_specs, out_specs=out_specs, check_vma=False)
```

```python
import functools

import jax
import jax.numpy as jnp
from jax import lax
from jax.experimental import pallas as pl
from jax.experimental.pallas import tpu as pltpu
from jax.sharding import PartitionSpec as P

HD = 128
FT = 768
BK = 256
LOG2E = 1.4426950408889634
SCALE = HD ** -0.5 * LOG2E
LIMIT = 1e30
HIDDEN = 1e30
PARAMS = pltpu.CompilerParams(vmem_limit_bytes=12 * 1024 * 1024)
ANY_SPEC = pl.BlockSpec(memory_space=pl.ANY)
NEAR_COST = pl.CostEstimate(flops=8_000_000_000, bytes_accessed=1000, transcendentals=0)
COST = pl.CostEstimate(flops=1000, bytes_accessed=1000, transcendentals=0)
TOKEN = jax.ShapeDtypeStruct((8, 128), jnp.float32)


def dot(a, b):
    return jnp.dot(a, b, preferred_element_type=jnp.float32)


def span(start, size):
    return pl.ds(pl.multiple_of(start, size), size)


def rows_of(slot):
    return slice(slot * FT, (slot + 1) * FT)


def add_frame(lanes, kt, values, block):
    units = [(n, row) for n in range(len(lanes)) for row in range(0, FT, block)]

    def scores(unit):
        n, row = unit
        return dot(lanes[n][0][row : row + block, :], kt[...])

    ahead = scores(units[0])
    for at, (n, row) in enumerate(units):
        s = ahead
        if at + 1 < len(units):
            ahead = scores(units[at + 1])
        _, shift, add = lanes[n]
        weights = [
            jnp.exp2(s[:, c : c + HD] * SCALE - shift[row : row + block, :]).astype(jnp.bfloat16)
            for c in range(0, FT, HD)
        ]
        add(row, dot(jnp.concatenate(weights, axis=1), values[...]))


def visible(info, slot, frame):
    return (frame >= 1) & (frame >= info[2 + slot]) & (frame <= info[4 + slot])


def lanes_of(h, heads):
    share = HD // heads
    lane = lax.broadcasted_iota(jnp.int32, (1, HD), 1)
    return (lane >= h * share) & (lane < (h + 1) * share)


def spread(packed, h, heads):
    row = lax.broadcasted_iota(jnp.int32, (HD, HD), 0)
    chosen = jnp.where(row == h * (HD // heads), 1.0, 0.0).astype(jnp.bfloat16)
    high = packed.astype(jnp.bfloat16)
    low = (packed - high.astype(jnp.float32)).astype(jnp.bfloat16)
    return dot(high, chosen) + dot(low, chosen)


def shift_of(own, seen):
    return jnp.where(seen, own.astype(jnp.float32) * SCALE, HIDDEN)


def sums_into(acc_from, acc, sums, slot, column, h, heads):
    def add(row, added):
        rows = slice(slot * FT + row, slot * FT + row + added.shape[0])
        new = added[:, :HD]
        acc[rows, column] = new if acc_from is None else acc_from[rows, column] + new
        old = sums[rows, :]
        sums[rows, :] = jnp.where(lanes_of(h, heads), old + added[:, HD:], old)

    return add


def load_frame(kt, values, k, v, column):
    kt[...] = k[:, column].T
    values[:, :HD] = v[:, column]


def each_head(group, turn, part=None):
    offset, heads = group
    first, count = part or (0, heads)

    def body(h, carry):
        turn(h, span(h * HD, HD), span((h + offset) * HD, HD))
        return carry

    lax.fori_loop(first, first + count, body, 0)


def own_kernel(group, info, q, k, v, *refs):
    own, acc, sums, token, kt, values = refs
    heads = group[1]
    first = info[0]
    token[...] = jnp.zeros_like(token)
    values[:, HD:] = jnp.ones((FT, HD), jnp.bfloat16)
    ones = jnp.ones((HD, HD), jnp.bfloat16)
    sums[...] = jnp.zeros_like(sums)

    def turn(h, column, wide):
        for slot in (0, 1):
            rows = rows_of(slot)
            product = q[rows, wide].astype(jnp.float32) * k[rows, wide].astype(jnp.float32)
            own[rows, column] = dot(product.astype(jnp.bfloat16), ones).astype(jnp.bfloat16)
        for frame in (0, 1):
            load_frame(kt, values, k.at[rows_of(frame)], v.at[rows_of(frame)], wide)
            lanes = []
            for slot in (0, 1):
                rows = rows_of(slot)
                shift = shift_of(own[rows, column], visible(info, slot, first + frame))
                add = sums_into(acc if frame else None, acc, sums, slot, column, h, heads)
                lanes.append((q[rows, wide], shift, add))
            add_frame(lanes, kt, values, 256)

    each_head(group, turn)


def near_kernel(group, info, q, own, acc_in, sums_in, near_k, near_v, *refs):
    acc, sums, token, kt, values, k_buf, v_buf, sem = refs
    offset, heads = group
    token[...] = jnp.zeros_like(token)
    first = info[0]
    order = (1, 0)
    copies = {
        frame: [
            pltpu.make_async_copy(
                source.at[pl.ds(frame * FT, FT), pl.ds(offset * HD, heads * HD)],
                buf.at[frame],
                sem.at[frame, n],
            )
            for n, (source, buf) in enumerate(((near_k, k_buf), (near_v, v_buf)))
        ]
        for frame in order
    }
    for frame in order:
        for copy in copies[frame]:
            copy.start()
    values[:, HD:] = jnp.ones((FT, HD), jnp.bfloat16)
    sums[...] = sums_in[...]
    for frame in order:
        for copy in copies[frame]:
            copy.wait()

        def turn(h, column, wide):
            load_frame(kt, values, k_buf.at[frame], v_buf.at[frame], column)
            acc_from = acc_in if frame == order[0] else acc
            lanes = []
            for slot in (0, 1):
                rows = rows_of(slot)
                add = sums_into(acc_from, acc, sums, slot, column, h, heads)
                shift = shift_of(own[rows, column], visible(info, slot, first - 2 + frame))
                lanes.append((q[rows, wide], shift, add))
            add_frame(lanes, kt, values, 256)

        each_head(group, turn)


def final_kernel(
    group, part, info, q, own, acc_in, sums_in,
    sink_a, sink_b, far, relay, key_any, value_any, near_k, near_v, *refs,
):
    outs = refs[:-9]
    kt, values, k_buf, v_buf, results, acc, shift, too_large, sem = refs[-9:]
    first = info[0]
    core = info[6]
    far_seen = visible(info, 0, first - 3)
    offset, heads = group
    group_columns = pl.ds(offset * HD, heads * HD)
    part_first, part_heads = part
    values[:, HD:] = jnp.ones((FT, HD), jnp.bfloat16)

    own_columns = pl.ds(0, heads * HD)

    def copies(frame, k, k_row, v, v_row, columns):
        return [
            pltpu.make_async_copy(
                source.at[pl.ds(row, FT), columns], buf.at[frame], sem.at[frame, n]
            )
            for n, (source, row, buf) in enumerate(((k, k_row, k_buf), (v, v_row, v_buf)))
        ]

    arriving = {
        0: [
            (0, sink_a, 0, sink_b, 0, own_columns),
            (1, far, 0, far, FT, own_columns),
        ],
        1: [
            (0, sink_b, 0, sink_a, 0, own_columns),
            (1, relay, 0, relay, FT, group_columns),
        ],
    }
    for which, listed in arriving.items():

        @pl.when(core == which)
        def _():
            started = [copies(*entry) for entry in listed]
            for act in (lambda copy: copy.start(), lambda copy: copy.wait()):
                for pair in started:
                    for copy in pair:
                        act(copy)

    def write(slot, h, acc, total):
        attended = (acc / total).astype(jnp.bfloat16)
        column = span((h - part_first) * HD, HD)
        if len(outs) == 1:
            outs[0][span(slot * FT, FT), column] = attended
        else:

            @pl.when(info[1] == slot)
            def _():
                outs[0][:, column] = attended

            @pl.when(info[1] != slot)
            def _():
                outs[1][:, column] = attended

    def turn(h, column, wide):
        def into(ref, slot, old=None):
            def add(row, added):
                rows = slice(slot * FT + row, slot * FT + row + added.shape[0])
                ref[rows, :] = added if old is None else old[rows, :] + added

            return add

        def lane(slot, seen, add):
            rows = rows_of(slot)
            return q[rows, wide], shift_of(own[rows, column], seen), add

        load_frame(kt, values, k_buf.at[0], v_buf.at[0], column)
        add_frame([lane(slot, True, into(results, slot)) for slot in (1, 0)], kt, values, 256)
        load_frame(kt, values, k_buf.at[1], v_buf.at[1], column)
        add_frame([lane(0, far_seen, into(results, 0, results))], kt, values, 256)
        for slot in (0, 1):
            rows = rows_of(slot)
            total = spread(sums_in[rows, :], h, heads) + results[rows, HD:]
            write(slot, h, acc_in[rows, column] + results[rows, :HD], total)
            too_large[h, slot] = jnp.max(jnp.where(total < LIMIT, 0.0, 1.0))

    each_head(group, turn, part)

    def again(slot, h, column, wide):
        here, there = core == 0, core == 1
        far_here = far_seen & (slot == 0)
        sources = [
            (here, sink_a, 0, sink_b, 0, column), (there, sink_b, 0, sink_a, 0, column),
            (far_here & here, far, 0, far, FT, column),
            (far_here & there, relay, 0, relay, FT, wide),
        ]
        for frame in (0, 1):
            row = frame * FT
            shown = visible(info, slot, first + frame)
            sources.append((shown, key_any, row, value_any, row, wide))
            behind = visible(info, slot, first - 2 + frame)
            sources.append((behind, near_k, row, near_v, row, wide))
        one = (k_buf.at[0, :, :HD], v_buf.at[0, :, :HD])

        def sweep(step):
            def visit(t, carry):
                seen = False
                for n, (shown, k, k_row, v, v_row, where) in enumerate(sources):
                    chosen = (t == n) & shown
                    seen = seen | chosen

                    @pl.when(chosen)
                    def _():
                        for n, (ref, row) in enumerate(((k, k_row), (v, v_row))):
                            copy = pltpu.make_async_copy(
                                ref.at[pl.ds(row, FT), where], one[n], sem.at[0, n]
                            )
                            copy.start()
                            copy.wait()

                @pl.when(seen)
                def _():
                    load_frame(kt, values, k_buf.at[0], v_buf.at[0], slice(0, HD))
                    step()

                return carry

            lax.fori_loop(0, len(sources), visit, 0)

        def by_rows(step):
            def turn(i, carry):
                rows = span(i * HD, HD)
                queries = q[span(slot * FT + i * HD, HD), wide]
                for j in range(0, FT, BK):
                    step(rows, dot(queries, kt[:, j : j + BK]) * SCALE, values[j : j + BK, :])
                return carry

            lax.fori_loop(0, FT // HD, turn, 0)

        def peak(rows, s, _):
            shift[rows, :] = jnp.maximum(shift[rows, :], jnp.max(s, axis=1, keepdims=True))

        def more_sums(rows, s, some_values):
            weights = jnp.concatenate(
                [jnp.exp2(s[:, c : c + HD] - shift[rows, :]) for c in range(0, BK, HD)], axis=1
            )
            acc[rows, :] = acc[rows, :] + dot(weights.astype(jnp.bfloat16), some_values)

        shift[...] = jnp.full((FT, HD), -jnp.inf, jnp.float32)
        acc[...] = jnp.zeros((FT, 2 * HD), jnp.float32)
        sweep(lambda: by_rows(peak))
        sweep(lambda: by_rows(more_sums))
        write(slot, h, acc[:, :HD], acc[:, HD:])

    def check(h, column, wide):
        def turn(slot, carry):
            pl.when(too_large[h, slot] > 0.0)(lambda: again(slot, h, column, wide))
            return carry

        lax.fori_loop(0, 2, turn, 0)

    each_head(group, check, part)


VMEM_SPEC = pl.BlockSpec(memory_space=pltpu.VMEM)
SMEM_SPEC = pl.BlockSpec(memory_space=pltpu.SMEM)


def stage(kernel, arrays, in_any, outs, scratch, cost=None, tokens=()):
    n = len(arrays)

    def run(*refs):
        kernel(*refs[:n], *refs[n + len(tokens) :])

    return pl.pallas_call(
        run,
        in_specs=[SMEM_SPEC] + [VMEM_SPEC] * (n - in_any - 1)
        + [ANY_SPEC] * (in_any + len(tokens)),
        out_specs=[VMEM_SPEC] * len(outs),
        scratch_shapes=[
            pltpu.VMEM((HD, FT), jnp.bfloat16), pltpu.VMEM((FT, 2 * HD), jnp.bfloat16)
        ] + list(scratch),
        out_shape=outs,
        compiler_params=PARAMS,
        cost_estimate=cost or COST,
    )(*arrays, *tokens)


def pick(flag, taken, kept, tokens=(), columns=None):
    column, width = columns or (0, kept.shape[1])

    def kernel(flag, taken, kept, *refs):
        out, sem = refs[-2:]
        for value, source in ((1, taken), (0, kept)):

            @pl.when(flag[0] == value)
            def _():
                rows = source.at[pl.ds(0, FT), pl.ds(column, width)]
                copy = pltpu.make_async_copy(rows, out, sem)
                copy.start()
                copy.wait()

    return pl.pallas_call(
        kernel,
        in_specs=[SMEM_SPEC] + [ANY_SPEC] * (2 + len(tokens)),
        out_specs=VMEM_SPEC,
        out_shape=jax.ShapeDtypeStruct((FT, width), jnp.bfloat16),
        scratch_shapes=[pltpu.SemaphoreType.DMA],
        compiler_params=PARAMS,
        cost_estimate=COST,
    )(jnp.reshape(flag, (1,)).astype(jnp.int32), taken, kept, *tokens)


def last_frames(group, keys, values, tokens=()):
    columns = pl.ds(group[0] * HD, group[1] * HD)
    n = len(tokens)

    def kernel(keys, values, *refs):
        out, sem = refs[n:]
        started = [
            pltpu.make_async_copy(
                source.at[pl.ds(FT, FT), columns], out.at[pl.ds(i * FT, FT)], sem.at[i]
            )
            for i, source in enumerate((keys, values))
        ]
        for copy in started:
            copy.start()
        for copy in started:
            copy.wait()

    return pl.pallas_call(
        kernel,
        in_specs=[ANY_SPEC] * (2 + n),
        out_specs=VMEM_SPEC,
        out_shape=jax.ShapeDtypeStruct((2 * FT, group[1] * HD), jnp.bfloat16),
        scratch_shapes=[pltpu.SemaphoreType.DMA((2,))],
        compiler_params=PARAMS,
        cost_estimate=COST,
    )(keys, values, *tokens)


def sink_steps(size):
    bits = [1 << b for b in range(1, size.bit_length() - 1)]
    orders = (bits[::-1], bits[::-1])
    done = [0, 0]
    steps = []
    for step in range(len(bits)):
        pairs = []
        for which in (0, 1):
            bit = orders[which][step]
            holders = [i for i in range(0, size, 2) if i & ~done[which] == 0]
            pairs += [(i + which, (i | bit) + which) for i in holders]
            done[which] |= bit
        steps.append(pairs)
    return steps


def project(info, parts, weight, base=None, dtype=jnp.bfloat16):
    columns = weight.shape[1]
    turns = 6
    block = columns // turns
    rows = parts[0][0].shape[0]
    n = len(parts)
    bases = [] if base is None else [base]

    def kernel(info, *refs):
        weight, out = refs[n], refs[-1]
        column = span(pl.program_id(0) * block, block)
        total = None if base is None else refs[n + 1][:, column]
        for a, (array, place, received) in zip(refs[:n], parts):
            owner = 1 - info[1] if received else info[1]
            first = owner * (weight.shape[0] // 2) + place
            product = dot(a[...], weight[pl.ds(pl.multiple_of(first, HD), array.shape[1]), column])
            total = product if total is None else total + product
        out[...] = total.astype(dtype)

    return pl.pallas_call(
        kernel,
        grid=(turns,),
        in_specs=[SMEM_SPEC] + [VMEM_SPEC] * (n + 1 + len(bases)),
        out_specs=pl.BlockSpec((rows, block), lambda i: (0, i)),
        out_shape=jax.ShapeDtypeStruct((rows, columns), dtype),
        compiler_params=PARAMS,
        cost_estimate=COST,
    )(info, *[a for a, _, _ in parts], weight, *bases)


def local(query_states, key_states, value_states, win_start, group_end, out_weight):
    axis = "tm"
    size = lax.axis_size(axis)
    paired = lax.axis_size("head") == 2
    me = lax.axis_index(axis)
    core = me % 2
    heads = query_states.shape[1] // HD
    info = jnp.concatenate(
        [
            jnp.stack([me * 2, lax.axis_index("head")]).astype(jnp.int32),
            win_start.astype(jnp.int32),
            group_end.astype(jnp.int32),
            jnp.stack([core]).astype(jnp.int32),
        ]
    )
    groups = [(0, heads // 2), (heads // 2, heads // 2)] if heads % 2 == 0 else [(0, heads)]
    rows = query_states.shape[0]
    group_width = groups[0][1] * HD
    own_like = jax.ShapeDtypeStruct((rows, group_width), jnp.bfloat16)
    acc_like = jax.ShapeDtypeStruct((rows, group_width), jnp.float32)
    sums_like = jax.ShapeDtypeStruct((rows, HD), jnp.float32)
    frame_buffers = [pltpu.VMEM((2, FT, group_width), jnp.bfloat16)] * 2
    dma_sems = pltpu.SemaphoreType.DMA((2, 2))

    onward = [(i, i + 1) for i in range(size - 1)]
    near_k = lax.ppermute(key_states, axis, onward)
    near_v = lax.ppermute(value_states, axis, onward)
    moved = lax.ppermute(value_states, axis, [(0, 1)])
    held = pick(core, moved, key_states)

    def near_stage(group, state, tokens):
        return stage(
            functools.partial(near_kernel, group),
            [info, query_states, *state, near_k, near_v], 2, [acc_like, sums_like, TOKEN],
            frame_buffers + [dma_sems], NEAR_COST, tokens,
        )

    def flag_of(pairs):
        takes = jnp.zeros((), bool)
        for _, target in pairs:
            takes = takes | (me == target)
        return takes

    states = []
    *steps, last_step = sink_steps(size)
    for step, pairs in enumerate(steps):
        moved = lax.ppermute(held, axis, pairs)
        tokens = []
        if step < len(groups):
            *state, token = stage(
                functools.partial(own_kernel, groups[step]),
                [info, query_states, key_states, value_states], 0,
                [own_like, acc_like, sums_like, TOKEN], [], tokens=[held] * (step > 0),
            )
            states.append(state)
            tokens.append(token)
        if step < len(steps) - 1:
            held = pick(flag_of(pairs), moved, held, tokens)

    on_chip = [(i, i + 1) for i in range(0, size, 2)]
    near_last = last_frames((0, heads), near_k, near_v, tokens)
    relay = lax.ppermute(near_last, axis, on_chip)
    own_done, arrivals = tokens, [near_last]
    sends = []
    for g, group in enumerate(groups):
        columns = group[0] * HD, group[1] * HD
        own_last = last_frames(group, key_states, value_states, own_done)
        far = lax.ppermute(own_last, axis, [(i, i + 2) for i in range(0, size - 2, 2)])
        part = pick(flag_of(steps[-1]), moved, held, own_done + arrivals, columns)
        arriving = lax.ppermute(part, axis, last_step)
        if g == 0:
            tokens = []
            for n, state in enumerate(states):
                *sums_now, token = near_stage(groups[n], state, [part])
                states[n] = state[0], *sums_now
                tokens.append(token)
        part = pick(flag_of(last_step), arriving, part, [far] + tokens)
        other = lax.ppermute(part, axis, [(i, i ^ 1) for i in range(size)])
        own_done, arrivals = [part], []
        last = g == len(groups) - 1
        for first, count in [(h, 1) for h in range(group[1])] if last else [(0, group[1])]:
            out = jax.ShapeDtypeStruct((FT if paired else rows, count * HD), jnp.bfloat16)
            results = stage(
                functools.partial(final_kernel, group, (first, count)),
                [info, query_states, *states[g], part, other, far, relay,
                 key_states, value_states, near_k, near_v], 8,
                [out] * (2 if paired else 1),
                frame_buffers + [
                    pltpu.VMEM((rows, 2 * HD), jnp.float32),
                    pltpu.VMEM((FT, 2 * HD), jnp.float32),
                    pltpu.VMEM((FT, HD), jnp.float32),
                    pltpu.SMEM((group[1], 2), jnp.float32),
                    dma_sems,
                ],
            )
            received = None
            if paired:
                received = lax.ppermute(results[1], "head", [(0, 1), (1, 0)])
            sends.append((columns[0] + first * HD, results[0], received))
        tokens = [sends[0][1]]
    if not paired:
        attended = jnp.concatenate([mine for _, mine, _ in sends], axis=1)
        token_rows = lax.all_to_all(attended, "head", split_axis=0, concat_axis=1, tiled=True)
        return dot(token_rows, out_weight).astype(jnp.bfloat16)
    early = [(mine, place, False) for place, mine, _ in sends]
    early.append((sends[0][2], sends[0][0], True))
    late = [(received, place, True) for place, _, received in sends[1:]]
    base = project(info, early, out_weight, dtype=jnp.float32)
    return project(info, late, out_weight, base)


def solution(mesh):
    in_specs = (P("tm", "head"), P("tm", "head"), P("tm", "head"), P("tm"), P("tm"), P())
    out_specs = P(("tm", "head"), None)
    return jax.shard_map(local, mesh=mesh, in_specs=in_specs, out_specs=out_specs, check_vma=False)
```

```python
import functools

import jax
import jax.numpy as jnp
from jax import lax
from jax.experimental import pallas as pl
from jax.experimental.pallas import tpu as pltpu
from jax.sharding import PartitionSpec as P

HD = 128
FT = 768
BK = 256
LOG2E = 1.4426950408889634
SCALE = HD ** -0.5 * LOG2E
LIMIT = 1e30
HIDDEN = 1e30
PARAMS = pltpu.CompilerParams(vmem_limit_bytes=12 * 1024 * 1024)
ANY_SPEC = pl.BlockSpec(memory_space=pl.ANY)
NEAR_COST = pl.CostEstimate(flops=8_000_000_000, bytes_accessed=1000, transcendentals=0)
COST = pl.CostEstimate(flops=1000, bytes_accessed=1000, transcendentals=0)
TOKEN = jax.ShapeDtypeStruct((8, 128), jnp.float32)


def dot(a, b):
    return jnp.dot(a, b, preferred_element_type=jnp.float32)


def span(start, size):
    return pl.ds(pl.multiple_of(start, size), size)


def rows_of(slot):
    return slice(slot * FT, (slot + 1) * FT)


def add_frame(lanes, kt, values, block):
    units = [(n, row) for n in range(len(lanes)) for row in range(0, FT, block)]

    def scores(unit):
        n, row = unit
        return dot(lanes[n][0][row : row + block, :], kt[...])

    ahead = scores(units[0])
    for at, (n, row) in enumerate(units):
        s = ahead
        if at + 1 < len(units):
            ahead = scores(units[at + 1])
        _, shift, add = lanes[n]
        weights = [
            jnp.exp2(s[:, c : c + HD] * SCALE - shift[row : row + block, :]).astype(jnp.bfloat16)
            for c in range(0, FT, HD)
        ]
        add(row, dot(jnp.concatenate(weights, axis=1), values[...]))


def visible(info, slot, frame):
    return (frame >= 1) & (frame >= info[2 + slot]) & (frame <= info[4 + slot])


def lanes_of(h, heads):
    share = HD // heads
    lane = lax.broadcasted_iota(jnp.int32, (1, HD), 1)
    return (lane >= h * share) & (lane < (h + 1) * share)


def spread(packed, h, heads):
    row = lax.broadcasted_iota(jnp.int32, (HD, HD), 0)
    chosen = jnp.where(row == h * (HD // heads), 1.0, 0.0).astype(jnp.bfloat16)
    high = packed.astype(jnp.bfloat16)
    low = (packed - high.astype(jnp.float32)).astype(jnp.bfloat16)
    return dot(high, chosen) + dot(low, chosen)


def shift_of(own, seen):
    return jnp.where(seen, own.astype(jnp.float32) * SCALE, HIDDEN)


def sums_into(acc_from, acc, sums, slot, column, h, heads):
    def add(row, added):
        rows = slice(slot * FT + row, slot * FT + row + added.shape[0])
        new = added[:, :HD]
        acc[rows, column] = new if acc_from is None else acc_from[rows, column] + new
        old = sums[rows, :]
        sums[rows, :] = jnp.where(lanes_of(h, heads), old + added[:, HD:], old)

    return add


def load_frame(kt, values, k, v, column):
    kt[...] = k[:, column].T
    values[:, :HD] = v[:, column]


def each_head(group, turn, part=None):
    offset, heads = group
    first, count = part or (0, heads)

    def body(h, carry):
        turn(h, span(h * HD, HD), span((h + offset) * HD, HD))
        return carry

    lax.fori_loop(first, first + count, body, 0)


def own_kernel(group, info, q, k, v, *refs):
    own, acc, sums, token, kt, values = refs
    heads = group[1]
    first = info[0]
    token[...] = jnp.zeros_like(token)
    values[:, HD:] = jnp.ones((FT, HD), jnp.bfloat16)
    ones = jnp.ones((HD, HD), jnp.bfloat16)
    sums[...] = jnp.zeros_like(sums)

    def turn(h, column, wide):
        for slot in (0, 1):
            rows = rows_of(slot)
            product = q[rows, wide].astype(jnp.float32) * k[rows, wide].astype(jnp.float32)
            own[rows, column] = dot(product.astype(jnp.bfloat16), ones).astype(jnp.bfloat16)
        for frame in (0, 1):
            load_frame(kt, values, k.at[rows_of(frame)], v.at[rows_of(frame)], wide)
            lanes = []
            for slot in (0, 1):
                rows = rows_of(slot)
                shift = shift_of(own[rows, column], visible(info, slot, first + frame))
                add = sums_into(acc if frame else None, acc, sums, slot, column, h, heads)
                lanes.append((q[rows, wide], shift, add))
            add_frame(lanes, kt, values, 256)

    each_head(group, turn)


def near_kernel(group, info, q, own, acc_in, sums_in, near_k, near_v, *refs):
    acc, sums, token, kt, values, k_buf, v_buf, sem = refs
    offset, heads = group
    token[...] = jnp.zeros_like(token)
    first = info[0]
    order = (1, 0)
    copies = {
        frame: [
            pltpu.make_async_copy(
                source.at[pl.ds(frame * FT, FT), pl.ds(offset * HD, heads * HD)],
                buf.at[frame],
                sem.at[frame, n],
            )
            for n, (source, buf) in enumerate(((near_k, k_buf), (near_v, v_buf)))
        ]
        for frame in order
    }
    for frame in order:
        for copy in copies[frame]:
            copy.start()
    values[:, HD:] = jnp.ones((FT, HD), jnp.bfloat16)
    sums[...] = sums_in[...]
    for frame in order:
        for copy in copies[frame]:
            copy.wait()

        def turn(h, column, wide):
            load_frame(kt, values, k_buf.at[frame], v_buf.at[frame], column)
            acc_from = acc_in if frame == order[0] else acc
            lanes = []
            for slot in (0, 1):
                rows = rows_of(slot)
                add = sums_into(acc_from, acc, sums, slot, column, h, heads)
                shift = shift_of(own[rows, column], visible(info, slot, first - 2 + frame))
                lanes.append((q[rows, wide], shift, add))
            add_frame(lanes, kt, values, 256)

        each_head(group, turn)


def final_kernel(
    group, part, info, q, own, acc_in, sums_in,
    sink_a, sink_b, far, relay, key_any, value_any, near_k, near_v, *refs,
):
    outs = refs[:-9]
    kt, values, k_buf, v_buf, results, acc, shift, too_large, sem = refs[-9:]
    first = info[0]
    core = info[6]
    far_seen = visible(info, 0, first - 3)
    offset, heads = group
    group_columns = pl.ds(offset * HD, heads * HD)
    part_first, part_heads = part
    values[:, HD:] = jnp.ones((FT, HD), jnp.bfloat16)

    own_columns = pl.ds(0, heads * HD)

    def copies(frame, k, k_row, v, v_row, columns):
        return [
            pltpu.make_async_copy(
                source.at[pl.ds(row, FT), columns], buf.at[frame], sem.at[frame, n]
            )
            for n, (source, row, buf) in enumerate(((k, k_row, k_buf), (v, v_row, v_buf)))
        ]

    arriving = {
        0: [
            (0, sink_a, 0, sink_b, 0, own_columns),
            (1, far, 0, far, FT, own_columns),
        ],
        1: [
            (0, sink_b, 0, sink_a, 0, own_columns),
            (1, relay, 0, relay, FT, group_columns),
        ],
    }
    for which, listed in arriving.items():

        @pl.when(core == which)
        def _():
            started = [copies(*entry) for entry in listed]
            for act in (lambda copy: copy.start(), lambda copy: copy.wait()):
                for pair in started:
                    for copy in pair:
                        act(copy)

    def write(slot, h, acc, total):
        attended = (acc / total).astype(jnp.bfloat16)
        column = span((h - part_first) * HD, HD)
        if len(outs) == 1:
            outs[0][span(slot * FT, FT), column] = attended
        else:

            @pl.when(info[1] == slot)
            def _():
                outs[0][:, column] = attended

            @pl.when(info[1] != slot)
            def _():
                outs[1][:, column] = attended

    def turn(h, column, wide):
        def into(ref, slot, old=None):
            def add(row, added):
                rows = slice(slot * FT + row, slot * FT + row + added.shape[0])
                ref[rows, :] = added if old is None else old[rows, :] + added

            return add

        def lane(slot, seen, add):
            rows = rows_of(slot)
            return q[rows, wide], shift_of(own[rows, column], seen), add

        load_frame(kt, values, k_buf.at[0], v_buf.at[0], column)
        add_frame([lane(slot, True, into(results, slot)) for slot in (1, 0)], kt, values, 256)
        load_frame(kt, values, k_buf.at[1], v_buf.at[1], column)
        add_frame([lane(0, far_seen, into(results, 0, results))], kt, values, 256)
        for slot in (0, 1):
            rows = rows_of(slot)
            total = spread(sums_in[rows, :], h, heads) + results[rows, HD:]
            write(slot, h, acc_in[rows, column] + results[rows, :HD], total)
            too_large[h, slot] = jnp.max(jnp.where(total < LIMIT, 0.0, 1.0))

    each_head(group, turn, part)

    def again(slot, h, column, wide):
        here, there = core == 0, core == 1
        far_here = far_seen & (slot == 0)
        sources = [
            (here, sink_a, 0, sink_b, 0, column), (there, sink_b, 0, sink_a, 0, column),
            (far_here & here, far, 0, far, FT, column),
            (far_here & there, relay, 0, relay, FT, wide),
        ]
        for frame in (0, 1):
            row = frame * FT
            shown = visible(info, slot, first + frame)
            sources.append((shown, key_any, row, value_any, row, wide))
            behind = visible(info, slot, first - 2 + frame)
            sources.append((behind, near_k, row, near_v, row, wide))
        one = (k_buf.at[0, :, :HD], v_buf.at[0, :, :HD])

        def sweep(step):
            def visit(t, carry):
                seen = False
                for n, (shown, k, k_row, v, v_row, where) in enumerate(sources):
                    chosen = (t == n) & shown
                    seen = seen | chosen

                    @pl.when(chosen)
                    def _():
                        for n, (ref, row) in enumerate(((k, k_row), (v, v_row))):
                            copy = pltpu.make_async_copy(
                                ref.at[pl.ds(row, FT), where], one[n], sem.at[0, n]
                            )
                            copy.start()
                            copy.wait()

                @pl.when(seen)
                def _():
                    load_frame(kt, values, k_buf.at[0], v_buf.at[0], slice(0, HD))
                    step()

                return carry

            lax.fori_loop(0, len(sources), visit, 0)

        def by_rows(step):
            def turn(i, carry):
                rows = span(i * HD, HD)
                queries = q[span(slot * FT + i * HD, HD), wide]
                for j in range(0, FT, BK):
                    step(rows, dot(queries, kt[:, j : j + BK]) * SCALE, values[j : j + BK, :])
                return carry

            lax.fori_loop(0, FT // HD, turn, 0)

        def peak(rows, s, _):
            shift[rows, :] = jnp.maximum(shift[rows, :], jnp.max(s, axis=1, keepdims=True))

        def more_sums(rows, s, some_values):
            weights = jnp.concatenate(
                [jnp.exp2(s[:, c : c + HD] - shift[rows, :]) for c in range(0, BK, HD)], axis=1
            )
            acc[rows, :] = acc[rows, :] + dot(weights.astype(jnp.bfloat16), some_values)

        shift[...] = jnp.full((FT, HD), -jnp.inf, jnp.float32)
        acc[...] = jnp.zeros((FT, 2 * HD), jnp.float32)
        sweep(lambda: by_rows(peak))
        sweep(lambda: by_rows(more_sums))
        write(slot, h, acc[:, :HD], acc[:, HD:])

    def check(h, column, wide):
        def turn(slot, carry):
            pl.when(too_large[h, slot] > 0.0)(lambda: again(slot, h, column, wide))
            return carry

        lax.fori_loop(0, 2, turn, 0)

    each_head(group, check, part)


VMEM_SPEC = pl.BlockSpec(memory_space=pltpu.VMEM)
SMEM_SPEC = pl.BlockSpec(memory_space=pltpu.SMEM)


def stage(kernel, arrays, in_any, outs, scratch, cost=None, tokens=()):
    n = len(arrays)

    def run(*refs):
        kernel(*refs[:n], *refs[n + len(tokens) :])

    return pl.pallas_call(
        run,
        in_specs=[SMEM_SPEC] + [VMEM_SPEC] * (n - in_any - 1)
        + [ANY_SPEC] * (in_any + len(tokens)),
        out_specs=[VMEM_SPEC] * len(outs),
        scratch_shapes=[
            pltpu.VMEM((HD, FT), jnp.bfloat16), pltpu.VMEM((FT, 2 * HD), jnp.bfloat16)
        ] + list(scratch),
        out_shape=outs,
        compiler_params=PARAMS,
        cost_estimate=cost or COST,
    )(*arrays, *tokens)


def pick(flag, taken, kept, tokens=(), columns=None):
    column, width = columns or (0, kept.shape[1])

    def kernel(flag, taken, kept, *refs):
        out, sem = refs[-2:]
        for value, source in ((1, taken), (0, kept)):

            @pl.when(flag[0] == value)
            def _():
                rows = source.at[pl.ds(0, FT), pl.ds(column, width)]
                copy = pltpu.make_async_copy(rows, out, sem)
                copy.start()
                copy.wait()

    return pl.pallas_call(
        kernel,
        in_specs=[SMEM_SPEC] + [ANY_SPEC] * (2 + len(tokens)),
        out_specs=VMEM_SPEC,
        out_shape=jax.ShapeDtypeStruct((FT, width), jnp.bfloat16),
        scratch_shapes=[pltpu.SemaphoreType.DMA],
        compiler_params=PARAMS,
        cost_estimate=COST,
    )(jnp.reshape(flag, (1,)).astype(jnp.int32), taken, kept, *tokens)


def last_frames(group, keys, values, tokens=()):
    columns = pl.ds(group[0] * HD, group[1] * HD)
    n = len(tokens)

    def kernel(keys, values, *refs):
        out, sem = refs[n:]
        started = [
            pltpu.make_async_copy(
                source.at[pl.ds(FT, FT), columns], out.at[pl.ds(i * FT, FT)], sem.at[i]
            )
            for i, source in enumerate((keys, values))
        ]
        for copy in started:
            copy.start()
        for copy in started:
            copy.wait()

    return pl.pallas_call(
        kernel,
        in_specs=[ANY_SPEC] * (2 + n),
        out_specs=VMEM_SPEC,
        out_shape=jax.ShapeDtypeStruct((2 * FT, group[1] * HD), jnp.bfloat16),
        scratch_shapes=[pltpu.SemaphoreType.DMA((2,))],
        compiler_params=PARAMS,
        cost_estimate=COST,
    )(keys, values, *tokens)


def sink_steps(size):
    bits = [1 << b for b in range(1, size.bit_length() - 1)]
    orders = (bits[::-1], bits[::-1])
    done = [0, 0]
    steps = []
    for step in range(len(bits)):
        pairs = []
        for which in (0, 1):
            bit = orders[which][step]
            holders = [i for i in range(0, size, 2) if i & ~done[which] == 0]
            pairs += [(i + which, (i | bit) + which) for i in holders]
            done[which] |= bit
        steps.append(pairs)
    return steps


def project(info, parts, weight, base=None, dtype=jnp.bfloat16):
    columns = weight.shape[1]
    turns = 6
    block = columns // turns
    rows = parts[0][0].shape[0]
    n = len(parts)
    bases = [] if base is None else [base]

    def kernel(info, *refs):
        weight, out = refs[n], refs[-1]
        column = span(pl.program_id(0) * block, block)
        total = None if base is None else refs[n + 1][:, column]
        for a, (array, place, received) in zip(refs[:n], parts):
            owner = 1 - info[1] if received else info[1]
            first = owner * (weight.shape[0] // 2) + place
            product = dot(a[...], weight[pl.ds(pl.multiple_of(first, HD), array.shape[1]), column])
            total = product if total is None else total + product
        out[...] = total.astype(dtype)

    return pl.pallas_call(
        kernel,
        grid=(turns,),
        in_specs=[SMEM_SPEC] + [VMEM_SPEC] * (n + 1 + len(bases)),
        out_specs=pl.BlockSpec((rows, block), lambda i: (0, i)),
        out_shape=jax.ShapeDtypeStruct((rows, columns), dtype),
        compiler_params=PARAMS,
        cost_estimate=COST,
    )(info, *[a for a, _, _ in parts], weight, *bases)


def local(query_states, key_states, value_states, win_start, group_end, out_weight):
    axis = "tm"
    size = lax.axis_size(axis)
    paired = lax.axis_size("head") == 2
    me = lax.axis_index(axis)
    core = me % 2
    heads = query_states.shape[1] // HD
    info = jnp.concatenate(
        [
            jnp.stack([me * 2, lax.axis_index("head")]).astype(jnp.int32),
            win_start.astype(jnp.int32),
            group_end.astype(jnp.int32),
            jnp.stack([core]).astype(jnp.int32),
        ]
    )
    groups = [(0, heads // 2), (heads // 2, heads // 2)] if heads % 2 == 0 else [(0, heads)]
    rows = query_states.shape[0]
    group_width = groups[0][1] * HD
    own_like = jax.ShapeDtypeStruct((rows, group_width), jnp.bfloat16)
    acc_like = jax.ShapeDtypeStruct((rows, group_width), jnp.float32)
    sums_like = jax.ShapeDtypeStruct((rows, HD), jnp.float32)
    frame_buffers = [pltpu.VMEM((2, FT, group_width), jnp.bfloat16)] * 2
    dma_sems = pltpu.SemaphoreType.DMA((2, 2))

    onward = [(i, i + 1) for i in range(size - 1)]
    near_k = lax.ppermute(key_states, axis, onward)
    near_v = lax.ppermute(value_states, axis, onward)
    moved = lax.ppermute(value_states, axis, [(0, 1)])
    held = jnp.where(core == 0, key_states[:FT], moved[:FT])

    def near_stage(group, state, tokens):
        return stage(
            functools.partial(near_kernel, group),
            [info, query_states, *state, near_k, near_v], 2, [acc_like, sums_like, TOKEN],
            frame_buffers + [dma_sems], NEAR_COST, tokens,
        )

    def flag_of(pairs):
        takes = jnp.zeros((), bool)
        for _, target in pairs:
            takes = takes | (me == target)
        return takes

    states = []
    *steps, last_step = sink_steps(size)
    for step, pairs in enumerate(steps):
        moved = lax.ppermute(held, axis, pairs)
        tokens = []
        if step < len(groups):
            *state, token = stage(
                functools.partial(own_kernel, groups[step]),
                [info, query_states, key_states, value_states], 0,
                [own_like, acc_like, sums_like, TOKEN], [], tokens=[held] * (step > 0),
            )
            states.append(state)
            tokens.append(token)
        if step < len(steps) - 1:
            held = pick(flag_of(pairs), moved, held, tokens)

    on_chip = [(i, i + 1) for i in range(0, size, 2)]
    near_last = last_frames((0, heads), near_k, near_v, tokens)
    relay = lax.ppermute(near_last, axis, on_chip)
    before, arrivals = tokens, [near_last]
    halves = []
    near_after = []
    for g, group in enumerate(groups):
        columns = group[0] * HD, group[1] * HD
        own_last = last_frames(group, key_states, value_states, before)
        far = lax.ppermute(own_last, axis, [(i, i + 2) for i in range(0, size - 2, 2)])
        part = pick(flag_of(steps[-1]), moved, held, before + arrivals, columns)
        before, arrivals = [part], []
        arriving = lax.ppermute(part, axis, last_step)
        *sums_now, token = near_stage(group, states[g], near_after + [part])
        states[g] = states[g][0], *sums_now
        part = pick(flag_of(last_step), arriving, part, [far, token])
        near_after = [part]
        halves.append((part, lax.ppermute(part, axis, [(i, i ^ 1) for i in range(size)]), far))
    sends = []
    for g, group in enumerate(groups):
        part, other, far = halves[g]
        last = g == len(groups) - 1
        for first, count in [(h, 1) for h in range(group[1])] if last else [(0, group[1])]:
            out = jax.ShapeDtypeStruct((FT if paired else rows, count * HD), jnp.bfloat16)
            results = stage(
                functools.partial(final_kernel, group, (first, count)),
                [info, query_states, *states[g], part, other, far, relay,
                 key_states, value_states, near_k, near_v], 8,
                [out] * (2 if paired else 1),
                frame_buffers + [
                    pltpu.VMEM((rows, 2 * HD), jnp.float32),
                    pltpu.VMEM((FT, 2 * HD), jnp.float32),
                    pltpu.VMEM((FT, HD), jnp.float32),
                    pltpu.SMEM((group[1], 2), jnp.float32),
                    dma_sems,
                ],
            )
            received = None
            if paired:
                received = lax.ppermute(results[1], "head", [(0, 1), (1, 0)])
            sends.append(((group[0] + first) * HD, results[0], received))
    if not paired:
        attended = jnp.concatenate([mine for _, mine, _ in sends], axis=1)
        token_rows = lax.all_to_all(attended, "head", split_axis=0, concat_axis=1, tiled=True)
        return dot(token_rows, out_weight).astype(jnp.bfloat16)
    early = [(mine, place, False) for place, mine, _ in sends]
    early.append((sends[0][2], sends[0][0], True))
    late = [(received, place, True) for place, _, received in sends[1:]]
    base = project(info, early, out_weight, dtype=jnp.float32)
    return project(info, late, out_weight, base)


def solution(mesh):
    in_specs = (P("tm", "head"), P("tm", "head"), P("tm", "head"), P("tm"), P("tm"), P())
    out_specs = P(("tm", "head"), None)
    return jax.shard_map(local, mesh=mesh, in_specs=in_specs, out_specs=out_specs, check_vma=False)
```

```python
import functools

import jax
import jax.numpy as jnp
from jax import lax
from jax.experimental import pallas as pl
from jax.experimental.pallas import tpu as pltpu
from jax.sharding import PartitionSpec as P

HD = 128
FT = 768
BK = 256
LOG2E = 1.4426950408889634
SCALE = HD ** -0.5 * LOG2E
LIMIT = 1e30
HIDDEN = 1e30
PARAMS = pltpu.CompilerParams(vmem_limit_bytes=12 * 1024 * 1024)
ANY_SPEC = pl.BlockSpec(memory_space=pl.ANY)
NEAR_COST = pl.CostEstimate(flops=8_000_000_000, bytes_accessed=1000, transcendentals=0)
COST = pl.CostEstimate(flops=1000, bytes_accessed=1000, transcendentals=0)
TOKEN = jax.ShapeDtypeStruct((8, 128), jnp.float32)


def dot(a, b):
    return jnp.dot(a, b, preferred_element_type=jnp.float32)


def span(start, size):
    return pl.ds(pl.multiple_of(start, size), size)


def rows_of(slot):
    return slice(slot * FT, (slot + 1) * FT)


def add_frame(lanes, kt, values, block):
    units = [(n, row) for n in range(len(lanes)) for row in range(0, FT, block)]

    def scores(unit):
        n, row = unit
        return dot(lanes[n][0][row : row + block, :], kt[...])

    ahead = scores(units[0])
    for at, (n, row) in enumerate(units):
        s = ahead
        if at + 1 < len(units):
            ahead = scores(units[at + 1])
        _, shift, add = lanes[n]
        weights = [
            jnp.exp2(s[:, c : c + HD] * SCALE - shift[row : row + block, :]).astype(jnp.bfloat16)
            for c in range(0, FT, HD)
        ]
        add(row, dot(jnp.concatenate(weights, axis=1), values[...]))


def visible(info, slot, frame):
    return (frame >= 1) & (frame >= info[2 + slot]) & (frame <= info[4 + slot])


def lanes_of(h, heads):
    share = HD // heads
    lane = lax.broadcasted_iota(jnp.int32, (1, HD), 1)
    return (lane >= h * share) & (lane < (h + 1) * share)


def spread(packed, h, heads):
    row = lax.broadcasted_iota(jnp.int32, (HD, HD), 0)
    chosen = jnp.where(row == h * (HD // heads), 1.0, 0.0).astype(jnp.bfloat16)
    high = packed.astype(jnp.bfloat16)
    low = (packed - high.astype(jnp.float32)).astype(jnp.bfloat16)
    return dot(high, chosen) + dot(low, chosen)


def shift_of(own, seen):
    return jnp.where(seen, own.astype(jnp.float32) * SCALE, HIDDEN)


def sums_into(acc_from, acc, sums, slot, column, h, heads):
    def add(row, added):
        rows = slice(slot * FT + row, slot * FT + row + added.shape[0])
        new = added[:, :HD]
        acc[rows, column] = new if acc_from is None else acc_from[rows, column] + new
        old = sums[rows, :]
        sums[rows, :] = jnp.where(lanes_of(h, heads), old + added[:, HD:], old)

    return add


def load_frame(kt, values, k, v, column):
    kt[...] = k[:, column].T
    values[:, :HD] = v[:, column]


def each_head(group, turn, part=None):
    offset, heads = group
    first, count = part or (0, heads)

    def body(h, carry):
        turn(h, span(h * HD, HD), span((h + offset) * HD, HD))
        return carry

    lax.fori_loop(first, first + count, body, 0)


def own_kernel(group, info, q, k, v, *refs):
    own, acc, sums, token, kt, values = refs
    heads = group[1]
    first = info[0]
    token[...] = jnp.zeros_like(token)
    values[:, HD:] = jnp.ones((FT, HD), jnp.bfloat16)
    ones = jnp.ones((HD, HD), jnp.bfloat16)
    sums[...] = jnp.zeros_like(sums)

    def turn(h, column, wide):
        for slot in (0, 1):
            rows = rows_of(slot)
            product = q[rows, wide].astype(jnp.float32) * k[rows, wide].astype(jnp.float32)
            own[rows, column] = dot(product.astype(jnp.bfloat16), ones).astype(jnp.bfloat16)
        for frame in (0, 1):
            load_frame(kt, values, k.at[rows_of(frame)], v.at[rows_of(frame)], wide)
            lanes = []
            for slot in (0, 1):
                rows = rows_of(slot)
                shift = shift_of(own[rows, column], visible(info, slot, first + frame))
                add = sums_into(acc if frame else None, acc, sums, slot, column, h, heads)
                lanes.append((q[rows, wide], shift, add))
            add_frame(lanes, kt, values, 256)

    each_head(group, turn)


def near_kernel(group, info, q, own, acc_in, sums_in, near_k, near_v, *refs):
    acc, sums, token, kt, values, k_buf, v_buf, sem = refs
    offset, heads = group
    token[...] = jnp.zeros_like(token)
    first = info[0]
    order = (1, 0)
    copies = {
        frame: [
            pltpu.make_async_copy(
                source.at[pl.ds(frame * FT, FT), pl.ds(offset * HD, heads * HD)],
                buf.at[frame],
                sem.at[frame, n],
            )
            for n, (source, buf) in enumerate(((near_k, k_buf), (near_v, v_buf)))
        ]
        for frame in order
    }
    for frame in order:
        for copy in copies[frame]:
            copy.start()
    values[:, HD:] = jnp.ones((FT, HD), jnp.bfloat16)
    sums[...] = sums_in[...]
    for frame in order:
        for copy in copies[frame]:
            copy.wait()

        def turn(h, column, wide):
            load_frame(kt, values, k_buf.at[frame], v_buf.at[frame], column)
            acc_from = acc_in if frame == order[0] else acc
            lanes = []
            for slot in (0, 1):
                rows = rows_of(slot)
                add = sums_into(acc_from, acc, sums, slot, column, h, heads)
                shift = shift_of(own[rows, column], visible(info, slot, first - 2 + frame))
                lanes.append((q[rows, wide], shift, add))
            add_frame(lanes, kt, values, 256)

        each_head(group, turn)


def final_kernel(
    group, part, info, q, own, acc_in, sums_in,
    sink_a, sink_b, far, relay, key_any, value_any, near_k, near_v, *refs,
):
    outs = refs[:-9]
    kt, values, k_buf, v_buf, results, acc, shift, too_large, sem = refs[-9:]
    first = info[0]
    core = info[6]
    far_seen = visible(info, 0, first - 3)
    offset, heads = group
    group_columns = pl.ds(offset * HD, heads * HD)
    part_first, part_heads = part
    values[:, HD:] = jnp.ones((FT, HD), jnp.bfloat16)

    own_columns = pl.ds(0, heads * HD)

    def copies(frame, k, k_row, v, v_row, columns):
        return [
            pltpu.make_async_copy(
                source.at[pl.ds(row, FT), columns], buf.at[frame], sem.at[frame, n]
            )
            for n, (source, row, buf) in enumerate(((k, k_row, k_buf), (v, v_row, v_buf)))
        ]

    arriving = {
        0: [
            (0, sink_a, 0, sink_b, 0, group_columns),
            (1, far, 0, far, FT, own_columns),
        ],
        1: [
            (0, sink_b, 0, sink_a, 0, group_columns),
            (1, relay, 0, relay, FT, group_columns),
        ],
    }
    for which, listed in arriving.items():

        @pl.when(core == which)
        def _():
            started = [copies(*entry) for entry in listed]
            for act in (lambda copy: copy.start(), lambda copy: copy.wait()):
                for pair in started:
                    for copy in pair:
                        act(copy)

    def write(slot, h, acc, total):
        attended = (acc / total).astype(jnp.bfloat16)
        column = span((h - part_first) * HD, HD)
        if len(outs) == 1:
            outs[0][span(slot * FT, FT), column] = attended
        else:

            @pl.when(info[1] == slot)
            def _():
                outs[0][:, column] = attended

            @pl.when(info[1] != slot)
            def _():
                outs[1][:, column] = attended

    def turn(h, column, wide):
        def into(ref, slot, old=None):
            def add(row, added):
                rows = slice(slot * FT + row, slot * FT + row + added.shape[0])
                ref[rows, :] = added if old is None else old[rows, :] + added

            return add

        def lane(slot, seen, add):
            rows = rows_of(slot)
            return q[rows, wide], shift_of(own[rows, column], seen), add

        load_frame(kt, values, k_buf.at[0], v_buf.at[0], column)
        add_frame([lane(slot, True, into(results, slot)) for slot in (1, 0)], kt, values, 256)
        load_frame(kt, values, k_buf.at[1], v_buf.at[1], column)
        add_frame([lane(0, far_seen, into(results, 0, results))], kt, values, 256)
        for slot in (0, 1):
            rows = rows_of(slot)
            total = spread(sums_in[rows, :], h, heads) + results[rows, HD:]
            write(slot, h, acc_in[rows, column] + results[rows, :HD], total)
            too_large[h, slot] = jnp.max(jnp.where(total < LIMIT, 0.0, 1.0))

    each_head(group, turn, part)

    def again(slot, h, column, wide):
        here, there = core == 0, core == 1
        far_here = far_seen & (slot == 0)
        sources = [
            (here, sink_a, 0, sink_b, 0, wide), (there, sink_b, 0, sink_a, 0, wide),
            (far_here & here, far, 0, far, FT, column),
            (far_here & there, relay, 0, relay, FT, wide),
        ]
        for frame in (0, 1):
            row = frame * FT
            shown = visible(info, slot, first + frame)
            sources.append((shown, key_any, row, value_any, row, wide))
            behind = visible(info, slot, first - 2 + frame)
            sources.append((behind, near_k, row, near_v, row, wide))
        one = (k_buf.at[0, :, :HD], v_buf.at[0, :, :HD])

        def sweep(step):
            def visit(t, carry):
                seen = False
                for n, (shown, k, k_row, v, v_row, where) in enumerate(sources):
                    chosen = (t == n) & shown
                    seen = seen | chosen

                    @pl.when(chosen)
                    def _():
                        for n, (ref, row) in enumerate(((k, k_row), (v, v_row))):
                            copy = pltpu.make_async_copy(
                                ref.at[pl.ds(row, FT), where], one[n], sem.at[0, n]
                            )
                            copy.start()
                            copy.wait()

                @pl.when(seen)
                def _():
                    load_frame(kt, values, k_buf.at[0], v_buf.at[0], slice(0, HD))
                    step()

                return carry

            lax.fori_loop(0, len(sources), visit, 0)

        def by_rows(step):
            def turn(i, carry):
                rows = span(i * HD, HD)
                queries = q[span(slot * FT + i * HD, HD), wide]
                for j in range(0, FT, BK):
                    step(rows, dot(queries, kt[:, j : j + BK]) * SCALE, values[j : j + BK, :])
                return carry

            lax.fori_loop(0, FT // HD, turn, 0)

        def peak(rows, s, _):
            shift[rows, :] = jnp.maximum(shift[rows, :], jnp.max(s, axis=1, keepdims=True))

        def more_sums(rows, s, some_values):
            weights = jnp.concatenate(
                [jnp.exp2(s[:, c : c + HD] - shift[rows, :]) for c in range(0, BK, HD)], axis=1
            )
            acc[rows, :] = acc[rows, :] + dot(weights.astype(jnp.bfloat16), some_values)

        shift[...] = jnp.full((FT, HD), -jnp.inf, jnp.float32)
        acc[...] = jnp.zeros((FT, 2 * HD), jnp.float32)
        sweep(lambda: by_rows(peak))
        sweep(lambda: by_rows(more_sums))
        write(slot, h, acc[:, :HD], acc[:, HD:])

    def check(h, column, wide):
        def turn(slot, carry):
            pl.when(too_large[h, slot] > 0.0)(lambda: again(slot, h, column, wide))
            return carry

        lax.fori_loop(0, 2, turn, 0)

    each_head(group, check, part)


VMEM_SPEC = pl.BlockSpec(memory_space=pltpu.VMEM)
SMEM_SPEC = pl.BlockSpec(memory_space=pltpu.SMEM)


def stage(kernel, arrays, in_any, outs, scratch, cost=None, tokens=()):
    n = len(arrays)

    def run(*refs):
        kernel(*refs[:n], *refs[n + len(tokens) :])

    return pl.pallas_call(
        run,
        in_specs=[SMEM_SPEC] + [VMEM_SPEC] * (n - in_any - 1)
        + [ANY_SPEC] * (in_any + len(tokens)),
        out_specs=[VMEM_SPEC] * len(outs),
        scratch_shapes=[
            pltpu.VMEM((HD, FT), jnp.bfloat16), pltpu.VMEM((FT, 2 * HD), jnp.bfloat16)
        ] + list(scratch),
        out_shape=outs,
        compiler_params=PARAMS,
        cost_estimate=cost or COST,
    )(*arrays, *tokens)


def pick(flag, taken, kept, tokens=(), columns=None):
    column, width = columns or (0, kept.shape[1])

    def kernel(flag, taken, kept, *refs):
        out, sem = refs[-2:]
        for value, source in ((1, taken), (0, kept)):

            @pl.when(flag[0] == value)
            def _():
                rows = source.at[pl.ds(0, FT), pl.ds(column, width)]
                copy = pltpu.make_async_copy(rows, out, sem)
                copy.start()
                copy.wait()

    return pl.pallas_call(
        kernel,
        in_specs=[SMEM_SPEC] + [ANY_SPEC] * (2 + len(tokens)),
        out_specs=VMEM_SPEC,
        out_shape=jax.ShapeDtypeStruct((FT, width), jnp.bfloat16),
        scratch_shapes=[pltpu.SemaphoreType.DMA],
        compiler_params=PARAMS,
        cost_estimate=COST,
    )(jnp.reshape(flag, (1,)).astype(jnp.int32), taken, kept, *tokens)


def last_frames(group, keys, values, tokens=()):
    columns = pl.ds(group[0] * HD, group[1] * HD)
    n = len(tokens)

    def kernel(keys, values, *refs):
        out, sem = refs[n:]
        started = [
            pltpu.make_async_copy(
                source.at[pl.ds(FT, FT), columns], out.at[pl.ds(i * FT, FT)], sem.at[i]
            )
            for i, source in enumerate((keys, values))
        ]
        for copy in started:
            copy.start()
        for copy in started:
            copy.wait()

    return pl.pallas_call(
        kernel,
        in_specs=[ANY_SPEC] * (2 + n),
        out_specs=VMEM_SPEC,
        out_shape=jax.ShapeDtypeStruct((2 * FT, group[1] * HD), jnp.bfloat16),
        scratch_shapes=[pltpu.SemaphoreType.DMA((2,))],
        compiler_params=PARAMS,
        cost_estimate=COST,
    )(keys, values, *tokens)


def sink_steps(size):
    bits = [1 << b for b in range(1, size.bit_length() - 1)]
    orders = (bits[::-1], bits[::-1])
    done = [0, 0]
    steps = []
    for step in range(len(bits)):
        pairs = []
        for which in (0, 1):
            bit = orders[which][step]
            holders = [i for i in range(0, size, 2) if i & ~done[which] == 0]
            pairs += [(i + which, (i | bit) + which) for i in holders]
            done[which] |= bit
        steps.append(pairs)
    return steps


def project(info, parts, weight, base=None, dtype=jnp.bfloat16, turns=6):
    columns = weight.shape[1]
    block = columns // turns
    rows = parts[0][0].shape[0]
    n = len(parts)
    bases = [] if base is None else [base]

    def kernel(info, *refs):
        weight, out = refs[n], refs[-1]
        column = span(pl.program_id(0) * block, block)
        total = None if base is None else refs[n + 1][:, column]
        for a, (array, place, received) in zip(refs[:n], parts):
            owner = 1 - info[1] if received else info[1]
            first = owner * (weight.shape[0] // 2) + place
            product = dot(a[...], weight[pl.ds(pl.multiple_of(first, HD), array.shape[1]), column])
            total = product if total is None else total + product
        out[...] = total.astype(dtype)

    return pl.pallas_call(
        kernel,
        grid=(turns,),
        in_specs=[SMEM_SPEC] + [VMEM_SPEC] * (n + 1 + len(bases)),
        out_specs=pl.BlockSpec((rows, block), lambda i: (0, i)),
        out_shape=jax.ShapeDtypeStruct((rows, columns), dtype),
        compiler_params=PARAMS,
        cost_estimate=COST,
    )(info, *[a for a, _, _ in parts], weight, *bases)


def local(query_states, key_states, value_states, win_start, group_end, out_weight):
    axis = "tm"
    size = lax.axis_size(axis)
    paired = lax.axis_size("head") == 2
    me = lax.axis_index(axis)
    core = me % 2
    heads = query_states.shape[1] // HD
    info = jnp.concatenate(
        [
            jnp.stack([me * 2, lax.axis_index("head")]).astype(jnp.int32),
            win_start.astype(jnp.int32),
            group_end.astype(jnp.int32),
            jnp.stack([core]).astype(jnp.int32),
        ]
    )
    groups = [(0, heads // 2), (heads // 2, heads // 2)] if heads % 2 == 0 else [(0, heads)]
    rows = query_states.shape[0]
    group_width = groups[0][1] * HD
    own_like = jax.ShapeDtypeStruct((rows, group_width), jnp.bfloat16)
    acc_like = jax.ShapeDtypeStruct((rows, group_width), jnp.float32)
    sums_like = jax.ShapeDtypeStruct((rows, HD), jnp.float32)
    frame_buffers = [pltpu.VMEM((2, FT, group_width), jnp.bfloat16)] * 2
    dma_sems = pltpu.SemaphoreType.DMA((2, 2))

    onward = [(i, i + 1) for i in range(size - 1)]
    near_k = lax.ppermute(key_states, axis, onward)
    near_v = lax.ppermute(value_states, axis, onward)
    moved = lax.ppermute(value_states, axis, [(0, 1)])
    held = jnp.where(core == 0, key_states[:FT], moved[:FT])

    def near_stage(group, state, tokens):
        return stage(
            functools.partial(near_kernel, group),
            [info, query_states, *state, near_k, near_v], 2, [acc_like, sums_like, TOKEN],
            frame_buffers + [dma_sems], NEAR_COST, tokens,
        )

    def flag_of(pairs):
        takes = jnp.zeros((), bool)
        for _, target in pairs:
            takes = takes | (me == target)
        return takes

    states = []
    *steps, last_step = sink_steps(size)
    for step, pairs in enumerate(steps):
        moved = lax.ppermute(held, axis, pairs)
        tokens = []
        if step < len(groups):
            *state, token = stage(
                functools.partial(own_kernel, groups[step]),
                [info, query_states, key_states, value_states], 0,
                [own_like, acc_like, sums_like, TOKEN], [], tokens=[held] * (step > 0),
            )
            states.append(state)
            tokens.append(token)
        if step < len(steps) - 1:
            held = pick(flag_of(pairs), moved, held, tokens)

    on_chip = [(i, i + 1) for i in range(0, size, 2)]
    own_last = last_frames(groups[0], key_states, value_states, tokens)
    near_last = last_frames((0, heads), near_k, near_v, [own_last])
    relay = lax.ppermute(near_last, axis, on_chip)
    part = pick(flag_of(steps[-1]), moved, held, tokens + [near_last])
    arriving = lax.ppermute(part, axis, last_step)

    for g, group in enumerate(groups):
        *sums_now, token = near_stage(group, states[g], [part] + tokens)
        states[g] = states[g][0], *sums_now
        tokens = [token]

    def send_far(own_last):
        return lax.ppermute(own_last, axis, [(i, i + 2) for i in range(0, size - 2, 2)])

    fars = [send_far(own_last)]
    for group in groups[1:]:
        own_last = last_frames(group, key_states, value_states, tokens)
        tokens = tokens + [own_last]
        fars.append(send_far(own_last))
    sink = pick(flag_of(last_step), arriving, part, tokens)
    other = lax.ppermute(sink, axis, [(i, i ^ 1) for i in range(size)])
    sends = []

    def finish(g, pieces, far):
        for first, count in pieces:
            out = jax.ShapeDtypeStruct((FT if paired else rows, count * HD), jnp.bfloat16)
            results = stage(
                functools.partial(final_kernel, groups[g], (first, count)),
                [info, query_states, *states[g], sink, other, far, relay,
                 key_states, value_states, near_k, near_v], 8,
                [out] * (2 if paired else 1),
                frame_buffers + [
                    pltpu.VMEM((rows, 2 * HD), jnp.float32),
                    pltpu.VMEM((FT, 2 * HD), jnp.float32),
                    pltpu.VMEM((FT, HD), jnp.float32),
                    pltpu.SMEM((groups[g][1], 2), jnp.float32),
                    dma_sems,
                ],
            )
            received = None
            if paired:
                received = lax.ppermute(results[1], "head", [(0, 1), (1, 0)])
            sends.append(((groups[g][0] + first) * HD, results[0], received))

    for g, (_, count) in enumerate(groups):
        last = g == len(groups) - 1
        finish(g, [(h, 1) for h in range(count)] if last else [(0, count)], fars[g])
    if not paired:
        attended = jnp.concatenate([mine for _, mine, _ in sends], axis=1)
        token_rows = lax.all_to_all(attended, "head", split_axis=0, concat_axis=1, tiled=True)
        return dot(token_rows, out_weight).astype(jnp.bfloat16)
    early = [(mine, place, False) for place, mine, _ in sends]
    early.append((sends[0][2], sends[0][0], True))
    late = [(received, place, True) for place, _, received in sends[1:]]
    base = project(info, early, out_weight, dtype=jnp.float32)
    return project(info, late, out_weight, base, turns=3)


def solution(mesh):
    in_specs = (P("tm", "head"), P("tm", "head"), P("tm", "head"), P("tm"), P("tm"), P())
    out_specs = P(("tm", "head"), None)
    return jax.shard_map(local, mesh=mesh, in_specs=in_specs, out_specs=out_specs, check_vma=False)
```

```python
import functools

import jax
import jax.numpy as jnp
from jax import lax
from jax.experimental import pallas as pl
from jax.experimental.pallas import tpu as pltpu
from jax.sharding import PartitionSpec as P

HD = 128
FT = 768
BK = 256
LOG2E = 1.4426950408889634
SCALE = HD ** -0.5 * LOG2E
LIMIT = 1e30
HIDDEN = 1e30
PARAMS = pltpu.CompilerParams(vmem_limit_bytes=12 * 1024 * 1024)
ANY_SPEC = pl.BlockSpec(memory_space=pl.ANY)
NEAR_COST = pl.CostEstimate(flops=8_000_000_000, bytes_accessed=1000, transcendentals=0)
COST = pl.CostEstimate(flops=1000, bytes_accessed=1000, transcendentals=0)
TOKEN = jax.ShapeDtypeStruct((8, 128), jnp.float32)


def dot(a, b):
    return jnp.dot(a, b, preferred_element_type=jnp.float32)


def span(start, size):
    return pl.ds(pl.multiple_of(start, size), size)


def rows_of(slot):
    return slice(slot * FT, (slot + 1) * FT)


def add_frame(lanes, kt, values, block):
    units = [(n, row) for n in range(len(lanes)) for row in range(0, FT, block)]

    def scores(unit):
        n, row = unit
        return dot(lanes[n][0][row : row + block, :], kt[...])

    ahead = scores(units[0])
    for at, (n, row) in enumerate(units):
        s = ahead
        if at + 1 < len(units):
            ahead = scores(units[at + 1])
        _, shift, add = lanes[n]
        weights = [
            jnp.exp2(s[:, c : c + HD] * SCALE - shift[row : row + block, :]).astype(jnp.bfloat16)
            for c in range(0, FT, HD)
        ]
        add(row, dot(jnp.concatenate(weights, axis=1), values[...]))


def visible(info, slot, frame):
    return (frame >= 1) & (frame >= info[2 + slot]) & (frame <= info[4 + slot])


def lanes_of(h, heads):
    share = HD // heads
    lane = lax.broadcasted_iota(jnp.int32, (1, HD), 1)
    return (lane >= h * share) & (lane < (h + 1) * share)


def spread(packed, h, heads):
    row = lax.broadcasted_iota(jnp.int32, (HD, HD), 0)
    chosen = jnp.where(row == h * (HD // heads), 1.0, 0.0).astype(jnp.bfloat16)
    high = packed.astype(jnp.bfloat16)
    low = (packed - high.astype(jnp.float32)).astype(jnp.bfloat16)
    return dot(high, chosen) + dot(low, chosen)


def shift_of(own, seen):
    return jnp.where(seen, own.astype(jnp.float32) * SCALE, HIDDEN)


def sums_into(acc_from, acc, sums, slot, column, h, heads):
    def add(row, added):
        rows = slice(slot * FT + row, slot * FT + row + added.shape[0])
        new = added[:, :HD]
        acc[rows, column] = new if acc_from is None else acc_from[rows, column] + new
        old = sums[rows, :]
        sums[rows, :] = jnp.where(lanes_of(h, heads), old + added[:, HD:], old)

    return add


def load_frame(kt, values, k, v, column):
    kt[...] = k[:, column].T
    values[:, :HD] = v[:, column]


def each_head(group, turn, part=None):
    offset, heads = group
    first, count = part or (0, heads)

    def body(h, carry):
        turn(h, span(h * HD, HD), span((h + offset) * HD, HD))
        return carry

    lax.fori_loop(first, first + count, body, 0)


def own_kernel(group, info, q, k, v, *refs):
    own, acc, sums, token, kt, values = refs
    heads = group[1]
    first = info[0]
    token[...] = jnp.zeros_like(token)
    values[:, HD:] = jnp.ones((FT, HD), jnp.bfloat16)
    ones = jnp.ones((HD, HD), jnp.bfloat16)
    sums[...] = jnp.zeros_like(sums)

    def turn(h, column, wide):
        for slot in (0, 1):
            rows = rows_of(slot)
            product = q[rows, wide].astype(jnp.float32) * k[rows, wide].astype(jnp.float32)
            own[rows, column] = dot(product.astype(jnp.bfloat16), ones).astype(jnp.bfloat16)
        for frame in (0, 1):
            load_frame(kt, values, k.at[rows_of(frame)], v.at[rows_of(frame)], wide)
            lanes = []
            for slot in (0, 1):
                rows = rows_of(slot)
                shift = shift_of(own[rows, column], visible(info, slot, first + frame))
                add = sums_into(acc if frame else None, acc, sums, slot, column, h, heads)
                lanes.append((q[rows, wide], shift, add))
            add_frame(lanes, kt, values, 256)

    each_head(group, turn)


def near_kernel(group, info, q, own, acc_in, sums_in, near_k, near_v, *refs):
    acc, sums, token, kt, values, k_buf, v_buf, sem = refs
    offset, heads = group
    token[...] = jnp.zeros_like(token)
    first = info[0]
    order = (1, 0)
    copies = {
        frame: [
            pltpu.make_async_copy(
                source.at[pl.ds(frame * FT, FT), pl.ds(offset * HD, heads * HD)],
                buf.at[frame],
                sem.at[frame, n],
            )
            for n, (source, buf) in enumerate(((near_k, k_buf), (near_v, v_buf)))
        ]
        for frame in order
    }
    for frame in order:
        for copy in copies[frame]:
            copy.start()
    values[:, HD:] = jnp.ones((FT, HD), jnp.bfloat16)
    sums[...] = sums_in[...]
    for frame in order:
        for copy in copies[frame]:
            copy.wait()

        def turn(h, column, wide):
            load_frame(kt, values, k_buf.at[frame], v_buf.at[frame], column)
            acc_from = acc_in if frame == order[0] else acc
            lanes = []
            for slot in (0, 1):
                rows = rows_of(slot)
                add = sums_into(acc_from, acc, sums, slot, column, h, heads)
                shift = shift_of(own[rows, column], visible(info, slot, first - 2 + frame))
                lanes.append((q[rows, wide], shift, add))
            add_frame(lanes, kt, values, 256)

        each_head(group, turn)


def final_kernel(
    group, part, info, q, own, acc_in, sums_in,
    sink_a, sink_b, far, relay, key_any, value_any, near_k, near_v, *refs,
):
    outs = refs[:-9]
    kt, values, k_buf, v_buf, results, acc, shift, too_large, sem = refs[-9:]
    first = info[0]
    core = info[6]
    far_seen = visible(info, 0, first - 3)
    offset, heads = group
    group_columns = pl.ds(offset * HD, heads * HD)
    part_first, part_heads = part
    values[:, HD:] = jnp.ones((FT, HD), jnp.bfloat16)

    own_columns = pl.ds(0, heads * HD)

    def copies(frame, k, k_row, v, v_row, columns):
        return [
            pltpu.make_async_copy(
                source.at[pl.ds(row, FT), columns], buf.at[frame], sem.at[frame, n]
            )
            for n, (source, row, buf) in enumerate(((k, k_row, k_buf), (v, v_row, v_buf)))
        ]

    arriving = {
        0: [
            (0, sink_a, 0, sink_b, 0, group_columns),
            (1, far, 0, far, FT, own_columns),
        ],
        1: [
            (0, sink_b, 0, sink_a, 0, group_columns),
            (1, relay, 0, relay, FT, group_columns),
        ],
    }
    for which, listed in arriving.items():

        @pl.when(core == which)
        def _():
            started = [copies(*entry) for entry in listed]
            for act in (lambda copy: copy.start(), lambda copy: copy.wait()):
                for pair in started:
                    for copy in pair:
                        act(copy)

    def write(slot, h, acc, total):
        attended = (acc / total).astype(jnp.bfloat16)
        column = span((h - part_first) * HD, HD)
        if len(outs) == 1:
            outs[0][span(slot * FT, FT), column] = attended
        else:

            @pl.when(info[1] == slot)
            def _():
                outs[0][:, column] = attended

            @pl.when(info[1] != slot)
            def _():
                outs[1][:, column] = attended

    def turn(h, column, wide):
        def into(ref, slot, old=None):
            def add(row, added):
                rows = slice(slot * FT + row, slot * FT + row + added.shape[0])
                ref[rows, :] = added if old is None else old[rows, :] + added

            return add

        def lane(slot, seen, add):
            rows = rows_of(slot)
            return q[rows, wide], shift_of(own[rows, column], seen), add

        load_frame(kt, values, k_buf.at[0], v_buf.at[0], column)
        add_frame([lane(slot, True, into(results, slot)) for slot in (1, 0)], kt, values, 256)
        load_frame(kt, values, k_buf.at[1], v_buf.at[1], column)
        add_frame([lane(0, far_seen, into(results, 0, results))], kt, values, 256)
        for slot in (0, 1):
            rows = rows_of(slot)
            total = spread(sums_in[rows, :], h, heads) + results[rows, HD:]
            write(slot, h, acc_in[rows, column] + results[rows, :HD], total)
            too_large[h, slot] = jnp.max(jnp.where(total < LIMIT, 0.0, 1.0))

    each_head(group, turn, part)

    def again(slot, h, column, wide):
        here, there = core == 0, core == 1
        far_here = far_seen & (slot == 0)
        sources = [
            (here, sink_a, 0, sink_b, 0, wide), (there, sink_b, 0, sink_a, 0, wide),
            (far_here & here, far, 0, far, FT, column),
            (far_here & there, relay, 0, relay, FT, wide),
        ]
        for frame in (0, 1):
            row = frame * FT
            shown = visible(info, slot, first + frame)
            sources.append((shown, key_any, row, value_any, row, wide))
            behind = visible(info, slot, first - 2 + frame)
            sources.append((behind, near_k, row, near_v, row, wide))
        one = (k_buf.at[0, :, :HD], v_buf.at[0, :, :HD])

        def sweep(step):
            def visit(t, carry):
                seen = False
                for n, (shown, k, k_row, v, v_row, where) in enumerate(sources):
                    chosen = (t == n) & shown
                    seen = seen | chosen

                    @pl.when(chosen)
                    def _():
                        for n, (ref, row) in enumerate(((k, k_row), (v, v_row))):
                            copy = pltpu.make_async_copy(
                                ref.at[pl.ds(row, FT), where], one[n], sem.at[0, n]
                            )
                            copy.start()
                            copy.wait()

                @pl.when(seen)
                def _():
                    load_frame(kt, values, k_buf.at[0], v_buf.at[0], slice(0, HD))
                    step()

                return carry

            lax.fori_loop(0, len(sources), visit, 0)

        def by_rows(step):
            def turn(i, carry):
                rows = span(i * HD, HD)
                queries = q[span(slot * FT + i * HD, HD), wide]
                for j in range(0, FT, BK):
                    step(rows, dot(queries, kt[:, j : j + BK]) * SCALE, values[j : j + BK, :])
                return carry

            lax.fori_loop(0, FT // HD, turn, 0)

        def peak(rows, s, _):
            shift[rows, :] = jnp.maximum(shift[rows, :], jnp.max(s, axis=1, keepdims=True))

        def more_sums(rows, s, some_values):
            weights = jnp.concatenate(
                [jnp.exp2(s[:, c : c + HD] - shift[rows, :]) for c in range(0, BK, HD)], axis=1
            )
            acc[rows, :] = acc[rows, :] + dot(weights.astype(jnp.bfloat16), some_values)

        shift[...] = jnp.full((FT, HD), -jnp.inf, jnp.float32)
        acc[...] = jnp.zeros((FT, 2 * HD), jnp.float32)
        sweep(lambda: by_rows(peak))
        sweep(lambda: by_rows(more_sums))
        write(slot, h, acc[:, :HD], acc[:, HD:])

    def check(h, column, wide):
        def turn(slot, carry):
            pl.when(too_large[h, slot] > 0.0)(lambda: again(slot, h, column, wide))
            return carry

        lax.fori_loop(0, 2, turn, 0)

    each_head(group, check, part)


VMEM_SPEC = pl.BlockSpec(memory_space=pltpu.VMEM)
SMEM_SPEC = pl.BlockSpec(memory_space=pltpu.SMEM)


def stage(kernel, arrays, in_any, outs, scratch, cost=None, tokens=()):
    n = len(arrays)

    def run(*refs):
        kernel(*refs[:n], *refs[n + len(tokens) :])

    return pl.pallas_call(
        run,
        in_specs=[SMEM_SPEC] + [VMEM_SPEC] * (n - in_any - 1)
        + [ANY_SPEC] * (in_any + len(tokens)),
        out_specs=[VMEM_SPEC] * len(outs),
        scratch_shapes=[
            pltpu.VMEM((HD, FT), jnp.bfloat16), pltpu.VMEM((FT, 2 * HD), jnp.bfloat16)
        ] + list(scratch),
        out_shape=outs,
        compiler_params=PARAMS,
        cost_estimate=cost or COST,
    )(*arrays, *tokens)


def pick(flag, taken, kept, tokens=(), columns=None):
    column, width = columns or (0, kept.shape[1])

    def kernel(flag, taken, kept, *refs):
        out, sem = refs[-2:]
        for value, source in ((1, taken), (0, kept)):

            @pl.when(flag[0] == value)
            def _():
                rows = source.at[pl.ds(0, FT), pl.ds(column, width)]
                copy = pltpu.make_async_copy(rows, out, sem)
                copy.start()
                copy.wait()

    return pl.pallas_call(
        kernel,
        in_specs=[SMEM_SPEC] + [ANY_SPEC] * (2 + len(tokens)),
        out_specs=VMEM_SPEC,
        out_shape=jax.ShapeDtypeStruct((FT, width), jnp.bfloat16),
        scratch_shapes=[pltpu.SemaphoreType.DMA],
        compiler_params=PARAMS,
        cost_estimate=COST,
    )(jnp.reshape(flag, (1,)).astype(jnp.int32), taken, kept, *tokens)


def last_frames(group, keys, values, tokens=()):
    columns = pl.ds(group[0] * HD, group[1] * HD)
    n = len(tokens)

    def kernel(keys, values, *refs):
        out, sem = refs[n:]
        started = [
            pltpu.make_async_copy(
                source.at[pl.ds(FT, FT), columns], out.at[pl.ds(i * FT, FT)], sem.at[i]
            )
            for i, source in enumerate((keys, values))
        ]
        for copy in started:
            copy.start()
        for copy in started:
            copy.wait()

    return pl.pallas_call(
        kernel,
        in_specs=[ANY_SPEC] * (2 + n),
        out_specs=VMEM_SPEC,
        out_shape=jax.ShapeDtypeStruct((2 * FT, group[1] * HD), jnp.bfloat16),
        scratch_shapes=[pltpu.SemaphoreType.DMA((2,))],
        compiler_params=PARAMS,
        cost_estimate=COST,
    )(keys, values, *tokens)


def sink_steps(size):
    bits = [1 << b for b in range(1, size.bit_length() - 1)]
    orders = (bits[::-1], bits[::-1])
    done = [0, 0]
    steps = []
    for step in range(len(bits)):
        pairs = []
        for which in (0, 1):
            bit = orders[which][step]
            holders = [i for i in range(0, size, 2) if i & ~done[which] == 0]
            pairs += [(i + which, (i | bit) + which) for i in holders]
            done[which] |= bit
        steps.append(pairs)
    return steps


def project(info, parts, weight, base=None, dtype=jnp.bfloat16, turns=6):
    columns = weight.shape[1]
    block = columns // turns
    rows = parts[0][0].shape[0]
    n = len(parts)
    bases = [] if base is None else [base]

    def kernel(info, *refs):
        weight, out = refs[n], refs[-1]
        column = span(pl.program_id(0) * block, block)
        total = None if base is None else refs[n + 1][:, column]
        for a, (array, place, received) in zip(refs[:n], parts):
            owner = 1 - info[1] if received else info[1]
            first = owner * (weight.shape[0] // 2) + place
            product = dot(a[...], weight[pl.ds(pl.multiple_of(first, HD), array.shape[1]), column])
            total = product if total is None else total + product
        out[...] = total.astype(dtype)

    return pl.pallas_call(
        kernel,
        grid=(turns,),
        in_specs=[SMEM_SPEC] + [VMEM_SPEC] * (n + 1 + len(bases)),
        out_specs=pl.BlockSpec((rows, block), lambda i: (0, i)),
        out_shape=jax.ShapeDtypeStruct((rows, columns), dtype),
        compiler_params=PARAMS,
        cost_estimate=COST,
    )(info, *[a for a, _, _ in parts], weight, *bases)


def local(query_states, key_states, value_states, win_start, group_end, out_weight):
    axis = "tm"
    size = lax.axis_size(axis)
    paired = lax.axis_size("head") == 2
    me = lax.axis_index(axis)
    core = me % 2
    heads = query_states.shape[1] // HD
    info = jnp.concatenate(
        [
            jnp.stack([me * 2, lax.axis_index("head")]).astype(jnp.int32),
            win_start.astype(jnp.int32),
            group_end.astype(jnp.int32),
            jnp.stack([core]).astype(jnp.int32),
        ]
    )
    groups = [(0, heads // 2), (heads // 2, heads // 2)] if heads % 2 == 0 else [(0, heads)]
    rows = query_states.shape[0]
    group_width = groups[0][1] * HD
    own_like = jax.ShapeDtypeStruct((rows, group_width), jnp.bfloat16)
    acc_like = jax.ShapeDtypeStruct((rows, group_width), jnp.float32)
    sums_like = jax.ShapeDtypeStruct((rows, HD), jnp.float32)
    frame_buffers = [pltpu.VMEM((2, FT, group_width), jnp.bfloat16)] * 2
    dma_sems = pltpu.SemaphoreType.DMA((2, 2))

    onward = [(i, i + 1) for i in range(size - 1)]
    near_k = lax.ppermute(key_states, axis, onward)
    near_v = lax.ppermute(value_states, axis, onward)
    moved = lax.ppermute(value_states, axis, [(0, 1)])
    held = jnp.where(core == 0, key_states[:FT], moved[:FT])

    def near_stage(group, state, tokens):
        return stage(
            functools.partial(near_kernel, group),
            [info, query_states, *state, near_k, near_v], 2, [acc_like, sums_like, TOKEN],
            frame_buffers + [dma_sems], NEAR_COST, tokens,
        )

    def flag_of(pairs):
        takes = jnp.zeros((), bool)
        for _, target in pairs:
            takes = takes | (me == target)
        return takes

    states = []
    *steps, last_step = sink_steps(size)
    for step, pairs in enumerate(steps):
        moved = lax.ppermute(held, axis, pairs)
        tokens = []
        if step < len(groups):
            *state, token = stage(
                functools.partial(own_kernel, groups[step]),
                [info, query_states, key_states, value_states], 0,
                [own_like, acc_like, sums_like, TOKEN], [], tokens=[held] * (step > 0),
            )
            states.append(state)
            tokens.append(token)
        if step < len(steps) - 1:
            held = pick(flag_of(pairs), moved, held, tokens)

    on_chip = [(i, i + 1) for i in range(0, size, 2)]
    own_last = last_frames(groups[0], key_states, value_states, tokens)
    near_last = last_frames((0, heads), near_k, near_v, [own_last])
    relay = lax.ppermute(near_last, axis, on_chip)
    part = pick(flag_of(steps[-1]), moved, held, tokens + [near_last])
    arriving = lax.ppermute(part, axis, last_step)

    for g, group in enumerate(groups):
        *sums_now, token = near_stage(group, states[g], [part] + tokens)
        states[g] = states[g][0], *sums_now
        tokens = [token]

    def send_far(own_last):
        return lax.ppermute(own_last, axis, [(i, i + 2) for i in range(0, size - 2, 2)])

    fars = [send_far(own_last)]
    for group in groups[1:]:
        own_last = last_frames(group, key_states, value_states, tokens)
        tokens = tokens + [own_last]
        fars.append(send_far(own_last))
    sink = pick(flag_of(last_step), arriving, part, tokens)
    other = lax.ppermute(sink, axis, [(i, i ^ 1) for i in range(size)])
    sends = []

    def finish(g, pieces, far):
        for first, count in pieces:
            out = jax.ShapeDtypeStruct((FT if paired else rows, count * HD), jnp.bfloat16)
            results = stage(
                functools.partial(final_kernel, groups[g], (first, count)),
                [info, query_states, *states[g], sink, other, far, relay,
                 key_states, value_states, near_k, near_v], 8,
                [out] * (2 if paired else 1),
                frame_buffers + [
                    pltpu.VMEM((rows, 2 * HD), jnp.float32),
                    pltpu.VMEM((FT, 2 * HD), jnp.float32),
                    pltpu.VMEM((FT, HD), jnp.float32),
                    pltpu.SMEM((groups[g][1], 2), jnp.float32),
                    dma_sems,
                ],
            )
            received = None
            if paired:
                received = lax.ppermute(results[1], "head", [(0, 1), (1, 0)])
            sends.append(((groups[g][0] + first) * HD, results[0], received))

    for g, (_, count) in enumerate(groups):
        last = g == len(groups) - 1
        finish(g, [(0, count)] if last else [(h, 1) for h in range(count)], fars[g])
    if not paired:
        attended = jnp.concatenate([mine for _, mine, _ in sends], axis=1)
        token_rows = lax.all_to_all(attended, "head", split_axis=0, concat_axis=1, tiled=True)
        return dot(token_rows, out_weight).astype(jnp.bfloat16)
    early = [(mine, place, False) for place, mine, _ in sends]
    early += [(received, place, True) for place, _, received in sends[:-1]]
    late = [(received, place, True) for place, _, received in sends[-1:]]
    base = project(info, early, out_weight, dtype=jnp.float32, turns=3)
    return project(info, late, out_weight, base, turns=3)


def solution(mesh):
    in_specs = (P("tm", "head"), P("tm", "head"), P("tm", "head"), P("tm"), P("tm"), P())
    out_specs = P(("tm", "head"), None)
    return jax.shard_map(local, mesh=mesh, in_specs=in_specs, out_specs=out_specs, check_vma=False)
```
